32 devices in a mesh: groups: 2 (over y), src: 4 (over z), blk: 4 (over x, core).
Axes of the slice: x: 2, y: 2, z: 4, core: 2. Of those that a mesh axis runs over, the one named last changes fastest.
Arguments:
- pupils: float32 [8192, 2, 128], P(('groups', 'src', 'blk')), parts along dimension 0, may hold values from -6 to 6
- starts: int32 [8192], P(('groups', 'src', 'blk')), parts along dimension 0, may hold values from 0 to 127, as said below
- counts: int32 [8192], P(('groups', 'src', 'blk')), parts along dimension 0, may hold values from 0 to 2, as said below
- weights: float32 [8192], P(('groups', 'src', 'blk')), parts along dimension 0, may hold values from 0.25 to 2.5
- start_block: float32 [4, 8192, 128], P('groups', 'blk'), parts along dimension 0, may hold values from -6 to 6
Outputs:
- kernels: float32 [4, 8192, 128], P('groups', 'blk'), parts along dimension 0
The draws below stay inside these ranges and needn't reach their ends.
There are 2 independent parts, one for each index of `groups`. The reference program is written for one: setup_inputs(seed, part) draws one part's arguments, and reference() takes and returns one part's arrays. A program takes and returns all parts, laid end to end along the dimension named above; each array names one. Nothing has to cross between parts.
Inputs may be any that keep to these rules, and one draw needn't show every extreme that they name: starts[j] // 32 = (j // 256) % 4: every source begins in the region of the aligned block of 256 slots that holds it. In each aligned block of 256 slots the slots with counts > 0 come first; in every block whose index modulo 4 is 3 all slots have counts > 0.
All inputs are finite; a program needn't handle non-finite values.
Results may differ from the reference program's by a relative error of at most 0.00012.
Values sent between devices are 32-bit elements; how exact they have to be, the bound alone decides.
No kernel may reach another device: no remote copies, remote signals or barrier semaphores. Data moves between devices by JAX's collectives and lax.ppermute only.
A program may use at most 64 MiB of HBM per device.

```python
import math
from functools import partial
import jax
import jax.numpy as jnp
from jax import lax

BLOCK = 64
RB = 32
SLOTS = 256
ITERS = 2
M = 128
REGIONS = 4
F = 8192
SOURCES = 4096


def draw_starts(key, part):
    key = jax.random.fold_in(key, 11)
    position = jnp.arange(SOURCES, dtype=jnp.int32)
    region = position // SLOTS % REGIONS
    slot_index = position % SLOTS
    interior_place = jax.random.randint(key, (SOURCES,), 0, RB, dtype=jnp.int32)
    interior_place = jnp.where(slot_index == 0, RB - 1, interior_place)
    return (region * RB + interior_place).astype(jnp.int32)


def draw_counts(key, part):
    key = jax.random.fold_in(key, 12)
    first_key, second_key = jax.random.split(key)
    position = jnp.arange(SOURCES, dtype=jnp.int32)
    holder = position // SLOTS
    region = holder % REGIONS
    slot_index = position % SLOTS
    extra_live = jax.random.randint(first_key, (SOURCES // SLOTS,), 0, SLOTS // REGIONS + 1, dtype=jnp.int32)
    live_count = jnp.minimum(SLOTS, SLOTS * (region + 1) // REGIONS + extra_live[holder])
    run_length = jax.random.randint(second_key, (SOURCES,), 1, 3, dtype=jnp.int32)
    run_length = jnp.where(slot_index == 0, 2, run_length)
    return jnp.where(slot_index < live_count, run_length, 0).astype(jnp.int32)


def shard_levels(rng, shape, cuts, least, largest):
    def one(axis_at, shards_of):
        draws = jax.random.uniform(jax.random.fold_in(jax.random.fold_in(rng, 6), axis_at), (shards_of,), jnp.float32, least / len(cuts), largest / len(cuts))
        return jnp.repeat(jnp.exp(draws), shape[axis_at] // shards_of).reshape((-1,) + (1,) * (len(shape) - axis_at - 1))

    factor_of = one(*cuts[0])
    for cut in cuts[1:]:
        factor_of = factor_of * one(*cut)
    return factor_of


def centred(own_key, shape, scale, reach, shards=(), kind=jnp.bfloat16):
    result = jax.random.normal(own_key, shape, jnp.float32) * scale
    if len(shards) > 0:
        result = shard_levels(own_key, shape, shards, -0.22, 0.18) * result
    return jnp.clip(result, min=-reach, max=reach).astype(kind)


def setup_inputs(seed: int = 0, part: int = 0) -> dict:
    keys = jax.random.split(jax.random.key(seed), 6)
    own_keys = jax.random.split(jax.random.fold_in(keys[5], part), 6)
    pupils = centred(own_keys[0], (SOURCES, 2, 2 * BLOCK), 1.0, 6.0, ((0, 16),), jnp.float32)
    starts = draw_starts(jax.random.fold_in(jax.random.fold_in(keys[5], part), 71), part)
    counts = draw_counts(jax.random.fold_in(jax.random.fold_in(keys[5], part), 71), part)
    weights = jnp.clip(jnp.exp(math.log(2.5) - 2.3025851 * jax.random.uniform(own_keys[3], (SOURCES,), jnp.float32) ** shard_levels(own_keys[3], (SOURCES,), ((0, 16),), -0.2, 0.2)), 0.25, 2.5)
    start_block = centred(own_keys[4], (2, F, M), 1.0, 6.0, ((1, 4),), jnp.float32)
    return dict(pupils=pupils, starts=starts, counts=counts, weights=weights, start_block=start_block)


HIGH_ACCURACY = lax.Precision.HIGHEST

def apply_operator(pupils, starts, counts, weights, subspace_step):
    columns = subspace_step.shape[2]
    total_blocks = RB * REGIONS
    blocks = subspace_step.reshape(2, total_blocks, BLOCK, columns)
    padded = jnp.concatenate([blocks, jnp.zeros((2, 1, BLOCK, columns), jnp.float32)], axis=1)
    offset = jnp.arange(2, dtype=jnp.int32)
    living = (offset[None, :] < counts[:, None]).astype(jnp.float32)
    indices = (starts[:, None] + offset[None, :]).astype(jnp.int32)

    def one_group(carry, members):
        group_pupil, group_index, group_live, group_weight = members
        real_part = group_pupil[:, :, :BLOCK] * group_live[:, :, None]
        imag_part = group_pupil[:, :, BLOCK:] * group_live[:, :, None]
        near_re = padded[0][group_index]
        near_im = padded[1][group_index]
        inner = partial(jnp.einsum, 'slk,slkm->sm', precision=HIGH_ACCURACY)
        coef_re = (inner(real_part, near_re) + inner(imag_part, near_im)) * group_weight[:, None]
        coef_im = (inner(real_part, near_im) - inner(imag_part, near_re)) * group_weight[:, None]
        outer = partial(jnp.einsum, 'slk,sm->slkm', precision=HIGH_ACCURACY)
        result_re = outer(real_part, coef_re) - outer(imag_part, coef_im)
        result_im = outer(imag_part, coef_re) + outer(real_part, coef_im)
        carry = carry.at[0, group_index].add(result_re)
        carry = carry.at[1, group_index].add(result_im)
        return (carry, None)
    members = (pupils.reshape(-1, SLOTS, 2, 2 * BLOCK), indices.reshape(-1, SLOTS, 2), living.reshape(-1, SLOTS, 2), weights.reshape(-1, SLOTS))
    summed, unused = lax.scan(one_group, jnp.zeros_like(padded), members)
    return summed[:, :total_blocks].reshape(2, total_blocks * BLOCK, columns)

def orthonormalize(product):
    row_count = product.shape[1]
    gram = jnp.einsum('cfm,cfn->mn', product, product, precision=HIGH_ACCURACY) / (2.0 * row_count)
    factor = jnp.linalg.cholesky(gram)
    flattened = product.reshape(2 * row_count, product.shape[2])
    solved = lax.linalg.triangular_solve(factor, flattened, left_side=False, lower=True, transpose_a=True)
    return solved.reshape(product.shape)

def reference(pupils, starts, counts, weights, start_block):
    subspace_step = start_block
    for sweeps in range(ITERS):
        product = apply_operator(pupils, starts, counts, weights, subspace_step)
        subspace_step = orthonormalize(product)
    return subspace_step
```

```python
from functools import partial

import jax
import jax.numpy as jnp
from jax import lax
from jax.experimental import pallas as pl
from jax.experimental.pallas import tpu as pltpu
from jax.sharding import PartitionSpec as P

BLOCK = 64
RB = 32
GROUP = 8
M = 128
F32 = jnp.float32
BF16 = jnp.bfloat16
HIGHEST = lax.Precision.HIGHEST
VMEM = pl.BlockSpec(memory_space=pltpu.VMEM)
PARAMS = pltpu.CompilerParams(vmem_limit_bytes=40 * 1024 * 1024)


def split(x):
    hi = x.astype(BF16)
    return hi, (x - hi.astype(F32)).astype(BF16)


def dot(a, b):
    return jnp.dot(a, b, preferred_element_type=F32)


def dot_t(a, b):
    return lax.dot_general(a, b, (((0,), (0,)), ((), ())), preferred_element_type=F32)


def dot_f32(a, b):
    return jnp.dot(a, b, precision=HIGHEST, preferred_element_type=F32)


def build_kernel(add, *refs):
    if add:
        pupils, live, rows, before, out, lhs_hi, lhs_lo = refs
    else:
        pupils, live, rows, out, lhs_hi, lhs_lo = refs
    count = pupils.shape[0] // 2
    lane = lax.broadcasted_iota(jnp.int32, (count, 2 * BLOCK), 1)
    first = pupils[pl.ds(0, count, stride=2), :] * live[pl.ds(0, count, stride=2), :]
    second = pupils[pl.ds(1, count, stride=2), :] * live[pl.ds(1, count, stride=2), :]
    real = jnp.where(lane < BLOCK, first, pltpu.roll(second, BLOCK, 1))
    imag = jnp.where(lane < BLOCK, pltpu.roll(first, BLOCK, 1), second)
    right = jnp.concatenate(
        [
            jnp.concatenate([real, -imag], axis=1),
            jnp.concatenate([imag, real], axis=1),
        ],
        axis=0,
    )
    right_hi, right_lo = split(right)
    left = jnp.concatenate([real.T, imag.T], axis=1) * rows[1:2, :]
    left_hi, left_lo = split(left)
    left_hi = left_hi.reshape(8, 16, 2 * count)
    left_lo = left_lo.reshape(8, 16, 2 * count)
    place = jnp.broadcast_to(rows[0:1, :], (16, 2 * count))

    def one_group(g, carry):
        for j in range(GROUP):
            b = (g * GROUP + j).astype(F32)
            mask = jnp.where(place == b, 1.0, 0.0).astype(BF16)[None]
            lhs_hi[j * 128 : (j + 1) * 128, :] = (left_hi * mask).reshape(128, 2 * count)
            lhs_lo[j * 128 : (j + 1) * 128, :] = (left_lo * mask).reshape(128, 2 * count)
        at = pl.ds(pl.multiple_of(g * GROUP * 128, GROUP * 128), GROUP * 128)
        hi = lhs_hi[...]
        total = dot(hi, right_hi) + dot(hi, right_lo) + dot(lhs_lo[...], right_hi)
        out[at, :] = before[at, :] + total if add else total
        return carry

    lax.fori_loop(0, RB // GROUP, one_group, 0)


def build(pupils, live, rows, before):
    count = pupils.shape[0] // 2
    args = (pupils, live, rows) + (() if before is None else (before,))
    return pl.pallas_call(
        partial(build_kernel, before is not None),
        out_shape=jax.ShapeDtypeStruct((RB * 128, 256), F32),
        in_specs=[VMEM] * len(args),
        out_specs=VMEM,
        scratch_shapes=[pltpu.VMEM((GROUP * 128, 2 * count), BF16)] * 2,
        input_output_aliases={} if before is None else {3: 0},
        compiler_params=PARAMS,
        cost_estimate=pl.CostEstimate(
            flops=6 * RB * 128 * 2 * count * 256, bytes_accessed=10 << 20, transcendentals=0
        ),
        name="band_terms",
    )(*args)


def swapped(x):
    return jnp.concatenate([-x[:, M:], x[:, :M]], axis=1)


def gram_of(hi, lo):
    a = dot_t(hi, hi)
    b = dot_t(hi, lo)
    a = a[:M, :M] + a[M:, M:]
    b = b[:M, :M] + b[M:, M:]
    return a + b + b.T


def apply_kernel(band, left_band, right_band, x, x_left, x_right, z, grams,
                 g_hi, g_lo, x_hi, x_lo, s_hi, s_lo, p, p_hi, p_lo):
    pairs = RB + 3
    zero = jnp.zeros((BLOCK, 256), BF16)

    def put_g(e_rows, value):
        hi, lo = split(value)
        g_hi[e_rows, :] = hi
        g_lo[e_rows, :] = lo

    g_hi[0:BLOCK, :] = zero
    g_lo[0:BLOCK, :] = zero
    put_g(pl.ds(BLOCK, 3 * BLOCK), left_band[...])
    put_g(pl.ds((RB + 2) * 128, BLOCK), right_band[...])
    g_hi[(RB + 2) * 128 + BLOCK :, :] = zero
    g_lo[(RB + 2) * 128 + BLOCK :, :] = zero

    def put_x(at, value):
        hi, lo = split(value)
        x_hi[at, :] = hi
        x_lo[at, :] = lo
        hi, lo = split(swapped(value))
        s_hi[at, :] = hi
        s_lo[at, :] = lo

    put_x(pl.ds(0, 2 * BLOCK), jnp.concatenate([x_left[0], x_left[1]], axis=1))
    put_x(pl.ds((RB + 2) * BLOCK, 2 * BLOCK), jnp.concatenate([x_right[0], x_right[1]], axis=1))

    def prepare(i, carry):
        at = pl.ds(pl.multiple_of(i * 256, 256), 256)
        put_g(pl.ds(pl.multiple_of(256 + i * 256, 256), 256), band[at, :])
        half = pl.ds(pl.multiple_of(i * 128, 128), 128)
        put_x(
            pl.ds(pl.multiple_of(i * 128 + 128, 128), 128),
            jnp.concatenate([x[0, half, :], x[1, half, :]], axis=1),
        )
        return carry

    lax.fori_loop(0, RB // 2, prepare, 0)

    def pair(e):
        at = pl.ds(pl.multiple_of(e * 128, 128), 128)
        win = pl.ds(pl.multiple_of(e * BLOCK, BLOCK), 128)
        w_hi = jnp.concatenate([x_hi[win, :], s_hi[win, :]], axis=0)
        w_lo = jnp.concatenate([x_lo[win, :], s_lo[win, :]], axis=0)
        hi = g_hi[at, :]
        return dot(hi, w_hi) + dot(hi, w_lo) + dot(g_lo[at, :], w_hi)

    def first(e, carry):
        both = pair(e)
        p[pl.ds(pl.multiple_of(e * BLOCK, BLOCK), BLOCK), :] = both[:BLOCK] + carry
        return both[BLOCK:]

    lax.fori_loop(0, pairs, first, jnp.zeros((BLOCK, 256), F32))

    def prepare_again(i, carry):
        at = pl.ds(pl.multiple_of(i * 128, 128), 128)
        put_x(at, p[at, :])
        return carry

    lax.fori_loop(0, (RB + 4) // 2, prepare_again, 0)
    rows = RB * BLOCK
    inner = pl.ds(2 * BLOCK, rows)
    grams[0:M, :] = gram_of(x_hi[inner, :], x_lo[inner, :])

    def second(e, carry):
        both = pair(e)
        z[pl.ds(pl.multiple_of((e - 2) * BLOCK, BLOCK), BLOCK), :] = both[:BLOCK] + carry
        return both[BLOCK:]

    lax.fori_loop(2, RB + 2, second, pair(1)[BLOCK:])

    top = jnp.max(jnp.abs(z[...]), axis=0, keepdims=True)
    top = jnp.maximum(top[:, :M], top[:, M:])
    scale = jnp.where(top > 0, 1.0 / jnp.where(top > 0, top, 1.0), 1.0)
    scale = jnp.concatenate([scale, scale], axis=1)

    def prepare_z(i, carry):
        at = pl.ds(pl.multiple_of(i * 128, 128), 128)
        hi, lo = split(z[at, :] * scale)
        p_hi[at, :] = hi
        p_lo[at, :] = lo
        return carry

    lax.fori_loop(0, rows // 128, prepare_z, 0)
    grams[M : 2 * M, :] = gram_of(p_hi[...], p_lo[...])
    grams[2 * M :, :] = jnp.broadcast_to(top, (8, M))


def apply_twice(band, left_band, right_band, x, x_left, x_right):
    rows = RB * BLOCK
    wide = (RB + 4) * BLOCK
    return pl.pallas_call(
        apply_kernel,
        out_shape=(
            jax.ShapeDtypeStruct((rows, 256), F32),
            jax.ShapeDtypeStruct((2 * M + 8, M), F32),
        ),
        in_specs=[VMEM] * 6,
        out_specs=(VMEM, VMEM),
        scratch_shapes=[pltpu.VMEM(((RB + 3) * 128, 256), BF16)] * 2
        + [pltpu.VMEM((wide, 256), BF16)] * 4
        + [pltpu.VMEM((wide, 256), F32)]
        + [pltpu.VMEM((rows, 256), BF16)] * 2,
        compiler_params=PARAMS,
        cost_estimate=pl.CostEstimate(
            flops=12 * RB * 128 * 256 * 256, bytes_accessed=12 << 20, transcendentals=0
        ),
        name="apply_twice",
    )(band, left_band, right_band, x, x_left, x_right)


def inverse_factor(a, work):
    row = lax.broadcasted_iota(jnp.int32, (M, M), 0)
    col = lax.broadcasted_iota(jnp.int32, (M, M), 1)
    work[:, :M] = a
    work[:, M:] = jnp.where(row == col, 1.0, 0.0)
    sub = lax.broadcasted_iota(jnp.int32, (8, M), 0)
    sub2 = lax.broadcasted_iota(jnp.int32, (8, 2 * M), 0)
    for p in range(M // 8):
        at = slice(8 * p, 8 * p + 8)
        panel = work[at, :]
        cols = [
            jnp.broadcast_to(panel[:, 8 * p + k : 8 * p + k + 1], (8, M)) for k in range(8)
        ]
        scales = jnp.zeros((8, M), F32)
        for j in range(8):
            pivot = jnp.broadcast_to(cols[j][j : j + 1, :], (8, M))
            root = lax.rsqrt(pivot)
            scales = jnp.where(sub == j, root, scales)
            if j < 7:
                part = jnp.where(sub > j, cols[j] * (root * root), 0.0)
                for k in range(j + 1, 8):
                    cols[k] = cols[k] - part * cols[k][j : j + 1, :]
                panel = panel - jnp.concatenate([part, part], axis=1) * panel[j : j + 1, :]
        panel = panel * jnp.concatenate([scales, scales], axis=1)
        work[at, :] = panel
        if p < M // 8 - 1:
            update = lax.dot_general(
                panel[:, :M], panel, (((0,), (0,)), ((), ())),
                precision=HIGHEST, preferred_element_type=F32,
            )
            work[8 * p + 8 :, :] = work[8 * p + 8 :, :] - update[8 * p + 8 :, :]
    return work[:, M:]


def finish_kernel(total_rows, grams, z, out, work):
    peers = grams.shape[0]
    row = lax.broadcasted_iota(jnp.int32, (M, M), 0)
    col = lax.broadcasted_iota(jnp.int32, (M, M), 1)
    eye = jnp.where(row == col, 1.0, 0.0)

    def as_column(v):
        return jnp.sum(eye * v, axis=1, keepdims=True)

    gram = grams[0, :M, :]
    for r in range(1, peers):
        gram = gram + grams[r, :M, :]
    norm = lax.rsqrt(jnp.sum(eye * gram, axis=0, keepdims=True))
    inverse = inverse_factor(gram * norm * as_column(norm), work)
    gram = jnp.zeros((M, M), F32)
    for r in range(peers):
        size = norm * grams[r, 2 * M : 2 * M + 1, :]
        gram = gram + grams[r, M : 2 * M, :] * size * as_column(size)
    gram = dot_f32(dot_f32(inverse, gram), inverse.T)
    inverse = dot_f32(inverse_factor(gram, work), inverse)
    change = (inverse * (norm * (total_rows**0.5))).T
    c_hi, c_lo = split(change)
    right = jnp.concatenate(
        [
            jnp.concatenate([c_hi, c_lo], axis=1),
            jnp.concatenate([c_hi, jnp.zeros_like(c_lo)], axis=1),
        ],
        axis=0,
    )
    step = 256

    def rows_of(i, carry):
        at = pl.ds(pl.multiple_of(i * step, step), step)
        value = z[at, :]
        for part in range(2):
            hi, lo = split(value[:, part * M : (part + 1) * M])
            both = dot(jnp.concatenate([hi, lo], axis=1), right)
            out[part, at, :] = both[:, :M] + both[:, M:]
        return carry

    lax.fori_loop(0, z.shape[0] // step, rows_of, 0)


def finish(grams, z, total_rows):
    return pl.pallas_call(
        partial(finish_kernel, total_rows),
        out_shape=jax.ShapeDtypeStruct((2, z.shape[0], M), F32),
        in_specs=[VMEM] * 2,
        out_specs=VMEM,
        scratch_shapes=[pltpu.VMEM((M, 2 * M), F32)],
        compiler_params=PARAMS,
        name="finish",
    )(grams, z)


def shifted(x, by):
    peers = lax.axis_size("blk")
    pairs = [(i, i + by) for i in range(peers) if 0 <= i + by < peers]
    return lax.ppermute(x, "blk", pairs)


def per_device(pupils, starts, counts, weights, start_block):
    region = lax.axis_index("blk")
    me = lax.axis_index("src")
    regions = lax.axis_size("blk")
    peers = lax.axis_size("src")
    slots = pupils.shape[0]

    own = pupils.reshape(slots * 2, 2 * BLOCK)
    chunks = [own]
    for k in range(1, peers):
        chunks.append(lax.ppermute(own, "src", [(i, (i + k) % peers) for i in range(peers)]))

    last = jnp.where(starts + 1 < regions * RB, counts, jnp.minimum(counts, 1))
    facts = jnp.stack([(starts - region * RB).astype(F32), weights, last.astype(F32)])
    facts = lax.all_gather(facts, "src", axis=0)
    rows = jnp.tile(facts[:, :2], (1, 1, 2))
    rows = jnp.pad(rows, ((0, 0), (0, 6), (0, 0)))
    live = (jnp.arange(2, dtype=F32)[None, None, :] < facts[:, 2, :, None]).astype(F32)
    live = jnp.broadcast_to(live.reshape(peers, slots * 2, 1), (peers, slots * 2, 2 * BLOCK))

    edge = 2 * BLOCK
    size = start_block.shape[1]
    x_left = shifted(start_block[:, size - edge :], 1)
    x_right = shifted(start_block[:, :edge], -1)

    band = None
    for k in range(peers):
        at = lax.rem(me + peers - k, peers)
        band = build(
            chunks[k],
            lax.dynamic_index_in_dim(live, at, 0, keepdims=False),
            lax.dynamic_index_in_dim(rows, at, 0, keepdims=False),
            band,
        )
    left_band = shifted(band[RB * 128 - 192 :], 1)
    right_band = shifted(band[:BLOCK], -1)
    z, grams = apply_twice(band, left_band, right_band, start_block, x_left, x_right)
    grams = lax.all_gather(grams, "blk", axis=0)
    return finish(grams, z, 2.0 * size * regions)


def solution(mesh):
    placed = (
        P(("groups", "src", "blk"), None, None),
        P(("groups", "src", "blk")),
        P(("groups", "src", "blk")),
        P(("groups", "src", "blk")),
        P("groups", "blk", None),
    )
    return jax.shard_map(
        per_device, mesh=mesh, in_specs=placed, out_specs=P("groups", "blk", None), check_vma=False
    )
```

```python
from functools import partial

import jax
import jax.numpy as jnp
from jax import lax
from jax.experimental import pallas as pl
from jax.experimental.pallas import tpu as pltpu
from jax.sharding import PartitionSpec as P

BLOCK = 64
RB = 32
GROUP = 8
M = 128
F32 = jnp.float32
BF16 = jnp.bfloat16
HIGHEST = lax.Precision.HIGHEST
VMEM = pl.BlockSpec(memory_space=pltpu.VMEM)
PARAMS = pltpu.CompilerParams(vmem_limit_bytes=40 * 1024 * 1024)


def split(x):
    hi = x.astype(BF16)
    return hi, (x - hi.astype(F32)).astype(BF16)


def dot(a, b):
    return jnp.dot(a, b, preferred_element_type=F32)


def dot_t(a, b):
    return lax.dot_general(a, b, (((0,), (0,)), ((), ())), preferred_element_type=F32)


def dot_f32(a, b):
    return jnp.dot(a, b, precision=HIGHEST, preferred_element_type=F32)


def pack_kernel(total_blocks, pupils, starts, counts, weights, out):
    tiles = starts.shape[0]
    lane = lax.broadcasted_iota(jnp.int32, (128, 2 * BLOCK), 1)
    start = starts[...]
    root = jnp.sqrt(weights[...])
    first_live = jnp.where(counts[...] > 0, root, 0.0)
    second_live = jnp.where((counts[...] > 1) & (start + 1 < total_blocks), root, 0.0)
    for t in range(tiles):
        first_column = jnp.broadcast_to(first_live[t : t + 1, :], (128, 128)).T
        second_column = jnp.broadcast_to(second_live[t : t + 1, :], (128, 128)).T
        first = pupils[pl.ds(256 * t, 128, stride=2), :] * first_column
        second = pupils[pl.ds(256 * t + 1, 128, stride=2), :] * second_column
        real = jnp.where(lane < BLOCK, first, pltpu.roll(second, BLOCK, 1))
        imag = jnp.where(lane < BLOCK, pltpu.roll(first, BLOCK, 1), second)
        out[128 * t : 128 * t + 128, :] = real
        out[128 * (tiles + t) : 128 * (tiles + t) + 128, :] = imag
    out[256 * tiles :, :] = jnp.zeros((8, 128), F32)
    out[256 * tiles : 256 * tiles + tiles, :] = lax.rem(start, RB).astype(F32)


def pack(pupils, starts, counts, weights, total_blocks):
    slots = pupils.shape[0]
    return pl.pallas_call(
        partial(pack_kernel, total_blocks),
        out_shape=jax.ShapeDtypeStruct((2 * slots + 8, 128), F32),
        in_specs=[VMEM] * 4,
        out_specs=VMEM,
        compiler_params=PARAMS,
        name="pack",
    )(
        pupils.reshape(2 * slots, 128),
        starts.reshape(-1, 128),
        counts.reshape(-1, 128),
        weights.reshape(-1, 128),
    )


def build_kernel(add, *refs):
    if add:
        chunk, before, out, lhs_hi, lhs_lo = refs
    else:
        chunk, out, lhs_hi, lhs_lo = refs
    count = (chunk.shape[0] - 8) // 2
    real = chunk[:count, :]
    imag = chunk[count : 2 * count, :]
    right = jnp.concatenate(
        [
            jnp.concatenate([real, -imag], axis=1),
            jnp.concatenate([imag, real], axis=1),
        ],
        axis=0,
    )
    right_hi, right_lo = split(right)
    left = jnp.concatenate([real.T, imag.T], axis=1)
    left_hi, left_lo = split(left)
    left_hi = left_hi.reshape(8, 16, 2 * count)
    left_lo = left_lo.reshape(8, 16, 2 * count)
    places = [chunk[2 * count + t : 2 * count + t + 1, :] for t in range(count // 128)]
    place = jnp.broadcast_to(jnp.concatenate(places + places, axis=1), (16, 2 * count))

    def one_group(g, carry):
        for j in range(GROUP):
            b = (g * GROUP + j).astype(F32)
            mask = jnp.where(place == b, 1.0, 0.0).astype(BF16)[None]
            lhs_hi[j * 128 : (j + 1) * 128, :] = (left_hi * mask).reshape(128, 2 * count)
            lhs_lo[j * 128 : (j + 1) * 128, :] = (left_lo * mask).reshape(128, 2 * count)
        at = pl.ds(pl.multiple_of(g * GROUP * 128, GROUP * 128), GROUP * 128)
        hi = lhs_hi[...]
        total = dot(hi, right_hi) + dot(hi, right_lo) + dot(lhs_lo[...], right_hi)
        out[at, :] = before[at, :] + total if add else total
        return carry

    lax.fori_loop(0, RB // GROUP, one_group, 0)


def build(chunk, before):
    count = (chunk.shape[0] - 8) // 2
    args = (chunk,) + (() if before is None else (before,))
    return pl.pallas_call(
        partial(build_kernel, before is not None),
        out_shape=jax.ShapeDtypeStruct((RB * 128, 256), F32),
        in_specs=[VMEM] * len(args),
        out_specs=VMEM,
        scratch_shapes=[pltpu.VMEM((GROUP * 128, 2 * count), BF16)] * 2,
        input_output_aliases={} if before is None else {1: 0},
        compiler_params=PARAMS,
        cost_estimate=pl.CostEstimate(
            flops=6 * RB * 128 * 2 * count * 256, bytes_accessed=10 << 20, transcendentals=0
        ),
        name="band_terms",
    )(*args)


def swapped(x):
    return jnp.concatenate([-x[:, M:], x[:, :M]], axis=1)


def gram_of(hi, lo):
    a = dot_t(hi, hi)
    b = dot_t(hi, lo)
    a = a[:M, :M] + a[M:, M:]
    b = b[:M, :M] + b[M:, M:]
    return a + b + b.T


def apply_kernel(band, left_band, right_band, x, x_left, x_right, z, grams,
                 g_hi, g_lo, x_hi, x_lo, s_hi, s_lo, p, p_hi, p_lo):
    pairs = RB + 3
    zero = jnp.zeros((BLOCK, 256), BF16)

    def put_g(e_rows, value):
        hi, lo = split(value)
        g_hi[e_rows, :] = hi
        g_lo[e_rows, :] = lo

    g_hi[0:BLOCK, :] = zero
    g_lo[0:BLOCK, :] = zero
    put_g(pl.ds(BLOCK, 3 * BLOCK), left_band[...])
    put_g(pl.ds((RB + 2) * 128, BLOCK), right_band[...])
    g_hi[(RB + 2) * 128 + BLOCK :, :] = zero
    g_lo[(RB + 2) * 128 + BLOCK :, :] = zero

    def put_x(at, value):
        hi, lo = split(value)
        x_hi[at, :] = hi
        x_lo[at, :] = lo
        hi, lo = split(swapped(value))
        s_hi[at, :] = hi
        s_lo[at, :] = lo

    put_x(pl.ds(0, 2 * BLOCK), jnp.concatenate([x_left[0], x_left[1]], axis=1))
    put_x(pl.ds((RB + 2) * BLOCK, 2 * BLOCK), jnp.concatenate([x_right[0], x_right[1]], axis=1))

    def prepare(i, carry):
        at = pl.ds(pl.multiple_of(i * 256, 256), 256)
        put_g(pl.ds(pl.multiple_of(256 + i * 256, 256), 256), band[at, :])
        half = pl.ds(pl.multiple_of(i * 128, 128), 128)
        put_x(
            pl.ds(pl.multiple_of(i * 128 + 128, 128), 128),
            jnp.concatenate([x[0, half, :], x[1, half, :]], axis=1),
        )
        return carry

    lax.fori_loop(0, RB // 2, prepare, 0)

    def pair(e):
        at = pl.ds(pl.multiple_of(e * 128, 128), 128)
        win = pl.ds(pl.multiple_of(e * BLOCK, BLOCK), 128)
        w_hi = jnp.concatenate([x_hi[win, :], s_hi[win, :]], axis=0)
        w_lo = jnp.concatenate([x_lo[win, :], s_lo[win, :]], axis=0)
        hi = g_hi[at, :]
        return dot(hi, w_hi) + dot(hi, w_lo) + dot(g_lo[at, :], w_hi)

    def first(e, carry):
        both = pair(e)
        p[pl.ds(pl.multiple_of(e * BLOCK, BLOCK), BLOCK), :] = both[:BLOCK] + carry
        return both[BLOCK:]

    lax.fori_loop(0, pairs, first, jnp.zeros((BLOCK, 256), F32))

    def prepare_again(i, carry):
        at = pl.ds(pl.multiple_of(i * 128, 128), 128)
        put_x(at, p[at, :])
        return carry

    lax.fori_loop(0, (RB + 4) // 2, prepare_again, 0)
    rows = RB * BLOCK
    inner = pl.ds(2 * BLOCK, rows)
    grams[0:M, :] = gram_of(x_hi[inner, :], x_lo[inner, :])

    def second(e, carry):
        both = pair(e)
        z[pl.ds(pl.multiple_of((e - 2) * BLOCK, BLOCK), BLOCK), :] = both[:BLOCK] + carry
        return both[BLOCK:]

    lax.fori_loop(2, RB + 2, second, pair(1)[BLOCK:])

    top = jnp.max(jnp.abs(z[...]), axis=0, keepdims=True)
    top = jnp.maximum(top[:, :M], top[:, M:])
    scale = jnp.where(top > 0, 1.0 / jnp.where(top > 0, top, 1.0), 1.0)
    scale = jnp.concatenate([scale, scale], axis=1)

    def prepare_z(i, carry):
        at = pl.ds(pl.multiple_of(i * 128, 128), 128)
        hi, lo = split(z[at, :] * scale)
        p_hi[at, :] = hi
        p_lo[at, :] = lo
        return carry

    lax.fori_loop(0, rows // 128, prepare_z, 0)
    grams[M : 2 * M, :] = gram_of(p_hi[...], p_lo[...])
    grams[2 * M :, :] = jnp.broadcast_to(top, (8, M))


def apply_twice(band, left_band, right_band, x, x_left, x_right):
    rows = RB * BLOCK
    wide = (RB + 4) * BLOCK
    return pl.pallas_call(
        apply_kernel,
        out_shape=(
            jax.ShapeDtypeStruct((rows, 256), F32),
            jax.ShapeDtypeStruct((2 * M + 8, M), F32),
        ),
        in_specs=[VMEM] * 6,
        out_specs=(VMEM, VMEM),
        scratch_shapes=[pltpu.VMEM(((RB + 3) * 128, 256), BF16)] * 2
        + [pltpu.VMEM((wide, 256), BF16)] * 4
        + [pltpu.VMEM((wide, 256), F32)]
        + [pltpu.VMEM((rows, 256), BF16)] * 2,
        compiler_params=PARAMS,
        cost_estimate=pl.CostEstimate(
            flops=12 * RB * 128 * 256 * 256, bytes_accessed=12 << 20, transcendentals=0
        ),
        name="apply_twice",
    )(band, left_band, right_band, x, x_left, x_right)


def inverse_factor(a, work):
    row = lax.broadcasted_iota(jnp.int32, (M, M), 0)
    col = lax.broadcasted_iota(jnp.int32, (M, M), 1)
    work[:, :M] = a
    work[:, M:] = jnp.where(row == col, 1.0, 0.0)
    sub = lax.broadcasted_iota(jnp.int32, (8, M), 0)
    sub2 = lax.broadcasted_iota(jnp.int32, (8, 2 * M), 0)
    for p in range(M // 8):
        at = slice(8 * p, 8 * p + 8)
        panel = work[at, :]
        cols = [
            jnp.broadcast_to(panel[:, 8 * p + k : 8 * p + k + 1], (8, M)) for k in range(8)
        ]
        scales = jnp.zeros((8, M), F32)
        for j in range(8):
            pivot = jnp.broadcast_to(cols[j][j : j + 1, :], (8, M))
            root = lax.rsqrt(pivot)
            scales = jnp.where(sub == j, root, scales)
            if j < 7:
                part = jnp.where(sub > j, cols[j] * (root * root), 0.0)
                for k in range(j + 1, 8):
                    cols[k] = cols[k] - part * cols[k][j : j + 1, :]
                panel = panel - jnp.concatenate([part, part], axis=1) * panel[j : j + 1, :]
        panel = panel * jnp.concatenate([scales, scales], axis=1)
        work[at, :] = panel
        if p < M // 8 - 1:
            update = lax.dot_general(
                panel[:, :M], panel, (((0,), (0,)), ((), ())),
                precision=HIGHEST, preferred_element_type=F32,
            )
            work[8 * p + 8 :, :] = work[8 * p + 8 :, :] - update[8 * p + 8 :, :]
    return work[:, M:]


def finish_kernel(total_rows, grams, z, out, work):
    peers = grams.shape[0]
    row = lax.broadcasted_iota(jnp.int32, (M, M), 0)
    col = lax.broadcasted_iota(jnp.int32, (M, M), 1)
    eye = jnp.where(row == col, 1.0, 0.0)

    def as_column(v):
        return jnp.sum(eye * v, axis=1, keepdims=True)

    gram = grams[0, :M, :]
    for r in range(1, peers):
        gram = gram + grams[r, :M, :]
    norm = lax.rsqrt(jnp.sum(eye * gram, axis=0, keepdims=True))
    inverse = inverse_factor(gram * norm * as_column(norm), work)
    gram = jnp.zeros((M, M), F32)
    for r in range(peers):
        size = norm * grams[r, 2 * M : 2 * M + 1, :]
        gram = gram + grams[r, M : 2 * M, :] * size * as_column(size)
    gram = dot_f32(dot_f32(inverse, gram), inverse.T)
    inverse = dot_f32(inverse_factor(gram, work), inverse)
    change = (inverse * (norm * (total_rows**0.5))).T
    c_hi, c_lo = split(change)
    right = jnp.concatenate(
        [
            jnp.concatenate([c_hi, c_lo], axis=1),
            jnp.concatenate([c_hi, jnp.zeros_like(c_lo)], axis=1),
        ],
        axis=0,
    )
    step = 256

    def rows_of(i, carry):
        at = pl.ds(pl.multiple_of(i * step, step), step)
        value = z[at, :]
        for part in range(2):
            hi, lo = split(value[:, part * M : (part + 1) * M])
            both = dot(jnp.concatenate([hi, lo], axis=1), right)
            out[part, at, :] = both[:, :M] + both[:, M:]
        return carry

    lax.fori_loop(0, z.shape[0] // step, rows_of, 0)


def finish(grams, z, total_rows):
    return pl.pallas_call(
        partial(finish_kernel, total_rows),
        out_shape=jax.ShapeDtypeStruct((2, z.shape[0], M), F32),
        in_specs=[VMEM] * 2,
        out_specs=VMEM,
        scratch_shapes=[pltpu.VMEM((M, 2 * M), F32)],
        compiler_params=PARAMS,
        name="finish",
    )(grams, z)


def shifted(x, by):
    peers = lax.axis_size("blk")
    pairs = [(i, i + by) for i in range(peers) if 0 <= i + by < peers]
    return lax.ppermute(x, "blk", pairs)


def per_device(pupils, starts, counts, weights, start_block):
    regions = lax.axis_size("blk")
    peers = lax.axis_size("src")

    own = pack(pupils, starts, counts, weights, regions * RB)
    chunks = [own]
    for k in range(1, peers):
        chunks.append(lax.ppermute(own, "src", [(i, (i + k) % peers) for i in range(peers)]))

    edge = 2 * BLOCK
    size = start_block.shape[1]
    x_left = shifted(start_block[:, size - edge :], 1)
    x_right = shifted(start_block[:, :edge], -1)

    band = build(own, None)
    band, x_left, x_right = lax.optimization_barrier((band, x_left, x_right))
    for k in range(1, peers):
        band = build(chunks[k], band)
    left_band = shifted(band[RB * 128 - 192 :], 1)
    right_band = shifted(band[:BLOCK], -1)
    z, grams = apply_twice(band, left_band, right_band, start_block, x_left, x_right)
    grams = lax.all_gather(grams, "blk", axis=0)
    return finish(grams, z, 2.0 * size * regions)


def solution(mesh):
    placed = (
        P(("groups", "src", "blk"), None, None),
        P(("groups", "src", "blk")),
        P(("groups", "src", "blk")),
        P(("groups", "src", "blk")),
        P("groups", "blk", None),
    )
    return jax.shard_map(
        per_device, mesh=mesh, in_specs=placed, out_specs=P("groups", "blk", None), check_vma=False
    )
```

```python
from functools import partial

import jax
import jax.numpy as jnp
from jax import lax
from jax.experimental import pallas as pl
from jax.experimental.pallas import tpu as pltpu
from jax.sharding import PartitionSpec as P

BLOCK = 64
RB = 32
GROUP = 8
UNROLL = 8
OUTER = 64
M = 128
F32 = jnp.float32
BF16 = jnp.bfloat16
HIGHEST = lax.Precision.HIGHEST
VMEM = pl.BlockSpec(memory_space=pltpu.VMEM)
PARAMS = pltpu.CompilerParams(vmem_limit_bytes=40 * 1024 * 1024)


def split(x):
    hi = x.astype(BF16)
    return hi, (x - hi.astype(F32)).astype(BF16)


def dot(a, b):
    return jnp.dot(a, b, preferred_element_type=F32)


def dot_t(a, b):
    return lax.dot_general(a, b, (((0,), (0,)), ((), ())), preferred_element_type=F32)


def dot_f32(a, b):
    return jnp.dot(a, b, precision=HIGHEST, preferred_element_type=F32)


def pack_kernel(total_blocks, *refs):
    sent, out, held, sems = refs[:4], refs[4], refs[5:9], refs[9]
    copies = [pltpu.make_async_copy(sent[i], held[i], sems.at[i]) for i in range(4)]
    for copy in copies:
        copy.start()
    for copy in copies:
        copy.wait()
    pupils, starts, counts, weights = held
    tiles = starts.shape[0]
    lane = lax.broadcasted_iota(jnp.int32, (128, 2 * BLOCK), 1)
    start = starts[...]
    root = jnp.sqrt(weights[...])
    first_live = jnp.where(counts[...] > 0, root, 0.0)
    second_live = jnp.where((counts[...] > 1) & (start + 1 < total_blocks), root, 0.0)
    for t in range(tiles):
        first_column = jnp.broadcast_to(first_live[t : t + 1, :], (128, 128)).T
        second_column = jnp.broadcast_to(second_live[t : t + 1, :], (128, 128)).T
        first = pupils[pl.ds(256 * t, 128, stride=2), :] * first_column
        second = pupils[pl.ds(256 * t + 1, 128, stride=2), :] * second_column
        real = jnp.where(lane < BLOCK, first, pltpu.roll(second, BLOCK, 1))
        imag = jnp.where(lane < BLOCK, pltpu.roll(first, BLOCK, 1), second)
        out[128 * t : 128 * t + 128, :] = real
        out[128 * (tiles + t) : 128 * (tiles + t) + 128, :] = imag
    out[256 * tiles :, :] = jnp.zeros((8, 128), F32)
    out[256 * tiles : 256 * tiles + tiles, :] = lax.rem(start, RB).astype(F32)


def pack(pupils, starts, counts, weights, total_blocks):
    slots = pupils.shape[0]
    return pl.pallas_call(
        partial(pack_kernel, total_blocks),
        out_shape=jax.ShapeDtypeStruct((2 * slots + 8, 128), F32),
        in_specs=[pl.BlockSpec(memory_space=pltpu.HBM)] * 4,
        out_specs=VMEM,
        scratch_shapes=[
            pltpu.VMEM((2 * slots, 128), F32),
            pltpu.VMEM((slots // 128, 128), jnp.int32),
            pltpu.VMEM((slots // 128, 128), jnp.int32),
            pltpu.VMEM((slots // 128, 128), F32),
            pltpu.SemaphoreType.DMA((4,)),
        ],
        compiler_params=PARAMS,
        name="pack",
    )(
        pupils.reshape(2 * slots, 128),
        starts.reshape(-1, 128),
        counts.reshape(-1, 128),
        weights.reshape(-1, 128),
    )


def build_kernel(add, *refs):
    if add:
        chunk, before, out, lhs_hi, lhs_lo = refs
    else:
        chunk, out, lhs_hi, lhs_lo = refs
    count = (chunk.shape[0] - 8) // 2
    real = chunk[:count, :]
    imag = chunk[count : 2 * count, :]
    right = jnp.concatenate(
        [
            jnp.concatenate([real, -imag], axis=1),
            jnp.concatenate([imag, real], axis=1),
        ],
        axis=0,
    )
    right_hi, right_lo = split(right)
    left = jnp.concatenate([real.T, imag.T], axis=1)
    left_hi, left_lo = split(left)
    left_hi = left_hi.reshape(8, 16, 2 * count)
    left_lo = left_lo.reshape(8, 16, 2 * count)
    places = [chunk[2 * count + t : 2 * count + t + 1, :] for t in range(count // 128)]
    place = jnp.broadcast_to(jnp.concatenate(places + places, axis=1), (16, 2 * count))

    def one_group(g, carry):
        for j in range(GROUP):
            b = (g * GROUP + j).astype(F32)
            mask = jnp.where(place == b, 1.0, 0.0).astype(BF16)[None]
            lhs_hi[j * 128 : (j + 1) * 128, :] = (left_hi * mask).reshape(128, 2 * count)
            lhs_lo[j * 128 : (j + 1) * 128, :] = (left_lo * mask).reshape(128, 2 * count)
        at = pl.ds(pl.multiple_of(g * GROUP * 128, GROUP * 128), GROUP * 128)
        hi = lhs_hi[...]
        total = dot(hi, right_hi) + dot(hi, right_lo) + dot(lhs_lo[...], right_hi)
        out[at, :] = before[at, :] + total if add else total
        return carry

    lax.fori_loop(0, RB // GROUP, one_group, 0)


def build(chunk, before):
    count = (chunk.shape[0] - 8) // 2
    args = (chunk,) + (() if before is None else (before,))
    return pl.pallas_call(
        partial(build_kernel, before is not None),
        out_shape=jax.ShapeDtypeStruct((RB * 128, 256), F32),
        in_specs=[VMEM] * len(args),
        out_specs=VMEM,
        scratch_shapes=[pltpu.VMEM((GROUP * 128, 2 * count), BF16)] * 2,
        input_output_aliases={} if before is None else {1: 0},
        compiler_params=PARAMS,
        cost_estimate=pl.CostEstimate(
            flops=6 * RB * 128 * 2 * count * 256, bytes_accessed=10 << 20, transcendentals=0
        ),
        name="band_terms",
    )(*args)


def swapped(x):
    return jnp.concatenate([-x[:, M:], x[:, :M]], axis=1)


def gram_of(hi, lo):
    a = dot_t(hi, hi)
    b = dot_t(hi, lo)
    a = a[:M, :M] + a[M:, M:]
    b = b[:M, :M] + b[M:, M:]
    return a + b + b.T


def apply_kernel(band, left_band, right_band, x, x_left, x_right, z, grams,
                 g_hi, g_lo, x_hi, x_lo, s_hi, s_lo, p, p_hi, p_lo):
    pairs = RB + 3
    zero = jnp.zeros((BLOCK, 256), BF16)

    def put_g(e_rows, value):
        hi, lo = split(value)
        g_hi[e_rows, :] = hi
        g_lo[e_rows, :] = lo

    g_hi[0:BLOCK, :] = zero
    g_lo[0:BLOCK, :] = zero
    put_g(pl.ds(BLOCK, 3 * BLOCK), left_band[...])
    put_g(pl.ds((RB + 2) * 128, BLOCK), right_band[...])
    g_hi[(RB + 2) * 128 + BLOCK :, :] = zero
    g_lo[(RB + 2) * 128 + BLOCK :, :] = zero

    def put_x(at, value):
        hi, lo = split(value)
        x_hi[at, :] = hi
        x_lo[at, :] = lo
        hi, lo = split(swapped(value))
        s_hi[at, :] = hi
        s_lo[at, :] = lo

    put_x(pl.ds(0, 2 * BLOCK), jnp.concatenate([x_left[0], x_left[1]], axis=1))
    put_x(pl.ds((RB + 2) * BLOCK, 2 * BLOCK), jnp.concatenate([x_right[0], x_right[1]], axis=1))

    def prepare(i, carry):
        at = pl.ds(pl.multiple_of(i * 256, 256), 256)
        put_g(pl.ds(pl.multiple_of(256 + i * 256, 256), 256), band[at, :])
        half = pl.ds(pl.multiple_of(i * 128, 128), 128)
        put_x(
            pl.ds(pl.multiple_of(i * 128 + 128, 128), 128),
            jnp.concatenate([x[0, half, :], x[1, half, :]], axis=1),
        )
        return carry

    lax.fori_loop(0, RB // 2, prepare, 0)

    def pair(e):
        at = pl.ds(pl.multiple_of(e * 128, 128), 128)
        win = pl.ds(pl.multiple_of(e * BLOCK, BLOCK), 128)
        w_hi = jnp.concatenate([x_hi[win, :], s_hi[win, :]], axis=0)
        w_lo = jnp.concatenate([x_lo[win, :], s_lo[win, :]], axis=0)
        hi = g_hi[at, :]
        return dot(hi, w_hi) + dot(hi, w_lo) + dot(g_lo[at, :], w_hi)

    def first(e, carry):
        both = pair(e)
        p[pl.ds(pl.multiple_of(e * BLOCK, BLOCK), BLOCK), :] = both[:BLOCK] + carry
        return both[BLOCK:]

    lax.fori_loop(0, pairs, first, jnp.zeros((BLOCK, 256), F32), unroll=UNROLL)

    def prepare_again(i, carry):
        at = pl.ds(pl.multiple_of(i * 128, 128), 128)
        put_x(at, p[at, :])
        return carry

    lax.fori_loop(0, (RB + 4) // 2, prepare_again, 0)
    rows = RB * BLOCK
    inner = pl.ds(2 * BLOCK, rows)
    gram_1 = gram_of(x_hi[inner, :], x_lo[inner, :])

    def second(e, carry):
        both = pair(e)
        z[pl.ds(pl.multiple_of((e - 2) * BLOCK, BLOCK), BLOCK), :] = both[:BLOCK] + carry
        return both[BLOCK:]

    lax.fori_loop(2, RB + 2, second, pair(1)[BLOCK:], unroll=UNROLL)

    top = jnp.max(jnp.abs(z[...]), axis=0, keepdims=True)
    top = jnp.maximum(top[:, :M], top[:, M:])
    scale = jnp.where(top > 0, 1.0 / jnp.where(top > 0, top, 1.0), 1.0)
    scale = jnp.concatenate([scale, scale], axis=1)

    def prepare_z(i, carry):
        at = pl.ds(pl.multiple_of(i * 128, 128), 128)
        hi, lo = split(z[at, :] * scale)
        p_hi[at, :] = hi
        p_lo[at, :] = lo
        return carry

    lax.fori_loop(0, rows // 128, prepare_z, 0)
    gram_2 = gram_of(p_hi[...], p_lo[...])
    row = lax.broadcasted_iota(jnp.int32, (M, M), 0)
    col = lax.broadcasted_iota(jnp.int32, (M, M), 1)
    grams[:M, :] = jnp.where(row >= col, gram_1, gram_2)
    diagonal = jnp.sum(jnp.where(row == col, gram_2, 0.0), axis=0, keepdims=True)
    grams[M:, :] = jnp.concatenate([diagonal, top, jnp.zeros((6, M), F32)], axis=0)


def apply_twice(band, left_band, right_band, x, x_left, x_right):
    rows = RB * BLOCK
    wide = (RB + 4) * BLOCK
    return pl.pallas_call(
        apply_kernel,
        out_shape=(
            jax.ShapeDtypeStruct((rows, 256), F32),
            jax.ShapeDtypeStruct((M + 8, M), F32),
        ),
        in_specs=[VMEM] * 6,
        out_specs=(VMEM, VMEM),
        scratch_shapes=[pltpu.VMEM(((RB + 3) * 128, 256), BF16)] * 2
        + [pltpu.VMEM((wide, 256), BF16)] * 4
        + [pltpu.VMEM((wide, 256), F32)]
        + [pltpu.VMEM((rows, 256), BF16)] * 2,
        compiler_params=PARAMS,
        cost_estimate=pl.CostEstimate(
            flops=12 * RB * 128 * 256 * 256, bytes_accessed=12 << 20, transcendentals=0
        ),
        name="apply_twice",
    )(band, left_band, right_band, x, x_left, x_right)


def inverse_factor(a, work):
    row = lax.broadcasted_iota(jnp.int32, (M, M), 0)
    col = lax.broadcasted_iota(jnp.int32, (M, M), 1)
    work[:, :M] = a
    work[:, M:] = jnp.where(row == col, 1.0, 0.0)
    sub = lax.broadcasted_iota(jnp.int32, (8, M), 0)
    groups = OUTER // 8

    def line(x, j):
        return x[j : j + 1, :]

    def wide(x, j):
        return jnp.broadcast_to(line(x, j), (8, M))

    for top in range(0, M, OUTER):
        left = [work[top + 8 * g : top + 8 * g + 8, :M] for g in range(groups)]
        right = [work[top + 8 * g : top + 8 * g + 8, M:] for g in range(groups)]
        for q in range(groups):
            at = top + 8 * q
            cols = {
                g: [jnp.broadcast_to(left[g][:, at + k : at + k + 1], (8, M)) for k in range(8)]
                for g in range(q, groups)
            }
            scales = jnp.zeros((8, M), F32)
            for j in range(0, 8, 2):
                a0, a1, a2 = wide(cols[q][j], j), wide(cols[q][j], j + 1), wide(cols[q][j + 1], j + 1)
                det = a0 * a2 - a1 * a1
                inverse = pltpu.reciprocal(det, approx=False)
                root = lax.rsqrt(a0)
                ratio = a1 * (root * root)
                scales = jnp.where(sub == j, root, scales)
                scales = jnp.where(sub == j + 1, lax.rsqrt(det) * (a0 * root), scales)
                row_0 = [line(cols[q][k], j) for k in range(8)]
                row_1 = [line(cols[q][k], j + 1) for k in range(8)]
                left_0, left_1 = line(left[q], j), line(left[q], j + 1)
                right_0, right_1 = line(right[q], j), line(right[q], j + 1)
                for g in range(q, groups):
                    c0, c1 = cols[g][j], cols[g][j + 1]
                    y0 = a2 * c0 - a1 * c1
                    y1 = a0 * c1 - a1 * c0
                    if g == q:
                        y0 = jnp.where(sub > j + 1, y0, 0.0)
                        y1 = jnp.where(sub > j + 1, y1, 0.0)
                    for k in range(j + 2, 8):
                        cols[g][k] = cols[g][k] - (y0 * row_0[k] + y1 * row_1[k]) * inverse
                    x0, x1 = y0 * inverse, y1 * inverse
                    if g == q:
                        x0 = jnp.where(sub == j + 1, ratio, x0)
                    left[g] = left[g] - (x0 * left_0 + x1 * left_1)
                    right[g] = right[g] - (x0 * right_0 + x1 * right_1)
            left[q] = left[q] * scales
            right[q] = right[q] * scales
        for g in range(groups):
            work[top + 8 * g : top + 8 * g + 8, :M] = left[g]
            work[top + 8 * g : top + 8 * g + 8, M:] = right[g]
        if top + OUTER < M:
            panel = work[top : top + OUTER, :]
            update = lax.dot_general(
                panel[:, :M], panel, (((0,), (0,)), ((), ())),
                precision=HIGHEST, preferred_element_type=F32,
            )
            work[top + OUTER :, :] = work[top + OUTER :, :] - update[top + OUTER :, :]
    return work[:, M:]


def finish_kernel(total_rows, grams, z, out, work):
    peers = grams.shape[0]
    row = lax.broadcasted_iota(jnp.int32, (M, M), 0)
    col = lax.broadcasted_iota(jnp.int32, (M, M), 1)
    eye = jnp.where(row == col, 1.0, 0.0)

    def as_column(v):
        return jnp.sum(eye * v, axis=1, keepdims=True)

    def row_of(x):
        return jnp.sum(eye * x, axis=0, keepdims=True)

    total = grams[0, :M, :]
    for r in range(1, peers):
        total = total + grams[r, :M, :]
    gram = jnp.where(row >= col, total, total.T)
    norm = lax.rsqrt(row_of(gram))
    inverse = inverse_factor(gram * norm * as_column(norm), work)
    total = jnp.zeros((M, M), F32)
    for r in range(peers):
        size = norm * grams[r, M + 1 : M + 2, :]
        second = jnp.where(row == col, grams[r, M : M + 1, :], grams[r, :M, :])
        total = total + second * size * as_column(size)
    gram = jnp.where(row <= col, total, total.T)
    gram = dot_f32(dot_f32(inverse, gram), inverse.T)
    scale = lax.rsqrt(row_of(gram))
    second = inverse_factor(gram * scale * as_column(scale), work) * scale
    inverse = dot_f32(second, inverse)
    change = (inverse * (norm * (total_rows**0.5))).T
    c_hi, c_lo = split(change)
    right = jnp.concatenate(
        [
            jnp.concatenate([c_hi, c_lo], axis=1),
            jnp.concatenate([c_hi, jnp.zeros_like(c_lo)], axis=1),
        ],
        axis=0,
    )
    step = 256

    def rows_of(i, carry):
        at = pl.ds(pl.multiple_of(i * step, step), step)
        value = z[at, :]
        for part in range(2):
            hi, lo = split(value[:, part * M : (part + 1) * M])
            both = dot(jnp.concatenate([hi, lo], axis=1), right)
            out[part, at, :] = both[:, :M] + both[:, M:]
        return carry

    lax.fori_loop(0, z.shape[0] // step, rows_of, 0, unroll=2)


def finish(grams, z, total_rows):
    return pl.pallas_call(
        partial(finish_kernel, total_rows),
        out_shape=jax.ShapeDtypeStruct((2, z.shape[0], M), F32),
        in_specs=[VMEM] * 2,
        out_specs=VMEM,
        scratch_shapes=[pltpu.VMEM((M, 2 * M), F32)],
        compiler_params=PARAMS,
        name="finish",
    )(grams, z)


def shifted(x, by):
    peers = lax.axis_size("blk")
    pairs = [(i, i + by) for i in range(peers) if 0 <= i + by < peers]
    return lax.ppermute(x, "blk", pairs)


def per_device(pupils, starts, counts, weights, start_block):
    regions = lax.axis_size("blk")
    peers = lax.axis_size("src")

    own = pack(pupils, starts, counts, weights, regions * RB)
    chunks = [own]
    for k in range(1, peers):
        chunks.append(lax.ppermute(own, "src", [(i, (i + k) % peers) for i in range(peers)]))

    edge = 2 * BLOCK
    size = start_block.shape[1]
    x_left = shifted(start_block[:, size - edge :], 1)
    x_right = shifted(start_block[:, :edge], -1)

    band = build(own, None)
    band, x_left, x_right = lax.optimization_barrier((band, x_left, x_right))
    for k in range(1, peers):
        band = build(chunks[k], band)
    left_band = shifted(band[RB * 128 - 192 :], 1)
    right_band = shifted(band[:BLOCK], -1)
    z, grams = apply_twice(band, left_band, right_band, start_block, x_left, x_right)
    grams = lax.all_gather(grams, "blk", axis=0)
    return finish(grams, z, 2.0 * size * regions)


def solution(mesh):
    placed = (
        P(("groups", "src", "blk"), None, None),
        P(("groups", "src", "blk")),
        P(("groups", "src", "blk")),
        P(("groups", "src", "blk")),
        P("groups", "blk", None),
    )
    return jax.shard_map(
        per_device, mesh=mesh, in_specs=placed, out_specs=P("groups", "blk", None), check_vma=False
    )
```

```python
from functools import partial

import jax
import jax.numpy as jnp
from jax import lax
from jax.experimental import pallas as pl
from jax.experimental.pallas import tpu as pltpu
from jax.sharding import PartitionSpec as P

BLOCK = 64
RB = 32
GROUP = 8
UNROLL = 8
OUTER = 64
M = 128
F32 = jnp.float32
BF16 = jnp.bfloat16
HIGHEST = lax.Precision.HIGHEST
VMEM = pl.BlockSpec(memory_space=pltpu.VMEM)
PARAMS = pltpu.CompilerParams(vmem_limit_bytes=40 * 1024 * 1024)


def split(x):
    hi = x.astype(BF16)
    return hi, (x - hi.astype(F32)).astype(BF16)


def dot(a, b):
    return jnp.dot(a, b, preferred_element_type=F32)


def dot_t(a, b):
    return lax.dot_general(a, b, (((0,), (0,)), ((), ())), preferred_element_type=F32)


def dot_f32(a, b):
    return jnp.dot(a, b, precision=HIGHEST, preferred_element_type=F32)


def pack_kernel(total_blocks, *refs):
    sent, out, held, sems = refs[:4], refs[4], refs[5:9], refs[9]
    copies = [pltpu.make_async_copy(sent[i], held[i], sems.at[i]) for i in range(4)]
    for copy in copies:
        copy.start()
    for copy in copies:
        copy.wait()
    pupils, starts, counts, weights = held
    tiles = starts.shape[0]
    lane = lax.broadcasted_iota(jnp.int32, (128, 2 * BLOCK), 1)
    start = starts[...]
    root = jnp.sqrt(weights[...])
    first_live = jnp.where(counts[...] > 0, root, 0.0)
    second_live = jnp.where((counts[...] > 1) & (start + 1 < total_blocks), root, 0.0)
    for t in range(tiles):
        first_column = jnp.broadcast_to(first_live[t : t + 1, :], (128, 128)).T
        second_column = jnp.broadcast_to(second_live[t : t + 1, :], (128, 128)).T
        first = pupils[pl.ds(256 * t, 128, stride=2), :] * first_column
        second = pupils[pl.ds(256 * t + 1, 128, stride=2), :] * second_column
        real = jnp.where(lane < BLOCK, first, pltpu.roll(second, BLOCK, 1))
        imag = jnp.where(lane < BLOCK, pltpu.roll(first, BLOCK, 1), second)
        out[128 * t : 128 * t + 128, :] = real
        out[128 * (tiles + t) : 128 * (tiles + t) + 128, :] = imag
    out[256 * tiles :, :] = jnp.zeros((8, 128), F32)
    out[256 * tiles : 256 * tiles + tiles, :] = lax.rem(start, RB).astype(F32)


def pack(pupils, starts, counts, weights, total_blocks):
    slots = pupils.shape[0]
    return pl.pallas_call(
        partial(pack_kernel, total_blocks),
        out_shape=jax.ShapeDtypeStruct((2 * slots + 8, 128), F32),
        in_specs=[pl.BlockSpec(memory_space=pl.ANY)] * 4,
        out_specs=VMEM,
        scratch_shapes=[
            pltpu.VMEM((2 * slots, 128), F32),
            pltpu.VMEM((slots // 128, 128), jnp.int32),
            pltpu.VMEM((slots // 128, 128), jnp.int32),
            pltpu.VMEM((slots // 128, 128), F32),
            pltpu.SemaphoreType.DMA((4,)),
        ],
        compiler_params=PARAMS,
        name="pack",
    )(
        *(
            pltpu.with_memory_space_constraint(x, pltpu.HBM)
            for x in (
                pupils.reshape(2 * slots, 128),
                starts.reshape(-1, 128),
                counts.reshape(-1, 128),
                weights.reshape(-1, 128),
            )
        )
    )


def factors(chunk):
    count = (chunk.shape[0] - 8) // 2
    real = chunk[:count, :]
    imag = chunk[count : 2 * count, :]
    right = jnp.concatenate(
        [
            jnp.concatenate([real, -imag], axis=1),
            jnp.concatenate([imag, real], axis=1),
        ],
        axis=0,
    )
    left = jnp.concatenate([real.T, imag.T], axis=1)
    places = [chunk[2 * count + t : 2 * count + t + 1, :] for t in range(count // 128)]
    place = jnp.broadcast_to(jnp.concatenate(places + places, axis=1), (16, 2 * count))
    return split(left), split(right), place


def at_block(part, place, b):
    mask = jnp.where(place == b, 1.0, 0.0).astype(BF16)[None]
    return (part.reshape(8, 16, -1) * mask).reshape(part.shape)


def build_kernel(add, *refs):
    if add:
        chunk, before, out, lhs_hi, lhs_lo = refs
    else:
        chunk, out, lhs_hi, lhs_lo = refs
    (left_hi, left_lo), (right_hi, right_lo), place = factors(chunk)

    def one_group(g, carry):
        for j in range(GROUP):
            b = (g * GROUP + j).astype(F32)
            lhs_hi[j * 128 : (j + 1) * 128, :] = at_block(left_hi, place, b)
            lhs_lo[j * 128 : (j + 1) * 128, :] = at_block(left_lo, place, b)
        at = pl.ds(pl.multiple_of(g * GROUP * 128, GROUP * 128), GROUP * 128)
        hi = lhs_hi[...]
        total = dot(hi, right_hi) + dot(hi, right_lo) + dot(lhs_lo[...], right_hi)
        out[at, :] = before[at, :] + total if add else total
        return carry

    lax.fori_loop(0, RB // GROUP, one_group, 0)


def build(chunk, before):
    count = (chunk.shape[0] - 8) // 2
    args = (chunk,) + (() if before is None else (before,))
    return pl.pallas_call(
        partial(build_kernel, before is not None),
        out_shape=jax.ShapeDtypeStruct((RB * 128, 256), F32),
        in_specs=[VMEM] * len(args),
        out_specs=VMEM,
        scratch_shapes=[pltpu.VMEM((GROUP * 128, 2 * count), BF16)] * 2,
        input_output_aliases={} if before is None else {1: 0},
        compiler_params=PARAMS,
        cost_estimate=pl.CostEstimate(
            flops=6 * RB * 128 * 2 * count * 256, bytes_accessed=10 << 20, transcendentals=0
        ),
        name="band_terms",
    )(*args)


def edge_kernel(chunk, before, after_out, before_out):
    (left_hi, left_lo), (right_hi, right_lo), place = factors(chunk)
    hi = jnp.concatenate([at_block(left_hi, place, float(b)) for b in (0, RB - 2, RB - 1)], axis=0)
    lo = jnp.concatenate([at_block(left_lo, place, float(b)) for b in (0, RB - 2, RB - 1)], axis=0)
    total = dot(hi, right_hi) + dot(hi, right_lo) + dot(lo, right_hi)
    after_out[...] = before[RB * 128 - 192 :, :] + total[192:]
    before_out[...] = before[:BLOCK, :] + total[:BLOCK]


def build_edges(chunk, before):
    return pl.pallas_call(
        edge_kernel,
        out_shape=(
            jax.ShapeDtypeStruct((3 * BLOCK, 256), F32),
            jax.ShapeDtypeStruct((BLOCK, 256), F32),
        ),
        in_specs=[VMEM] * 2,
        out_specs=(VMEM, VMEM),
        compiler_params=PARAMS,
        name="edge_terms",
    )(chunk, before)


def swapped(x):
    return jnp.concatenate([-x[:, M:], x[:, :M]], axis=1)


def gram_of(hi, lo):
    a = dot_t(hi, hi)
    b = dot_t(hi, lo)
    a = a[:M, :M] + a[M:, M:]
    b = b[:M, :M] + b[M:, M:]
    return a + b + b.T


def apply_kernel(band, left_band, right_band, x, x_left, x_right, z, grams,
                 g_hi, g_lo, x_hi, x_lo, s_hi, s_lo, p, p_hi, p_lo):
    pairs = RB + 3
    zero = jnp.zeros((BLOCK, 256), BF16)

    def put_g(e_rows, value):
        hi, lo = split(value)
        g_hi[e_rows, :] = hi
        g_lo[e_rows, :] = lo

    g_hi[0:BLOCK, :] = zero
    g_lo[0:BLOCK, :] = zero
    put_g(pl.ds(BLOCK, 3 * BLOCK), left_band[...])
    put_g(pl.ds((RB + 2) * 128, BLOCK), right_band[...])
    g_hi[(RB + 2) * 128 + BLOCK :, :] = zero
    g_lo[(RB + 2) * 128 + BLOCK :, :] = zero

    def put_x(at, value):
        hi, lo = split(value)
        x_hi[at, :] = hi
        x_lo[at, :] = lo
        hi, lo = split(swapped(value))
        s_hi[at, :] = hi
        s_lo[at, :] = lo

    put_x(pl.ds(0, 2 * BLOCK), jnp.concatenate([x_left[0], x_left[1]], axis=1))
    put_x(pl.ds((RB + 2) * BLOCK, 2 * BLOCK), jnp.concatenate([x_right[0], x_right[1]], axis=1))

    def prepare(i, carry):
        at = pl.ds(pl.multiple_of(i * 256, 256), 256)
        put_g(pl.ds(pl.multiple_of(256 + i * 256, 256), 256), band[at, :])
        half = pl.ds(pl.multiple_of(i * 128, 128), 128)
        put_x(
            pl.ds(pl.multiple_of(i * 128 + 128, 128), 128),
            jnp.concatenate([x[0, half, :], x[1, half, :]], axis=1),
        )
        return carry

    lax.fori_loop(0, RB // 2, prepare, 0)

    def pair(e):
        at = pl.ds(pl.multiple_of(e * 128, 128), 128)
        win = pl.ds(pl.multiple_of(e * BLOCK, BLOCK), 128)
        w_hi = jnp.concatenate([x_hi[win, :], s_hi[win, :]], axis=0)
        w_lo = jnp.concatenate([x_lo[win, :], s_lo[win, :]], axis=0)
        hi = g_hi[at, :]
        return dot(hi, w_hi) + dot(hi, w_lo) + dot(g_lo[at, :], w_hi)

    def first(e, carry):
        both = pair(e)
        p[pl.ds(pl.multiple_of(e * BLOCK, BLOCK), BLOCK), :] = both[:BLOCK] + carry
        return both[BLOCK:]

    lax.fori_loop(0, pairs, first, jnp.zeros((BLOCK, 256), F32), unroll=UNROLL)

    def prepare_again(i, carry):
        at = pl.ds(pl.multiple_of(i * 128, 128), 128)
        put_x(at, p[at, :])
        return carry

    lax.fori_loop(0, (RB + 4) // 2, prepare_again, 0)
    rows = RB * BLOCK
    inner = pl.ds(2 * BLOCK, rows)
    gram_1 = gram_of(x_hi[inner, :], x_lo[inner, :])

    def second(e, carry):
        both = pair(e)
        z[pl.ds(pl.multiple_of((e - 2) * BLOCK, BLOCK), BLOCK), :] = both[:BLOCK] + carry
        return both[BLOCK:]

    lax.fori_loop(2, RB + 2, second, pair(1)[BLOCK:], unroll=UNROLL)

    top = jnp.max(jnp.abs(z[...]), axis=0, keepdims=True)
    top = jnp.maximum(top[:, :M], top[:, M:])
    scale = jnp.where(top > 0, 1.0 / jnp.where(top > 0, top, 1.0), 1.0)
    scale = jnp.concatenate([scale, scale], axis=1)

    def prepare_z(i, carry):
        at = pl.ds(pl.multiple_of(i * 128, 128), 128)
        hi, lo = split(z[at, :] * scale)
        p_hi[at, :] = hi
        p_lo[at, :] = lo
        return carry

    lax.fori_loop(0, rows // 128, prepare_z, 0)
    gram_2 = gram_of(p_hi[...], p_lo[...])
    row = lax.broadcasted_iota(jnp.int32, (M, M), 0)
    col = lax.broadcasted_iota(jnp.int32, (M, M), 1)
    grams[:M, :] = jnp.where(row >= col, gram_1, gram_2)
    diagonal = jnp.sum(jnp.where(row == col, gram_2, 0.0), axis=0, keepdims=True)
    grams[M:, :] = jnp.concatenate([diagonal, top, jnp.zeros((6, M), F32)], axis=0)


def apply_twice(band, left_band, right_band, x, x_left, x_right):
    rows = RB * BLOCK
    wide = (RB + 4) * BLOCK
    return pl.pallas_call(
        apply_kernel,
        out_shape=(
            jax.ShapeDtypeStruct((rows, 256), F32),
            jax.ShapeDtypeStruct((M + 8, M), F32),
        ),
        in_specs=[VMEM] * 6,
        out_specs=(VMEM, VMEM),
        scratch_shapes=[pltpu.VMEM(((RB + 3) * 128, 256), BF16)] * 2
        + [pltpu.VMEM((wide, 256), BF16)] * 4
        + [pltpu.VMEM((wide, 256), F32)]
        + [pltpu.VMEM((rows, 256), BF16)] * 2,
        compiler_params=PARAMS,
        cost_estimate=pl.CostEstimate(
            flops=12 * RB * 128 * 256 * 256, bytes_accessed=12 << 20, transcendentals=0
        ),
        name="apply_twice",
    )(band, left_band, right_band, x, x_left, x_right)


def inverse_factor(a, work):
    row = lax.broadcasted_iota(jnp.int32, (M, M), 0)
    col = lax.broadcasted_iota(jnp.int32, (M, M), 1)
    work[:, :M] = a
    work[:, M:] = jnp.where(row == col, 1.0, 0.0)
    sub = lax.broadcasted_iota(jnp.int32, (8, M), 0)
    groups = OUTER // 8

    def line(x, j):
        return x[j : j + 1, :]

    def wide(x, j):
        return jnp.broadcast_to(line(x, j), (8, M))

    for top in range(0, M, OUTER):
        left = [work[top + 8 * g : top + 8 * g + 8, :M] for g in range(groups)]
        right = [work[top + 8 * g : top + 8 * g + 8, M:] for g in range(groups)]
        for q in range(groups):
            at = top + 8 * q
            cols = {
                g: [jnp.broadcast_to(left[g][:, at + k : at + k + 1], (8, M)) for k in range(8)]
                for g in range(q, groups)
            }
            scales = jnp.zeros((8, M), F32)
            for j in range(0, 8, 2):
                a0, a1, a2 = wide(cols[q][j], j), wide(cols[q][j], j + 1), wide(cols[q][j + 1], j + 1)
                det = a0 * a2 - a1 * a1
                inverse = pltpu.reciprocal(det, approx=False)
                root = lax.rsqrt(a0)
                ratio = a1 * (root * root)
                scales = jnp.where(sub == j, root, scales)
                scales = jnp.where(sub == j + 1, lax.rsqrt(det) * (a0 * root), scales)
                row_0 = [line(cols[q][k], j) for k in range(8)]
                row_1 = [line(cols[q][k], j + 1) for k in range(8)]
                left_0, left_1 = line(left[q], j), line(left[q], j + 1)
                right_0, right_1 = line(right[q], j), line(right[q], j + 1)
                for g in range(q, groups):
                    c0, c1 = cols[g][j], cols[g][j + 1]
                    y0 = a2 * c0 - a1 * c1
                    y1 = a0 * c1 - a1 * c0
                    if g == q:
                        y0 = jnp.where(sub > j + 1, y0, 0.0)
                        y1 = jnp.where(sub > j + 1, y1, 0.0)
                    for k in range(j + 2, 8):
                        cols[g][k] = cols[g][k] - (y0 * row_0[k] + y1 * row_1[k]) * inverse
                    x0, x1 = y0 * inverse, y1 * inverse
                    if g == q:
                        x0 = jnp.where(sub == j + 1, ratio, x0)
                    left[g] = left[g] - (x0 * left_0 + x1 * left_1)
                    right[g] = right[g] - (x0 * right_0 + x1 * right_1)
            left[q] = left[q] * scales
            right[q] = right[q] * scales
        for g in range(groups):
            work[top + 8 * g : top + 8 * g + 8, :M] = left[g]
            work[top + 8 * g : top + 8 * g + 8, M:] = right[g]
        if top + OUTER < M:
            panel = work[top : top + OUTER, :]
            update = lax.dot_general(
                panel[:, :M], panel, (((0,), (0,)), ((), ())),
                precision=HIGHEST, preferred_element_type=F32,
            )
            work[top + OUTER :, :] = work[top + OUTER :, :] - update[top + OUTER :, :]
    return work[:, M:]


def finish_kernel(total_rows, grams, z, out, work):
    peers = grams.shape[0]
    row = lax.broadcasted_iota(jnp.int32, (M, M), 0)
    col = lax.broadcasted_iota(jnp.int32, (M, M), 1)
    eye = jnp.where(row == col, 1.0, 0.0)

    def as_column(v):
        return jnp.sum(eye * v, axis=1, keepdims=True)

    def row_of(x):
        return jnp.sum(eye * x, axis=0, keepdims=True)

    total = grams[0, :M, :]
    for r in range(1, peers):
        total = total + grams[r, :M, :]
    gram = jnp.where(row >= col, total, total.T)
    norm = lax.rsqrt(row_of(gram))
    inverse = inverse_factor(gram * norm * as_column(norm), work)
    total = jnp.zeros((M, M), F32)
    for r in range(peers):
        size = norm * grams[r, M + 1 : M + 2, :]
        second = jnp.where(row == col, grams[r, M : M + 1, :], grams[r, :M, :])
        total = total + second * size * as_column(size)
    gram = jnp.where(row <= col, total, total.T)
    gram = dot_f32(dot_f32(inverse, gram), inverse.T)
    scale = lax.rsqrt(row_of(gram))
    second = inverse_factor(gram * scale * as_column(scale), work) * scale
    inverse = dot_f32(second, inverse)
    change = (inverse * (norm * (total_rows**0.5))).T
    c_hi, c_lo = split(change)
    right = jnp.concatenate(
        [
            jnp.concatenate([c_hi, c_lo], axis=1),
            jnp.concatenate([c_hi, jnp.zeros_like(c_lo)], axis=1),
        ],
        axis=0,
    )
    step = 256

    def rows_of(i, carry):
        at = pl.ds(pl.multiple_of(i * step, step), step)
        value = z[at, :]
        for part in range(2):
            hi, lo = split(value[:, part * M : (part + 1) * M])
            both = dot(jnp.concatenate([hi, lo], axis=1), right)
            out[part, at, :] = both[:, :M] + both[:, M:]
        return carry

    lax.fori_loop(0, z.shape[0] // step, rows_of, 0, unroll=2)


def finish(grams, z, total_rows):
    return pl.pallas_call(
        partial(finish_kernel, total_rows),
        out_shape=jax.ShapeDtypeStruct((2, z.shape[0], M), F32),
        in_specs=[VMEM] * 2,
        out_specs=VMEM,
        scratch_shapes=[pltpu.VMEM((M, 2 * M), F32)],
        compiler_params=PARAMS,
        name="finish",
    )(grams, z)


def shifted(x, by):
    peers = lax.axis_size("blk")
    pairs = [(i, i + by) for i in range(peers) if 0 <= i + by < peers]
    return lax.ppermute(x, "blk", pairs)


def gathered(own):
    peers = lax.axis_size("src")
    chunks = [own]
    if peers & (peers - 1):
        for k in range(1, peers):
            chunks.append(lax.ppermute(own, "src", [(i, (i + k) % peers) for i in range(peers)]))
        return chunks
    far = peers // 2
    while far:
        pairs = [(i, i ^ far) for i in range(peers)]
        chunks = chunks + [lax.ppermute(chunk, "src", pairs) for chunk in chunks]
        far //= 2
    if len(chunks) == 4:
        chunks = [chunks[i] for i in (0, 2, 1, 3)]
    return chunks


def per_device(pupils, starts, counts, weights, start_block):
    regions = lax.axis_size("blk")
    peers = lax.axis_size("src")

    own = pack(pupils, starts, counts, weights, regions * RB)
    chunks = gathered(own)
    edge = 2 * BLOCK
    size = start_block.shape[1]
    x_left = shifted(start_block[:, size - edge :], 1)
    x_right = shifted(start_block[:, :edge], -1)

    band = build(own, None)
    band, x_left, x_right = lax.optimization_barrier((band, x_left, x_right))
    for chunk in chunks[1:-1]:
        band = build(chunk, band)
    left_band, right_band = build_edges(chunks[-1], band)
    left_band = shifted(left_band, 1)
    right_band = shifted(right_band, -1)
    band = build(chunks[-1], band)
    z, grams = apply_twice(band, left_band, right_band, start_block, x_left, x_right)
    grams = lax.all_gather(grams, "blk", axis=0)
    return finish(grams, z, 2.0 * size * regions)


def solution(mesh):
    placed = (
        P(("groups", "src", "blk"), None, None),
        P(("groups", "src", "blk")),
        P(("groups", "src", "blk")),
        P(("groups", "src", "blk")),
        P("groups", "blk", None),
    )
    return jax.shard_map(
        per_device, mesh=mesh, in_specs=placed, out_specs=P("groups", "blk", None), check_vma=False
    )
```

```python
from functools import partial

import jax
import jax.numpy as jnp
from jax import lax
from jax.experimental import pallas as pl
from jax.experimental.pallas import tpu as pltpu
from jax.sharding import PartitionSpec as P

BLOCK = 64
RB = 32
GROUP = 8
UNROLL = 8
OUTER = 64
M = 128
F32 = jnp.float32
BF16 = jnp.bfloat16
HIGHEST = lax.Precision.HIGHEST
VMEM = pl.BlockSpec(memory_space=pltpu.VMEM)
PARAMS = pltpu.CompilerParams(vmem_limit_bytes=40 * 1024 * 1024)


def split(x):
    hi = x.astype(BF16)
    return hi, (x - hi.astype(F32)).astype(BF16)


def dot(a, b):
    return jnp.dot(a, b, preferred_element_type=F32)


def dot_t(a, b):
    return lax.dot_general(a, b, (((0,), (0,)), ((), ())), preferred_element_type=F32)


def dot_f32(a, b):
    return jnp.dot(a, b, precision=HIGHEST, preferred_element_type=F32)


def pack_kernel(total_blocks, *refs):
    sent, out, held, sems = refs[:4], refs[4], refs[5:9], refs[9]
    copies = [pltpu.make_async_copy(sent[i], held[i], sems.at[i]) for i in range(4)]
    for copy in copies:
        copy.start()
    for copy in copies:
        copy.wait()
    pupils, starts, counts, weights = held
    tiles = starts.shape[0]
    lane = lax.broadcasted_iota(jnp.int32, (128, 2 * BLOCK), 1)
    start = starts[...]
    root = jnp.sqrt(weights[...])
    first_live = jnp.where(counts[...] > 0, root, 0.0)
    second_live = jnp.where((counts[...] > 1) & (start + 1 < total_blocks), root, 0.0)
    for t in range(tiles):
        first_column = jnp.broadcast_to(first_live[t : t + 1, :], (128, 128)).T
        second_column = jnp.broadcast_to(second_live[t : t + 1, :], (128, 128)).T
        first = pupils[pl.ds(256 * t, 128, stride=2), :] * first_column
        second = pupils[pl.ds(256 * t + 1, 128, stride=2), :] * second_column
        real = jnp.where(lane < BLOCK, first, pltpu.roll(second, BLOCK, 1))
        imag = jnp.where(lane < BLOCK, pltpu.roll(first, BLOCK, 1), second)
        out[128 * t : 128 * t + 128, :] = real
        out[128 * (tiles + t) : 128 * (tiles + t) + 128, :] = imag
    out[256 * tiles :, :] = jnp.zeros((8, 128), F32)
    out[256 * tiles : 256 * tiles + tiles, :] = lax.rem(start, RB).astype(F32)


def pack(pupils, starts, counts, weights, total_blocks):
    slots = pupils.shape[0]
    return pl.pallas_call(
        partial(pack_kernel, total_blocks),
        out_shape=jax.ShapeDtypeStruct((2 * slots + 8, 128), F32),
        in_specs=[pl.BlockSpec(memory_space=pl.ANY)] * 4,
        out_specs=VMEM,
        scratch_shapes=[
            pltpu.VMEM((2 * slots, 128), F32),
            pltpu.VMEM((slots // 128, 128), jnp.int32),
            pltpu.VMEM((slots // 128, 128), jnp.int32),
            pltpu.VMEM((slots // 128, 128), F32),
            pltpu.SemaphoreType.DMA((4,)),
        ],
        compiler_params=PARAMS,
        name="pack",
    )(
        *(
            pltpu.with_memory_space_constraint(x, pltpu.HBM)
            for x in (
                pupils.reshape(2 * slots, 128),
                starts.reshape(-1, 128),
                counts.reshape(-1, 128),
                weights.reshape(-1, 128),
            )
        )
    )


def factors(chunk):
    count = (chunk.shape[0] - 8) // 2
    real = chunk[:count, :]
    imag = chunk[count : 2 * count, :]
    right = jnp.concatenate(
        [
            jnp.concatenate([real, -imag], axis=1),
            jnp.concatenate([imag, real], axis=1),
        ],
        axis=0,
    )
    left = jnp.concatenate([real.T, imag.T], axis=1)
    places = [chunk[2 * count + t : 2 * count + t + 1, :] for t in range(count // 128)]
    place = jnp.broadcast_to(jnp.concatenate(places + places, axis=1), (16, 2 * count))
    return split(left), split(right), place


def at_block(part, place, b):
    mask = jnp.where(place == b, 1.0, 0.0).astype(BF16)[None]
    return (part.reshape(8, 16, -1) * mask).reshape(part.shape)


def build_kernel(add, last, chunk, *refs):
    refs = list(refs)
    before = refs.pop(0) if add else None
    lhs_lo, lhs_hi = refs.pop(), refs.pop()
    (left_hi, left_lo), (right_hi, right_lo), place = factors(chunk)

    def one_group(g, carry):
        for j in range(GROUP):
            b = (g * GROUP + j).astype(F32)
            lhs_hi[j * 128 : (j + 1) * 128, :] = at_block(left_hi, place, b)
            lhs_lo[j * 128 : (j + 1) * 128, :] = at_block(left_lo, place, b)
        at = pl.ds(pl.multiple_of(g * GROUP * 128, GROUP * 128), GROUP * 128)
        hi = lhs_hi[...]
        total = dot(hi, right_hi) + dot(hi, right_lo) + dot(lhs_lo[...], right_hi)
        if add:
            total = before[at, :] + total
        if last:
            refs[0][at, :], refs[1][at, :] = split(total)
        else:
            refs[0][at, :] = total
        return carry

    lax.fori_loop(0, RB // GROUP, one_group, 0)


def build(chunk, before, last=False):
    count = (chunk.shape[0] - 8) // 2
    add = before is not None
    shape = (RB * 128, 256)
    out = [jax.ShapeDtypeStruct(shape, BF16)] * 2 if last else [jax.ShapeDtypeStruct(shape, F32)]
    result = pl.pallas_call(
        partial(build_kernel, add, last),
        out_shape=out,
        in_specs=[VMEM] * (1 + add),
        out_specs=[VMEM] * len(out),
        scratch_shapes=[pltpu.VMEM((GROUP * 128, 2 * count), BF16)] * 2,
        input_output_aliases={1: 0} if add and not last else {},
        compiler_params=PARAMS,
        cost_estimate=pl.CostEstimate(
            flops=1 << 20, bytes_accessed=1 << 16, transcendentals=0
        ),
        name="band_terms",
    )(chunk, *([before] if add else []))
    return result if last else result[0]


def wide(parts):
    return jnp.concatenate([parts[0], parts[1]], axis=1)


def edge_kernel(chunk, before, x, after_out, before_out):
    (left_hi, left_lo), (right_hi, right_lo), place = factors(chunk)
    hi = jnp.concatenate([at_block(left_hi, place, float(b)) for b in (0, RB - 2, RB - 1)], axis=0)
    lo = jnp.concatenate([at_block(left_lo, place, float(b)) for b in (0, RB - 2, RB - 1)], axis=0)
    total = dot(hi, right_hi) + dot(hi, right_lo) + dot(lo, right_hi)
    after_out[: 3 * BLOCK, :] = before[RB * 128 - 192 :, :] + total[192:]
    after_out[3 * BLOCK :, :] = wide(x[:, x.shape[1] - 2 * BLOCK :, :])
    before_out[:BLOCK, :] = before[:BLOCK, :] + total[:BLOCK]
    before_out[BLOCK:, :] = wide(x[:, : 2 * BLOCK, :])


def build_edges(chunk, before, x):
    return pl.pallas_call(
        edge_kernel,
        out_shape=(
            jax.ShapeDtypeStruct((5 * BLOCK, 256), F32),
            jax.ShapeDtypeStruct((3 * BLOCK, 256), F32),
        ),
        in_specs=[VMEM] * 3,
        out_specs=(VMEM, VMEM),
        compiler_params=PARAMS,
        name="edge_terms",
    )(chunk, before, x)


def real_form(rows):
    return jnp.concatenate(
        [rows, jnp.concatenate([-rows[:, M:], rows[:, :M]], axis=1)], axis=0
    )


def times(g_hi, g_lo, hi, lo):
    hi, lo = real_form(hi), real_form(lo)
    return dot(g_hi, hi) + dot(g_hi, lo) + dot(g_lo, hi)


def gram_of(hi, lo):
    a = dot_t(hi, hi)
    b = dot_t(hi, lo)
    a = a[:M, :M] + a[M:, M:]
    b = b[:M, :M] + b[M:, M:]
    return a + b + b.T


def prepare_kernel(x, hi_out, lo_out):
    for i in range(0, x.shape[1], 256):
        hi_out[i : i + 256, :], lo_out[i : i + 256, :] = split(wide(x[:, i : i + 256, :]))


def prepare(x):
    shape = jax.ShapeDtypeStruct((x.shape[1], 256), BF16)
    return pl.pallas_call(
        prepare_kernel,
        out_shape=(shape, shape),
        in_specs=[VMEM],
        out_specs=(VMEM, VMEM),
        compiler_params=PARAMS,
        cost_estimate=pl.CostEstimate(flops=1 << 20, bytes_accessed=4 << 20, transcendentals=0),
        name="prepare",
    )(x)


def apply_kernel(g_hi, g_lo, left, right, x_hi, x_lo, z_hi, z_lo, grams, p_hi, p_lo):
    rows = RB * BLOCK
    left_hi, left_lo = split(left[: 3 * BLOCK, :])
    right_hi, right_lo = split(right[:BLOCK, :])

    def put(e, block):
        at = pl.ds(pl.multiple_of(e * BLOCK, BLOCK), BLOCK)
        p_hi[at, :], p_lo[at, :] = split(block)

    def join(a, b):
        return jnp.concatenate([a, b], axis=0)

    head = split(left[3 * BLOCK :, :])
    tail = split(right[BLOCK:, :])
    spill = times(left_hi[:BLOCK], left_lo[:BLOCK], head[0], head[1])
    both = times(
        left_hi[BLOCK:],
        left_lo[BLOCK:],
        join(head[0][BLOCK:], x_hi[:BLOCK, :]),
        join(head[1][BLOCK:], x_lo[:BLOCK, :]),
    )
    first_block = spill + both[:BLOCK]
    put(0, first_block)

    def first(b, carry):
        spill, top = carry
        at = pl.ds(pl.multiple_of(b * 128, 128), 128)
        win = pl.ds(pl.multiple_of(b * BLOCK, BLOCK), 128)
        both = times(g_hi[at, :], g_lo[at, :], x_hi[win, :], x_lo[win, :])
        block = both[:BLOCK] + spill
        put(b + 1, block)
        return both[BLOCK:], jnp.maximum(top, jnp.abs(block))

    spill, top = lax.fori_loop(
        0, RB - 1, first, (both[BLOCK:], jnp.abs(first_block)), unroll=UNROLL
    )
    both = times(
        g_hi[(RB - 1) * 128 :, :],
        g_lo[(RB - 1) * 128 :, :],
        join(x_hi[rows - BLOCK :, :], tail[0][:BLOCK]),
        join(x_lo[rows - BLOCK :, :], tail[1][:BLOCK]),
    )
    block = both[:BLOCK] + spill
    put(RB, block)
    last_block = both[BLOCK:] + times(right_hi, right_lo, tail[0], tail[1])
    put(RB + 1, last_block)
    top = jnp.maximum(jnp.maximum(top, jnp.abs(block)), jnp.abs(last_block))
    top = jnp.max(top, axis=0, keepdims=True)
    top = jnp.maximum(top[:, :M], top[:, M:])
    scale = jnp.where(top > 0, 1.0 / jnp.where(top > 0, top, 1.0), 0.0)
    scale = jnp.concatenate([scale, scale], axis=1)

    inner = pl.ds(BLOCK, rows)
    gram_1 = gram_of(p_hi[inner, :], p_lo[inner, :])

    def second(b, spill):
        at = pl.ds(pl.multiple_of(b * 128, 128), 128)
        win = pl.ds(pl.multiple_of((b + 1) * BLOCK, BLOCK), 128)
        both = times(g_hi[at, :], g_lo[at, :], p_hi[win, :], p_lo[win, :])
        out = pl.ds(pl.multiple_of(b * BLOCK, BLOCK), BLOCK)
        z_hi[out, :], z_lo[out, :] = split((both[:BLOCK] + spill) * scale)
        return both[BLOCK:]

    spill = times(left_hi[2 * BLOCK :], left_lo[2 * BLOCK :], p_hi[:128, :], p_lo[:128, :])
    lax.fori_loop(0, RB, second, spill, unroll=UNROLL)
    gram_2 = gram_of(z_hi[...], z_lo[...])
    row = lax.broadcasted_iota(jnp.int32, (M, M), 0)
    col = lax.broadcasted_iota(jnp.int32, (M, M), 1)
    grams[:M, :] = jnp.where(row >= col, gram_1, gram_2)
    diagonal = jnp.sum(jnp.where(row == col, gram_2, 0.0), axis=0, keepdims=True)
    grams[M:, :] = jnp.concatenate([diagonal, top, jnp.zeros((6, M), F32)], axis=0)


def apply_twice(g_hi, g_lo, left, right, x_hi, x_lo):
    rows = RB * BLOCK
    return pl.pallas_call(
        apply_kernel,
        out_shape=(
            jax.ShapeDtypeStruct((rows, 256), BF16),
            jax.ShapeDtypeStruct((rows, 256), BF16),
            jax.ShapeDtypeStruct((M + 8, M), F32),
        ),
        in_specs=[VMEM] * 6,
        out_specs=(VMEM, VMEM, VMEM),
        scratch_shapes=[pltpu.VMEM((rows + 2 * BLOCK, 256), BF16)] * 2,
        compiler_params=PARAMS,
        cost_estimate=pl.CostEstimate(
            flops=12 * RB * 128 * 256 * 256, bytes_accessed=12 << 20, transcendentals=0
        ),
        name="apply_twice",
    )(g_hi, g_lo, left, right, x_hi, x_lo)


def inverse_factor(a, work):
    row = lax.broadcasted_iota(jnp.int32, (M, M), 0)
    col = lax.broadcasted_iota(jnp.int32, (M, M), 1)
    work[:, :M] = a
    work[:, M:] = jnp.where(row == col, 1.0, 0.0)
    sub = lax.broadcasted_iota(jnp.int32, (8, M), 0)
    groups = OUTER // 8

    def line(x, j):
        return x[j : j + 1, :]

    def wide(x, j):
        return jnp.broadcast_to(line(x, j), (8, M))

    for top in range(0, M, OUTER):
        left = [work[top + 8 * g : top + 8 * g + 8, :M] for g in range(groups)]
        right = [work[top + 8 * g : top + 8 * g + 8, M:] for g in range(groups)]
        for q in range(groups):
            at = top + 8 * q
            cols = {
                g: [jnp.broadcast_to(left[g][:, at + k : at + k + 1], (8, M)) for k in range(8)]
                for g in range(q, groups)
            }
            scales = jnp.zeros((8, M), F32)
            for j in range(0, 8, 2):
                a0, a1, a2 = wide(cols[q][j], j), wide(cols[q][j], j + 1), wide(cols[q][j + 1], j + 1)
                det = a0 * a2 - a1 * a1
                inverse = pltpu.reciprocal(det, approx=False)
                root = lax.rsqrt(a0)
                ratio = a1 * (root * root)
                scales = jnp.where(sub == j, root, scales)
                scales = jnp.where(sub == j + 1, lax.rsqrt(det) * (a0 * root), scales)
                row_0 = [line(cols[q][k], j) for k in range(8)]
                row_1 = [line(cols[q][k], j + 1) for k in range(8)]
                left_0, left_1 = line(left[q], j), line(left[q], j + 1)
                right_0, right_1 = line(right[q], j), line(right[q], j + 1)
                for g in range(q, groups):
                    c0, c1 = cols[g][j], cols[g][j + 1]
                    y0 = a2 * c0 - a1 * c1
                    y1 = a0 * c1 - a1 * c0
                    if g == q:
                        y0 = jnp.where(sub > j + 1, y0, 0.0)
                        y1 = jnp.where(sub > j + 1, y1, 0.0)
                    for k in range(j + 2, 8):
                        cols[g][k] = cols[g][k] - (y0 * row_0[k] + y1 * row_1[k]) * inverse
                    x0, x1 = y0 * inverse, y1 * inverse
                    if g == q:
                        x0 = jnp.where(sub == j + 1, ratio, x0)
                    left[g] = left[g] - (x0 * left_0 + x1 * left_1)
                    right[g] = right[g] - (x0 * right_0 + x1 * right_1)
            left[q] = left[q] * scales
            right[q] = right[q] * scales
        for g in range(groups):
            work[top + 8 * g : top + 8 * g + 8, :M] = left[g]
            work[top + 8 * g : top + 8 * g + 8, M:] = right[g]
        if top + OUTER < M:
            panel = work[top : top + OUTER, :]
            update = lax.dot_general(
                panel[:, :M], panel, (((0,), (0,)), ((), ())),
                precision=HIGHEST, preferred_element_type=F32,
            )
            work[top + OUTER :, :] = work[top + OUTER :, :] - update[top + OUTER :, :]
    return work[:, M:]


def finish_kernel(total_rows, grams, own, z_hi, z_lo, out, work):
    peers = grams.shape[0]
    row = lax.broadcasted_iota(jnp.int32, (M, M), 0)
    col = lax.broadcasted_iota(jnp.int32, (M, M), 1)
    eye = jnp.where(row == col, 1.0, 0.0)

    def as_column(v):
        return jnp.sum(eye * v, axis=1, keepdims=True)

    def row_of(x):
        return jnp.sum(eye * x, axis=0, keepdims=True)

    total = grams[0, :M, :]
    for r in range(1, peers):
        total = total + grams[r, :M, :]
    gram = jnp.where(row >= col, total, total.T)
    norm = lax.rsqrt(row_of(gram))
    inverse = inverse_factor(gram * norm * as_column(norm), work)
    total = jnp.zeros((M, M), F32)
    for r in range(peers):
        size = norm * grams[r, M + 1 : M + 2, :]
        second = jnp.where(row == col, grams[r, M : M + 1, :], grams[r, :M, :])
        total = total + second * size * as_column(size)
    gram = jnp.where(row <= col, total, total.T)
    gram = dot_f32(dot_f32(inverse, gram), inverse.T)
    scale = lax.rsqrt(row_of(gram))
    second = inverse_factor(gram * scale * as_column(scale), work) * scale
    inverse = dot_f32(second, inverse)
    change = (inverse * (norm * own[M + 1 : M + 2, :] * (total_rows**0.5))).T
    c_hi, c_lo = split(change)
    right = jnp.concatenate(
        [
            jnp.concatenate([c_hi, c_lo], axis=1),
            jnp.concatenate([c_hi, jnp.zeros_like(c_lo)], axis=1),
        ],
        axis=0,
    )
    step = 256

    def rows_of(i, carry):
        at = pl.ds(pl.multiple_of(i * step, step), step)
        hi, lo = z_hi[at, :], z_lo[at, :]
        for part in range(2):
            cols = slice(part * M, part * M + M)
            both = dot(jnp.concatenate([hi[:, cols], lo[:, cols]], axis=1), right)
            out[part, at, :] = both[:, :M] + both[:, M:]
        return carry

    lax.fori_loop(0, z_hi.shape[0] // step, rows_of, 0, unroll=True)


def finish(grams, own, z_hi, z_lo, total_rows):
    return pl.pallas_call(
        partial(finish_kernel, total_rows),
        out_shape=jax.ShapeDtypeStruct((2, z_hi.shape[0], M), F32),
        in_specs=[VMEM] * 4,
        out_specs=VMEM,
        scratch_shapes=[pltpu.VMEM((M, 2 * M), F32)],
        compiler_params=PARAMS,
        name="finish",
    )(grams, own, z_hi, z_lo)


def shifted(x, by):
    peers = lax.axis_size("blk")
    pairs = [(i, i + by) for i in range(peers) if 0 <= i + by < peers]
    return lax.ppermute(x, "blk", pairs)


def swapped(x, far):
    peers = lax.axis_size("src")
    return lax.ppermute(x, "src", [(i, i ^ far) for i in range(peers)])


def gathered(own, ready):
    peers = lax.axis_size("src")
    if peers & (peers - 1):
        chunks = [
            lax.ppermute(own, "src", [(i, (i + k) % peers) for i in range(peers)])
            for k in range(1, peers)
        ]
        return chunks, ready
    far = peers // 2
    chunks = []
    while far:
        if chunks:
            chunks, ready = lax.optimization_barrier((chunks, ready))
        chunks = chunks + [swapped(c, far) for c in [own] + chunks]
        far //= 2
    return chunks, ready


def per_device(pupils, starts, counts, weights, start_block):
    regions = lax.axis_size("blk")
    size = start_block.shape[1]

    own = pack(pupils, starts, counts, weights, regions * RB)
    ready = (build(own, None), *prepare(start_block))
    chunks, ready = gathered(own, ready)
    band, x_hi, x_lo = ready
    for chunk in chunks[:-1]:
        band = build(chunk, band)
    after, before = build_edges(chunks[-1], band, start_block)
    left, right = shifted(after, 1), shifted(before, -1)
    g_hi, g_lo = build(chunks[-1], band, last=True)
    z_hi, z_lo, own_grams = apply_twice(g_hi, g_lo, left, right, x_hi, x_lo)
    grams = lax.all_gather(own_grams, "blk", axis=0)
    return finish(grams, own_grams, z_hi, z_lo, 2.0 * size * regions)


def solution(mesh):
    placed = (
        P(("groups", "src", "blk"), None, None),
        P(("groups", "src", "blk")),
        P(("groups", "src", "blk")),
        P(("groups", "src", "blk")),
        P("groups", "blk", None),
    )
    return jax.shard_map(
        per_device, mesh=mesh, in_specs=placed, out_specs=P("groups", "blk", None), check_vma=False
    )
```

```python
from functools import partial

import jax
import jax.numpy as jnp
from jax import lax
from jax.experimental import pallas as pl
from jax.experimental.pallas import tpu as pltpu
from jax.sharding import PartitionSpec as P

BLOCK = 64
RB = 32
GROUP = 8
UNROLL = 8
OUTER = 64
M = 128
F32 = jnp.float32
BF16 = jnp.bfloat16
HIGHEST = lax.Precision.HIGHEST
VMEM = pl.BlockSpec(memory_space=pltpu.VMEM)
PARAMS = pltpu.CompilerParams(vmem_limit_bytes=40 * 1024 * 1024)


def split(x):
    hi = x.astype(BF16)
    return hi, (x - hi.astype(F32)).astype(BF16)


def dot(a, b):
    return jnp.dot(a, b, preferred_element_type=F32)


def dot_t(a, b):
    return lax.dot_general(a, b, (((0,), (0,)), ((), ())), preferred_element_type=F32)


def dot_f32(a, b):
    return jnp.dot(a, b, precision=HIGHEST, preferred_element_type=F32)


def pack_kernel(total_blocks, *refs):
    sent, out, held, sems = refs[:4], refs[4], refs[5:9], refs[9]
    copies = [pltpu.make_async_copy(sent[i], held[i], sems.at[i]) for i in range(4)]
    for copy in copies:
        copy.start()
    for copy in copies:
        copy.wait()
    pupils, starts, counts, weights = held
    tiles = starts.shape[0]
    lane = lax.broadcasted_iota(jnp.int32, (128, 2 * BLOCK), 1)
    start = starts[...]
    root = jnp.sqrt(weights[...])
    first_live = jnp.where(counts[...] > 0, root, 0.0)
    second_live = jnp.where((counts[...] > 1) & (start + 1 < total_blocks), root, 0.0)
    for t in range(tiles):
        first_column = jnp.broadcast_to(first_live[t : t + 1, :], (128, 128)).T
        second_column = jnp.broadcast_to(second_live[t : t + 1, :], (128, 128)).T
        first = pupils[pl.ds(256 * t, 128, stride=2), :] * first_column
        second = pupils[pl.ds(256 * t + 1, 128, stride=2), :] * second_column
        real = jnp.where(lane < BLOCK, first, pltpu.roll(second, BLOCK, 1))
        imag = jnp.where(lane < BLOCK, pltpu.roll(first, BLOCK, 1), second)
        out[128 * t : 128 * t + 128, :] = real
        out[128 * (tiles + t) : 128 * (tiles + t) + 128, :] = imag
    out[256 * tiles :, :] = jnp.zeros((8, 128), F32)
    out[256 * tiles : 256 * tiles + tiles, :] = lax.rem(start, RB).astype(F32)


def pack(pupils, starts, counts, weights, total_blocks):
    slots = pupils.shape[0]
    return pl.pallas_call(
        partial(pack_kernel, total_blocks),
        out_shape=jax.ShapeDtypeStruct((2 * slots + 8, 128), F32),
        in_specs=[pl.BlockSpec(memory_space=pl.ANY)] * 4,
        out_specs=VMEM,
        scratch_shapes=[
            pltpu.VMEM((2 * slots, 128), F32),
            pltpu.VMEM((slots // 128, 128), jnp.int32),
            pltpu.VMEM((slots // 128, 128), jnp.int32),
            pltpu.VMEM((slots // 128, 128), F32),
            pltpu.SemaphoreType.DMA((4,)),
        ],
        compiler_params=PARAMS,
        name="pack",
    )(
        *(
            pltpu.with_memory_space_constraint(x, pltpu.HBM)
            for x in (
                pupils.reshape(2 * slots, 128),
                starts.reshape(-1, 128),
                counts.reshape(-1, 128),
                weights.reshape(-1, 128),
            )
        )
    )


def factors(chunk):
    count = (chunk.shape[0] - 8) // 2
    real = chunk[:count, :]
    imag = chunk[count : 2 * count, :]
    left = jnp.concatenate([real.T, imag.T], axis=1).astype(BF16)
    right = []
    for scale, real, imag in zip((0.5, 1.0), split(real), split(imag)):
        right.append(
            jnp.concatenate(
                [
                    jnp.concatenate([real, -imag], axis=1),
                    jnp.concatenate([imag, real], axis=1),
                ],
                axis=0,
            )
            * jnp.asarray(scale, BF16)
        )
    places = [chunk[2 * count + t : 2 * count + t + 1, :] for t in range(count // 128)]
    place = jnp.broadcast_to(jnp.concatenate(places + places, axis=1), (16, 2 * count))
    return left, right[0], right[1], place


def at_block(part, place, b):
    mask = jnp.where(place == b, 1.0, 0.0).astype(BF16)[None]
    return (part.reshape(8, 16, -1) * mask).reshape(part.shape)


def hermitian(q):
    real, imag = q[:, :128], q[:, 128:]
    return jnp.concatenate([real + real.T, imag - imag.T], axis=1)


def build_kernel(add, last, chunk, *refs):
    refs = list(refs)
    before = refs.pop(0) if add else None
    lhs = refs.pop()
    left, right_hi, right_lo, place = factors(chunk)

    def one_group(g, carry):
        for j in range(GROUP):
            b = (g * GROUP + j).astype(F32)
            lhs[j * 128 : (j + 1) * 128, :] = at_block(left, place, b)
        at = pl.ds(pl.multiple_of(g * GROUP * 128, GROUP * 128), GROUP * 128)
        hi = lhs[...]
        total = dot(hi, right_hi) + dot(hi, right_lo)
        if add:
            total = before[at, :] + total
        if last:
            for j in range(GROUP):
                one = pl.ds(pl.multiple_of((g * GROUP + j) * 128, 128), 128)
                refs[0][one, :], refs[1][one, :] = split(
                    hermitian(total[j * 128 : (j + 1) * 128, :])
                )
        else:
            refs[0][at, :] = total
        return carry

    lax.fori_loop(0, RB // GROUP, one_group, 0)


def build(chunk, before, last=False):
    count = (chunk.shape[0] - 8) // 2
    add = before is not None
    shape = (RB * 128, 256)
    out = [jax.ShapeDtypeStruct(shape, BF16)] * 2 if last else [jax.ShapeDtypeStruct(shape, F32)]
    result = pl.pallas_call(
        partial(build_kernel, add, last),
        out_shape=out,
        in_specs=[VMEM] * (1 + add),
        out_specs=[VMEM] * len(out),
        scratch_shapes=[pltpu.VMEM((GROUP * 128, 2 * count), BF16)],
        input_output_aliases={1: 0} if add and not last else {},
        compiler_params=PARAMS,
        cost_estimate=pl.CostEstimate(
            flops=1 << 20, bytes_accessed=1 << 16, transcendentals=0
        ),
        name="band_terms",
    )(chunk, *([before] if add else []))
    return result if last else result[0]


def wide(parts):
    return jnp.concatenate([parts[0], parts[1]], axis=1)


def edge_kernel(chunk, before, x, after_out, before_out):
    left, right_hi, right_lo, place = factors(chunk)
    blocks = (0, RB - 2, RB - 1)
    left = jnp.concatenate([at_block(left, place, float(b)) for b in blocks], axis=0)
    total = dot(left, right_hi) + dot(left, right_lo)
    first, second, third = [
        hermitian(before[b * 128 : (b + 1) * 128, :] + total[i * 128 : (i + 1) * 128, :])
        for i, b in enumerate(blocks)
    ]
    after_out[:BLOCK, :] = second[BLOCK:, :]
    after_out[BLOCK : 3 * BLOCK, :] = third
    after_out[3 * BLOCK :, :] = wide(x[:, x.shape[1] - 2 * BLOCK :, :])
    before_out[:BLOCK, :] = first[:BLOCK, :]
    before_out[BLOCK:, :] = wide(x[:, : 2 * BLOCK, :])


def build_edges(chunk, before, x):
    return pl.pallas_call(
        edge_kernel,
        out_shape=(
            jax.ShapeDtypeStruct((5 * BLOCK, 256), F32),
            jax.ShapeDtypeStruct((3 * BLOCK, 256), F32),
        ),
        in_specs=[VMEM] * 3,
        out_specs=(VMEM, VMEM),
        compiler_params=PARAMS,
        name="edge_terms",
    )(chunk, before, x)


def real_form(rows):
    return jnp.concatenate(
        [rows, jnp.concatenate([-rows[:, M:], rows[:, :M]], axis=1)], axis=0
    )


def times(g_hi, g_lo, hi, lo):
    hi, lo = real_form(hi), real_form(lo)
    return dot(g_hi, hi) + dot(g_hi, lo) + dot(g_lo, hi)


def gram_of(hi, lo):
    a = dot_t(hi, hi)
    b = dot_t(hi, lo)
    a = a[:M, :M] + a[M:, M:]
    b = b[:M, :M] + b[M:, M:]
    return a + b + b.T


def prepare_kernel(x, hi_out, lo_out):
    for i in range(0, x.shape[1], 256):
        hi_out[i : i + 256, :], lo_out[i : i + 256, :] = split(wide(x[:, i : i + 256, :]))


def prepare(x):
    shape = jax.ShapeDtypeStruct((x.shape[1], 256), BF16)
    return pl.pallas_call(
        prepare_kernel,
        out_shape=(shape, shape),
        in_specs=[VMEM],
        out_specs=(VMEM, VMEM),
        compiler_params=PARAMS,
        cost_estimate=pl.CostEstimate(flops=1 << 20, bytes_accessed=4 << 20, transcendentals=0),
        name="prepare",
    )(x)


def apply_kernel(g_hi, g_lo, left, right, x_hi, x_lo, z_hi, z_lo, grams, p_hi, p_lo):
    rows = RB * BLOCK
    left_hi, left_lo = split(left[: 3 * BLOCK, :])
    right_hi, right_lo = split(right[:BLOCK, :])

    def put(e, block):
        at = pl.ds(pl.multiple_of(e * BLOCK, BLOCK), BLOCK)
        p_hi[at, :], p_lo[at, :] = split(block)

    def join(a, b):
        return jnp.concatenate([a, b], axis=0)

    head = split(left[3 * BLOCK :, :])
    tail = split(right[BLOCK:, :])
    spill = times(left_hi[:BLOCK], left_lo[:BLOCK], head[0], head[1])
    both = times(
        left_hi[BLOCK:],
        left_lo[BLOCK:],
        join(head[0][BLOCK:], x_hi[:BLOCK, :]),
        join(head[1][BLOCK:], x_lo[:BLOCK, :]),
    )
    first_block = spill + both[:BLOCK]
    put(0, first_block)

    def first(b, carry):
        spill, top = carry
        at = pl.ds(pl.multiple_of(b * 128, 128), 128)
        win = pl.ds(pl.multiple_of(b * BLOCK, BLOCK), 128)
        both = times(g_hi[at, :], g_lo[at, :], x_hi[win, :], x_lo[win, :])
        block = both[:BLOCK] + spill
        put(b + 1, block)
        return both[BLOCK:], jnp.maximum(top, jnp.abs(block))

    spill, top = lax.fori_loop(
        0, RB - 1, first, (both[BLOCK:], jnp.abs(first_block)), unroll=UNROLL
    )
    both = times(
        g_hi[(RB - 1) * 128 :, :],
        g_lo[(RB - 1) * 128 :, :],
        join(x_hi[rows - BLOCK :, :], tail[0][:BLOCK]),
        join(x_lo[rows - BLOCK :, :], tail[1][:BLOCK]),
    )
    block = both[:BLOCK] + spill
    put(RB, block)
    last_block = both[BLOCK:] + times(right_hi, right_lo, tail[0], tail[1])
    put(RB + 1, last_block)
    top = jnp.maximum(jnp.maximum(top, jnp.abs(block)), jnp.abs(last_block))
    top = jnp.max(top, axis=0, keepdims=True)
    top = jnp.maximum(top[:, :M], top[:, M:])
    scale = jnp.where(top > 0, 1.0 / jnp.where(top > 0, top, 1.0), 0.0)
    scale = jnp.concatenate([scale, scale], axis=1)

    inner = pl.ds(BLOCK, rows)
    gram_1 = gram_of(p_hi[inner, :], p_lo[inner, :])

    def second(b, spill):
        at = pl.ds(pl.multiple_of(b * 128, 128), 128)
        win = pl.ds(pl.multiple_of((b + 1) * BLOCK, BLOCK), 128)
        both = times(g_hi[at, :], g_lo[at, :], p_hi[win, :], p_lo[win, :])
        out = pl.ds(pl.multiple_of(b * BLOCK, BLOCK), BLOCK)
        z_hi[out, :], z_lo[out, :] = split((both[:BLOCK] + spill) * scale)
        return both[BLOCK:]

    spill = times(left_hi[2 * BLOCK :], left_lo[2 * BLOCK :], p_hi[:128, :], p_lo[:128, :])
    lax.fori_loop(0, RB, second, spill, unroll=UNROLL)
    gram_2 = gram_of(z_hi[...], z_lo[...])
    row = lax.broadcasted_iota(jnp.int32, (M, M), 0)
    col = lax.broadcasted_iota(jnp.int32, (M, M), 1)
    grams[:M, :] = jnp.where(row >= col, gram_1, gram_2)
    diagonal = jnp.sum(jnp.where(row == col, gram_2, 0.0), axis=0, keepdims=True)
    grams[M:, :] = jnp.concatenate([diagonal, top, jnp.zeros((6, M), F32)], axis=0)


def apply_twice(g_hi, g_lo, left, right, x_hi, x_lo):
    rows = RB * BLOCK
    return pl.pallas_call(
        apply_kernel,
        out_shape=(
            jax.ShapeDtypeStruct((rows, 256), BF16),
            jax.ShapeDtypeStruct((rows, 256), BF16),
            jax.ShapeDtypeStruct((M + 8, M), F32),
        ),
        in_specs=[VMEM] * 6,
        out_specs=(VMEM, VMEM, VMEM),
        scratch_shapes=[pltpu.VMEM((rows + 2 * BLOCK, 256), BF16)] * 2,
        compiler_params=PARAMS,
        cost_estimate=pl.CostEstimate(
            flops=12 * RB * 128 * 256 * 256, bytes_accessed=12 << 20, transcendentals=0
        ),
        name="apply_twice",
    )(g_hi, g_lo, left, right, x_hi, x_lo)


def inverse_factor(a, work):
    row = lax.broadcasted_iota(jnp.int32, (M, M), 0)
    col = lax.broadcasted_iota(jnp.int32, (M, M), 1)
    work[:, :M] = a
    work[:, M:] = jnp.where(row == col, 1.0, 0.0)
    sub = lax.broadcasted_iota(jnp.int32, (8, M), 0)
    groups = OUTER // 8

    def line(x, j):
        return x[j : j + 1, :]

    def wide(x, j):
        return jnp.broadcast_to(line(x, j), (8, M))

    for top in range(0, M, OUTER):
        left = [work[top + 8 * g : top + 8 * g + 8, :M] for g in range(groups)]
        right = [work[top + 8 * g : top + 8 * g + 8, M:] for g in range(groups)]
        for q in range(groups):
            at = top + 8 * q
            cols = {
                g: [jnp.broadcast_to(left[g][:, at + k : at + k + 1], (8, M)) for k in range(8)]
                for g in range(q, groups)
            }
            scales = jnp.zeros((8, M), F32)
            for j in range(0, 8, 2):
                a0, a1, a2 = wide(cols[q][j], j), wide(cols[q][j], j + 1), wide(cols[q][j + 1], j + 1)
                det = a0 * a2 - a1 * a1
                inverse = pltpu.reciprocal(det, approx=False)
                root = lax.rsqrt(a0)
                ratio = a1 * (root * root)
                scales = jnp.where(sub == j, root, scales)
                scales = jnp.where(sub == j + 1, lax.rsqrt(det) * (a0 * root), scales)
                row_0 = [line(cols[q][k], j) for k in range(8)]
                row_1 = [line(cols[q][k], j + 1) for k in range(8)]
                left_0, left_1 = line(left[q], j), line(left[q], j + 1)
                right_0, right_1 = line(right[q], j), line(right[q], j + 1)
                for g in range(q, groups):
                    c0, c1 = cols[g][j], cols[g][j + 1]
                    y0 = a2 * c0 - a1 * c1
                    y1 = a0 * c1 - a1 * c0
                    if g == q:
                        y0 = jnp.where(sub > j + 1, y0, 0.0)
                        y1 = jnp.where(sub > j + 1, y1, 0.0)
                    for k in range(j + 2, 8):
                        cols[g][k] = cols[g][k] - (y0 * row_0[k] + y1 * row_1[k]) * inverse
                    x0, x1 = y0 * inverse, y1 * inverse
                    if g == q:
                        x0 = jnp.where(sub == j + 1, ratio, x0)
                    left[g] = left[g] - (x0 * left_0 + x1 * left_1)
                    right[g] = right[g] - (x0 * right_0 + x1 * right_1)
            left[q] = left[q] * scales
            right[q] = right[q] * scales
        for g in range(groups):
            work[top + 8 * g : top + 8 * g + 8, :M] = left[g]
            work[top + 8 * g : top + 8 * g + 8, M:] = right[g]
        if top + OUTER < M:
            panel = work[top : top + OUTER, :]
            update = lax.dot_general(
                panel[:, :M], panel, (((0,), (0,)), ((), ())),
                precision=HIGHEST, preferred_element_type=F32,
            )
            work[top + OUTER :, :] = work[top + OUTER :, :] - update[top + OUTER :, :]
    return work[:, M:]


def finish_kernel(total_rows, grams, own, z_hi, z_lo, out, work):
    peers = grams.shape[0]
    row = lax.broadcasted_iota(jnp.int32, (M, M), 0)
    col = lax.broadcasted_iota(jnp.int32, (M, M), 1)
    eye = jnp.where(row == col, 1.0, 0.0)

    def as_column(v):
        return jnp.sum(eye * v, axis=1, keepdims=True)

    def row_of(x):
        return jnp.sum(eye * x, axis=0, keepdims=True)

    total = grams[0, :M, :]
    for r in range(1, peers):
        total = total + grams[r, :M, :]
    gram = jnp.where(row >= col, total, total.T)
    norm = lax.rsqrt(row_of(gram))
    inverse = inverse_factor(gram * norm * as_column(norm), work)
    total = jnp.zeros((M, M), F32)
    for r in range(peers):
        size = norm * grams[r, M + 1 : M + 2, :]
        second = jnp.where(row == col, grams[r, M : M + 1, :], grams[r, :M, :])
        total = total + second * size * as_column(size)
    gram = jnp.where(row <= col, total, total.T)
    gram = dot_f32(dot_f32(inverse, gram), inverse.T)
    scale = lax.rsqrt(row_of(gram))
    second = inverse_factor(gram * scale * as_column(scale), work) * scale
    inverse = dot_f32(second, inverse)
    change = (inverse * (norm * own[M + 1 : M + 2, :] * (total_rows**0.5))).T
    c_hi, c_lo = split(change)
    right = jnp.concatenate(
        [
            jnp.concatenate([c_hi, c_lo], axis=1),
            jnp.concatenate([c_hi, jnp.zeros_like(c_lo)], axis=1),
        ],
        axis=0,
    )
    step = 256

    def rows_of(i, carry):
        at = pl.ds(pl.multiple_of(i * step, step), step)
        hi, lo = z_hi[at, :], z_lo[at, :]
        for part in range(2):
            cols = slice(part * M, part * M + M)
            both = dot(jnp.concatenate([hi[:, cols], lo[:, cols]], axis=1), right)
            out[part, at, :] = both[:, :M] + both[:, M:]
        return carry

    lax.fori_loop(0, z_hi.shape[0] // step, rows_of, 0, unroll=True)


def finish(grams, own, z_hi, z_lo, total_rows):
    return pl.pallas_call(
        partial(finish_kernel, total_rows),
        out_shape=jax.ShapeDtypeStruct((2, z_hi.shape[0], M), F32),
        in_specs=[VMEM] * 4,
        out_specs=VMEM,
        scratch_shapes=[pltpu.VMEM((M, 2 * M), F32)],
        compiler_params=PARAMS,
        name="finish",
    )(grams, own, z_hi, z_lo)


def shifted(x, by):
    peers = lax.axis_size("blk")
    pairs = [(i, i + by) for i in range(peers) if 0 <= i + by < peers]
    return lax.ppermute(x, "blk", pairs)


def swapped(x, far):
    peers = lax.axis_size("src")
    return lax.ppermute(x, "src", [(i, i ^ far) for i in range(peers)])


def gathered(own, ready):
    peers = lax.axis_size("src")
    if peers & (peers - 1):
        chunks = [
            lax.ppermute(own, "src", [(i, (i + k) % peers) for i in range(peers)])
            for k in range(1, peers)
        ]
        return chunks, ready
    far = peers // 2
    chunks = []
    while far:
        if chunks:
            chunks, ready = lax.optimization_barrier((chunks, ready))
        chunks = chunks + [swapped(c, far) for c in [own] + chunks]
        far //= 2
    return chunks, ready


def per_device(pupils, starts, counts, weights, start_block):
    regions = lax.axis_size("blk")
    size = start_block.shape[1]

    own = pack(pupils, starts, counts, weights, regions * RB)
    ready = (build(own, None), *prepare(start_block))
    chunks, ready = gathered(own, ready)
    band, x_hi, x_lo = ready
    for chunk in chunks[:-1]:
        band = build(chunk, band)
    after, before = build_edges(chunks[-1], band, start_block)
    left, right = shifted(after, 1), shifted(before, -1)
    g_hi, g_lo = build(chunks[-1], band, last=True)
    z_hi, z_lo, own_grams = apply_twice(g_hi, g_lo, left, right, x_hi, x_lo)
    grams = lax.all_gather(own_grams, "blk", axis=0)
    return finish(grams, own_grams, z_hi, z_lo, 2.0 * size * regions)


def solution(mesh):
    placed = (
        P(("groups", "src", "blk"), None, None),
        P(("groups", "src", "blk")),
        P(("groups", "src", "blk")),
        P(("groups", "src", "blk")),
        P("groups", "blk", None),
    )
    return jax.shard_map(
        per_device, mesh=mesh, in_specs=placed, out_specs=P("groups", "blk", None), check_vma=False
    )
```

```python
from functools import partial

import jax
import jax.numpy as jnp
from jax import lax
from jax.experimental import pallas as pl
from jax.experimental.pallas import tpu as pltpu
from jax.sharding import PartitionSpec as P

BLOCK = 64
RB = 32
GROUP = 2
OUTER = 64
M = 128
F32 = jnp.float32
BF16 = jnp.bfloat16
HIGHEST = lax.Precision.HIGHEST
VMEM = pl.BlockSpec(memory_space=pltpu.VMEM)
PARAMS = pltpu.CompilerParams(vmem_limit_bytes=40 * 1024 * 1024)


def split(x):
    hi = x.astype(BF16)
    return hi, (x - hi.astype(F32)).astype(BF16)


def dot(a, b):
    return jnp.dot(a, b, preferred_element_type=F32)


def dot_t(a, b):
    return lax.dot_general(a, b, (((0,), (0,)), ((), ())), preferred_element_type=F32)


def dot_f32(a, b):
    return jnp.dot(a, b, precision=HIGHEST, preferred_element_type=F32)


def pack_kernel(total_blocks, *refs):
    sent, out, held, sems = refs[:4], refs[4], refs[5:9], refs[9]
    copies = [pltpu.make_async_copy(sent[i], held[i], sems.at[i]) for i in range(4)]
    for copy in copies:
        copy.start()
    for copy in copies:
        copy.wait()
    pupils, starts, counts, weights = held
    tiles = starts.shape[0]
    lane = lax.broadcasted_iota(jnp.int32, (128, 2 * BLOCK), 1)
    start = starts[...]
    root = jnp.sqrt(weights[...])
    first_live = jnp.where(counts[...] > 0, root, 0.0)
    second_live = jnp.where((counts[...] > 1) & (start + 1 < total_blocks), root, 0.0)
    for t in range(tiles):
        first_column = jnp.broadcast_to(first_live[t : t + 1, :], (128, 128)).T
        second_column = jnp.broadcast_to(second_live[t : t + 1, :], (128, 128)).T
        first = pupils[pl.ds(256 * t, 128, stride=2), :] * first_column
        second = pupils[pl.ds(256 * t + 1, 128, stride=2), :] * second_column
        real = jnp.where(lane < BLOCK, first, pltpu.roll(second, BLOCK, 1))
        imag = jnp.where(lane < BLOCK, pltpu.roll(first, BLOCK, 1), second)
        out[128 * t : 128 * t + 128, :] = real
        out[128 * (tiles + t) : 128 * (tiles + t) + 128, :] = imag
    out[256 * tiles :, :] = jnp.zeros((8, 128), F32)
    out[256 * tiles : 256 * tiles + tiles, :] = lax.rem(start, RB).astype(F32)


def pack(pupils, starts, counts, weights, total_blocks):
    slots = pupils.shape[0]
    return pl.pallas_call(
        partial(pack_kernel, total_blocks),
        out_shape=jax.ShapeDtypeStruct((2 * slots + 8, 128), F32),
        in_specs=[pl.BlockSpec(memory_space=pl.ANY)] * 4,
        out_specs=VMEM,
        scratch_shapes=[
            pltpu.VMEM((2 * slots, 128), F32),
            pltpu.VMEM((slots // 128, 128), jnp.int32),
            pltpu.VMEM((slots // 128, 128), jnp.int32),
            pltpu.VMEM((slots // 128, 128), F32),
            pltpu.SemaphoreType.DMA((4,)),
        ],
        compiler_params=PARAMS,
        name="pack",
    )(
        *(
            pltpu.with_memory_space_constraint(x, pltpu.HBM)
            for x in (
                pupils.reshape(2 * slots, 128),
                starts.reshape(-1, 128),
                counts.reshape(-1, 128),
                weights.reshape(-1, 128),
            )
        )
    )


def factors(chunk):
    count = (chunk.shape[0] - 8) // 2
    real = chunk[:count, :]
    imag = chunk[count : 2 * count, :]
    left = jnp.concatenate([real.T, imag.T], axis=1).astype(BF16)
    right = []
    for scale, real, imag in zip((0.5, 1.0), split(real), split(imag)):
        right.append(
            jnp.concatenate(
                [
                    jnp.concatenate([real, -imag], axis=1),
                    jnp.concatenate([imag, real], axis=1),
                ],
                axis=0,
            )
            * jnp.asarray(scale, BF16)
        )
    places = [chunk[2 * count + t : 2 * count + t + 1, :] for t in range(count // 128)]
    place = jnp.broadcast_to(jnp.concatenate(places + places, axis=1), (16, 2 * count))
    return left, right[0], right[1], place


def at_block(part, place, b):
    mask = jnp.where(place == b, 1.0, 0.0).astype(BF16)[None]
    return (part.reshape(8, 16, -1) * mask).reshape(part.shape)


def hermitian(q):
    real, imag = q[:, :128], q[:, 128:]
    return jnp.concatenate([real + real.T, imag - imag.T], axis=1)


def build_kernel(add, last, chunk, *refs):
    refs = list(refs)
    before = refs.pop(0) if add else None
    lhs = refs.pop()
    left, right_hi, right_lo, place = factors(chunk)

    def one_group(g, carry):
        for j in range(GROUP):
            b = (g * GROUP + j).astype(F32)
            lhs[j * 128 : (j + 1) * 128, :] = at_block(left, place, b)
        at = pl.ds(pl.multiple_of(g * GROUP * 128, GROUP * 128), GROUP * 128)
        hi = lhs[...]
        total = dot(hi, right_hi) + dot(hi, right_lo)
        if add:
            total = before[at, :] + total
        if last:
            for j in range(GROUP):
                one = pl.ds(pl.multiple_of((g * GROUP + j) * 128, 128), 128)
                refs[0][one, :], refs[1][one, :] = split(
                    hermitian(total[j * 128 : (j + 1) * 128, :])
                )
        else:
            refs[0][at, :] = total
        return carry

    lax.fori_loop(0, RB // GROUP, one_group, 0, unroll=RB // GROUP)


def build(chunk, before, last=False):
    count = (chunk.shape[0] - 8) // 2
    add = before is not None
    shape = (RB * 128, 256)
    out = [jax.ShapeDtypeStruct(shape, BF16)] * 2 if last else [jax.ShapeDtypeStruct(shape, F32)]
    result = pl.pallas_call(
        partial(build_kernel, add, last),
        out_shape=out,
        in_specs=[VMEM] * (1 + add),
        out_specs=[VMEM] * len(out),
        scratch_shapes=[pltpu.VMEM((GROUP * 128, 2 * count), BF16)],
        input_output_aliases={1: 0} if add and not last else {},
        compiler_params=PARAMS,
        cost_estimate=pl.CostEstimate(
            flops=1 << 20, bytes_accessed=1 << 16, transcendentals=0
        ),
        name="band_terms",
    )(chunk, *([before] if add else []))
    return result if last else result[0]


def wide(parts):
    return jnp.concatenate([parts[0], parts[1]], axis=1)


def edge_kernel(chunk, before, x, after_out, before_out):
    left, right_hi, right_lo, place = factors(chunk)
    blocks = (0, RB - 2, RB - 1)
    left = jnp.concatenate([at_block(left, place, float(b)) for b in blocks], axis=0)
    total = dot(left, right_hi) + dot(left, right_lo)
    first, second, third = [
        hermitian(before[b * 128 : (b + 1) * 128, :] + total[i * 128 : (i + 1) * 128, :])
        for i, b in enumerate(blocks)
    ]
    after_out[:BLOCK, :] = second[BLOCK:, :]
    after_out[BLOCK : 3 * BLOCK, :] = third
    after_out[3 * BLOCK :, :] = wide(x[:, x.shape[1] - 2 * BLOCK :, :])
    before_out[:BLOCK, :] = first[:BLOCK, :]
    before_out[BLOCK:, :] = wide(x[:, : 2 * BLOCK, :])


def build_edges(chunk, before, x):
    return pl.pallas_call(
        edge_kernel,
        out_shape=(
            jax.ShapeDtypeStruct((5 * BLOCK, 256), F32),
            jax.ShapeDtypeStruct((3 * BLOCK, 256), F32),
        ),
        in_specs=[VMEM] * 3,
        out_specs=(VMEM, VMEM),
        compiler_params=PARAMS,
        name="edge_terms",
    )(chunk, before, x)


def real_form(rows):
    return jnp.concatenate(
        [rows, jnp.concatenate([-rows[:, M:], rows[:, :M]], axis=1)], axis=0
    )


def times(g_hi, g_lo, hi, lo):
    hi, lo = real_form(hi), real_form(lo)
    return dot(g_hi, hi) + dot(g_hi, lo) + dot(g_lo, hi)


def gram_of(hi, lo):
    half = jnp.asarray(0.5, BF16)
    q = 0.0
    for cols in (slice(0, M), slice(M, 2 * M)):
        q += dot_t(hi[:, cols], jnp.concatenate([hi[:, cols] * half, lo[:, cols]], axis=1))
    q = q[:, :M] + q[:, M:]
    return q + q.T


def prepare_kernel(x, hi_out, lo_out):
    for i in range(0, x.shape[1], 256):
        hi_out[i : i + 256, :], lo_out[i : i + 256, :] = split(wide(x[:, i : i + 256, :]))


def prepare(x):
    shape = jax.ShapeDtypeStruct((x.shape[1], 256), BF16)
    return pl.pallas_call(
        prepare_kernel,
        out_shape=(shape, shape),
        in_specs=[VMEM],
        out_specs=(VMEM, VMEM),
        compiler_params=PARAMS,
        cost_estimate=pl.CostEstimate(flops=1 << 20, bytes_accessed=4 << 20, transcendentals=0),
        name="prepare",
    )(x)


def apply_kernel(g_hi, g_lo, left, right, x_hi, x_lo, z_hi, z_lo, grams, p_hi, p_lo):
    rows = RB * BLOCK
    left_hi, left_lo = split(left[: 3 * BLOCK, :])
    right_hi, right_lo = split(right[:BLOCK, :])

    def put(e, block):
        at = pl.ds(pl.multiple_of(e * BLOCK, BLOCK), BLOCK)
        p_hi[at, :], p_lo[at, :] = split(block)

    def join(a, b):
        return jnp.concatenate([a, b], axis=0)

    head = split(left[3 * BLOCK :, :])
    tail = split(right[BLOCK:, :])
    spill = times(left_hi[:BLOCK], left_lo[:BLOCK], head[0], head[1])
    both = times(
        left_hi[BLOCK:],
        left_lo[BLOCK:],
        join(head[0][BLOCK:], x_hi[:BLOCK, :]),
        join(head[1][BLOCK:], x_lo[:BLOCK, :]),
    )
    first_block = spill + both[:BLOCK]
    put(0, first_block)

    def first(b, carry):
        spill, top = carry
        at = pl.ds(pl.multiple_of(b * 128, 128), 128)
        win = pl.ds(pl.multiple_of(b * BLOCK, BLOCK), 128)
        both = times(g_hi[at, :], g_lo[at, :], x_hi[win, :], x_lo[win, :])
        block = both[:BLOCK] + spill
        put(b + 1, block)
        return both[BLOCK:], jnp.maximum(top, jnp.abs(block))

    carry = first(0, (both[BLOCK:], jnp.abs(first_block)))
    spill, top = lax.fori_loop(1, RB - 1, first, carry, unroll=RB - 2)
    both = times(
        g_hi[(RB - 1) * 128 :, :],
        g_lo[(RB - 1) * 128 :, :],
        join(x_hi[rows - BLOCK :, :], tail[0][:BLOCK]),
        join(x_lo[rows - BLOCK :, :], tail[1][:BLOCK]),
    )
    block = both[:BLOCK] + spill
    put(RB, block)
    last_block = both[BLOCK:] + times(right_hi, right_lo, tail[0], tail[1])
    put(RB + 1, last_block)
    top = jnp.maximum(jnp.maximum(top, jnp.abs(block)), jnp.abs(last_block))
    top = jnp.max(top, axis=0, keepdims=True)
    top = jnp.maximum(top[:, :M], top[:, M:])
    scale = jnp.where(top > 0, 1.0 / jnp.where(top > 0, top, 1.0), 0.0)
    scale = jnp.concatenate([scale, scale], axis=1)

    inner = pl.ds(BLOCK, rows)
    gram_1 = gram_of(p_hi[inner, :], p_lo[inner, :])

    def second(b, spill):
        at = pl.ds(pl.multiple_of(b * 128, 128), 128)
        win = pl.ds(pl.multiple_of((b + 1) * BLOCK, BLOCK), 128)
        both = times(g_hi[at, :], g_lo[at, :], p_hi[win, :], p_lo[win, :])
        out = pl.ds(pl.multiple_of(b * BLOCK, BLOCK), BLOCK)
        z_hi[out, :], z_lo[out, :] = split((both[:BLOCK] + spill) * scale)
        return both[BLOCK:]

    spill = times(left_hi[2 * BLOCK :], left_lo[2 * BLOCK :], p_hi[:128, :], p_lo[:128, :])
    lax.fori_loop(0, RB, second, spill, unroll=RB // 2)
    gram_2 = gram_of(z_hi[...], z_lo[...])
    row = lax.broadcasted_iota(jnp.int32, (M, M), 0)
    col = lax.broadcasted_iota(jnp.int32, (M, M), 1)
    grams[:M, :] = jnp.where(row >= col, gram_1, gram_2)
    diagonal = jnp.sum(jnp.where(row == col, gram_2, 0.0), axis=0, keepdims=True)
    grams[M:, :] = jnp.concatenate([diagonal, top, jnp.zeros((6, M), F32)], axis=0)


def apply_twice(g_hi, g_lo, left, right, x_hi, x_lo):
    rows = RB * BLOCK
    return pl.pallas_call(
        apply_kernel,
        out_shape=(
            jax.ShapeDtypeStruct((rows, 256), BF16),
            jax.ShapeDtypeStruct((rows, 256), BF16),
            jax.ShapeDtypeStruct((M + 8, M), F32),
        ),
        in_specs=[VMEM] * 6,
        out_specs=(VMEM, VMEM, VMEM),
        scratch_shapes=[pltpu.VMEM((rows + 2 * BLOCK, 256), BF16)] * 2,
        compiler_params=PARAMS,
        cost_estimate=pl.CostEstimate(
            flops=12 * RB * 128 * 256 * 256, bytes_accessed=12 << 20, transcendentals=0
        ),
        name="apply_twice",
    )(g_hi, g_lo, left, right, x_hi, x_lo)


def inverse_factor(a, work):
    row = lax.broadcasted_iota(jnp.int32, (M, M), 0)
    col = lax.broadcasted_iota(jnp.int32, (M, M), 1)
    work[:, :M] = a
    work[:, M:] = jnp.where(row == col, 1.0, 0.0)
    sub = lax.broadcasted_iota(jnp.int32, (8, M), 0)
    groups = OUTER // 8

    def line(x, j):
        return x[j : j + 1, :]

    def tall(x, j):
        return jnp.broadcast_to(line(x, j), (8, M))

    def spread(x, at):
        return [jnp.broadcast_to(x[:, at + k : at + k + 1], (8, M)) for k in range(8)]

    for top in range(0, M, OUTER):
        left = [work[top + 8 * g : top + 8 * g + 8, :M] for g in range(groups)]
        right = [work[top + 8 * g : top + 8 * g + 8, M:] for g in range(groups)]
        ahead = spread(left[0], top)
        for q in range(groups):
            at = top + 8 * q
            cols = {q: ahead, **{g: spread(left[g], at) for g in range(q + 1, groups)}}
            more = q + 1 < groups
            if more:
                ahead, mine = spread(left[q + 1], at + 8), spread(left[q], at + 8)
            scales = jnp.zeros((8, M), F32)
            for j in range(0, 8, 2):
                a0, a1, a2 = tall(cols[q][j], j), tall(cols[q][j], j + 1), tall(cols[q][j + 1], j + 1)
                det = a0 * a2 - a1 * a1
                inverse = pltpu.reciprocal(det, approx=False)
                root = lax.rsqrt(a0)
                ratio = a1 * (root * root)
                scales = jnp.where(sub == j, root, scales)
                scales = jnp.where(sub == j + 1, lax.rsqrt(det) * (a0 * root), scales)
                row_0 = [line(cols[q][k], j) for k in range(8)]
                row_1 = [line(cols[q][k], j + 1) for k in range(8)]
                left_0, left_1 = line(left[q], j), line(left[q], j + 1)
                right_0, right_1 = line(right[q], j), line(right[q], j + 1)
                if more:
                    mine_0 = [line(x, j) for x in mine]
                    mine_1 = [line(x, j + 1) for x in mine]
                for g in range(q, groups):
                    c0, c1 = cols[g][j], cols[g][j + 1]
                    y0 = a2 * c0 - a1 * c1
                    y1 = a0 * c1 - a1 * c0
                    if g == q:
                        y0 = jnp.where(sub > j + 1, y0, 0.0)
                        y1 = jnp.where(sub > j + 1, y1, 0.0)
                    for k in range(j + 2, 8):
                        cols[g][k] = cols[g][k] - (y0 * row_0[k] + y1 * row_1[k]) * inverse
                    x0, x1 = y0 * inverse, y1 * inverse
                    if g == q:
                        x0 = jnp.where(sub == j + 1, ratio, x0)
                    left[g] = left[g] - (x0 * left_0 + x1 * left_1)
                    right[g] = right[g] - (x0 * right_0 + x1 * right_1)
                    if more and g <= q + 1:
                        part = mine if g == q else ahead
                        for k in range(8):
                            part[k] = part[k] - (x0 * mine_0[k] + x1 * mine_1[k])
            left[q] = left[q] * scales
            right[q] = right[q] * scales
        for g in range(groups):
            work[top + 8 * g : top + 8 * g + 8, :M] = left[g]
            work[top + 8 * g : top + 8 * g + 8, M:] = right[g]
        if top + OUTER < M:
            panel = work[top : top + OUTER, :]
            update = lax.dot_general(
                panel[:, :M], panel, (((0,), (0,)), ((), ())),
                precision=HIGHEST, preferred_element_type=F32,
            )
            work[top + OUTER :, :] = work[top + OUTER :, :] - update[top + OUTER :, :]
    return work[:, M:]


def finish_kernel(total_rows, grams, own, z_hi, z_lo, out, work):
    peers = grams.shape[0]
    row = lax.broadcasted_iota(jnp.int32, (M, M), 0)
    col = lax.broadcasted_iota(jnp.int32, (M, M), 1)
    eye = jnp.where(row == col, 1.0, 0.0)

    def as_column(v):
        return jnp.sum(eye * v, axis=1, keepdims=True)

    def row_of(x):
        return jnp.sum(eye * x, axis=0, keepdims=True)

    total = grams[0, :M, :]
    for r in range(1, peers):
        total = total + grams[r, :M, :]
    gram = jnp.where(row >= col, total, total.T)
    norm = lax.rsqrt(row_of(gram))
    inverse = inverse_factor(gram * norm * as_column(norm), work)
    total = jnp.zeros((M, M), F32)
    for r in range(peers):
        size = norm * grams[r, M + 1 : M + 2, :]
        second = jnp.where(row == col, grams[r, M : M + 1, :], grams[r, :M, :])
        total = total + second * size * as_column(size)
    gram = jnp.where(row <= col, total, total.T)
    gram = dot_f32(dot_f32(inverse, gram), inverse.T)
    scale = lax.rsqrt(row_of(gram))
    second = inverse_factor(gram * scale * as_column(scale), work) * scale
    inverse = dot_f32(second, inverse)
    change = (inverse * (norm * own[M + 1 : M + 2, :] * (total_rows**0.5))).T
    c_hi, c_lo = split(change)
    right = jnp.concatenate(
        [
            jnp.concatenate([c_hi, c_lo], axis=1),
            jnp.concatenate([c_hi, jnp.zeros_like(c_lo)], axis=1),
        ],
        axis=0,
    )
    step = 256

    def rows_of(i, carry):
        at = pl.ds(pl.multiple_of(i * step, step), step)
        hi, lo = z_hi[at, :], z_lo[at, :]
        for part in range(2):
            cols = slice(part * M, part * M + M)
            both = dot(jnp.concatenate([hi[:, cols], lo[:, cols]], axis=1), right)
            out[part, at, :] = both[:, :M] + both[:, M:]
        return carry

    lax.fori_loop(0, z_hi.shape[0] // step, rows_of, 0, unroll=True)


def finish(grams, own, z_hi, z_lo, total_rows):
    return pl.pallas_call(
        partial(finish_kernel, total_rows),
        out_shape=jax.ShapeDtypeStruct((2, z_hi.shape[0], M), F32),
        in_specs=[VMEM] * 4,
        out_specs=VMEM,
        scratch_shapes=[pltpu.VMEM((M, 2 * M), F32)],
        compiler_params=PARAMS,
        name="finish",
    )(grams, own, z_hi, z_lo)


def shifted(x, by):
    peers = lax.axis_size("blk")
    pairs = [(i, i + by) for i in range(peers) if 0 <= i + by < peers]
    return lax.ppermute(x, "blk", pairs)


def swapped(x, far):
    peers = lax.axis_size("src")
    return lax.ppermute(x, "src", [(i, i ^ far) for i in range(peers)])


def gathered(own, ready):
    peers = lax.axis_size("src")
    if peers & (peers - 1):
        chunks = [
            lax.ppermute(own, "src", [(i, (i + k) % peers) for i in range(peers)])
            for k in range(1, peers)
        ]
        return chunks, ready
    far = peers // 2
    chunks = []
    while far:
        if chunks:
            chunks, ready = lax.optimization_barrier((chunks, ready))
        chunks = chunks + [swapped(c, far) for c in [own] + chunks]
        far //= 2
    return chunks, ready


def per_device(pupils, starts, counts, weights, start_block):
    regions = lax.axis_size("blk")
    size = start_block.shape[1]

    own = pack(pupils, starts, counts, weights, regions * RB)
    ready = (build(own, None), *prepare(start_block))
    chunks, ready = gathered(own, ready)
    band, x_hi, x_lo = ready
    for chunk in chunks[:-1]:
        band = build(chunk, band)
    after, before = build_edges(chunks[-1], band, start_block)
    left, right = shifted(after, 1), shifted(before, -1)
    g_hi, g_lo = build(chunks[-1], band, last=True)
    z_hi, z_lo, own_grams = apply_twice(g_hi, g_lo, left, right, x_hi, x_lo)
    grams = lax.all_gather(own_grams, "blk", axis=0)
    return finish(grams, own_grams, z_hi, z_lo, 2.0 * size * regions)


def solution(mesh):
    placed = (
        P(("groups", "src", "blk"), None, None),
        P(("groups", "src", "blk")),
        P(("groups", "src", "blk")),
        P(("groups", "src", "blk")),
        P("groups", "blk", None),
    )
    return jax.shard_map(
        per_device, mesh=mesh, in_specs=placed, out_specs=P("groups", "blk", None), check_vma=False
    )
```

```python
from functools import partial

import jax
import jax.numpy as jnp
from jax import lax
from jax.experimental import pallas as pl
from jax.experimental.pallas import tpu as pltpu
from jax.sharding import PartitionSpec as P

BLOCK = 64
RB = 32
GROUP = 2
OUTER = 64
M = 128
F32 = jnp.float32
BF16 = jnp.bfloat16
HIGHEST = lax.Precision.HIGHEST
VMEM = pl.BlockSpec(memory_space=pltpu.VMEM)
PARAMS = pltpu.CompilerParams(vmem_limit_bytes=16 * 1024 * 1024)


def split(x):
    hi = x.astype(BF16)
    return hi, (x - hi.astype(F32)).astype(BF16)


def dot(a, b):
    return jnp.dot(a, b, preferred_element_type=F32)


def dot_t(a, b):
    return lax.dot_general(a, b, (((0,), (0,)), ((), ())), preferred_element_type=F32)


def dot_f32(a, b):
    return jnp.dot(a, b, precision=HIGHEST, preferred_element_type=F32)


def pack_kernel(total_blocks, *refs):
    sent, out, held, sems = refs[:4], refs[4], refs[5:9], refs[9]
    copies = [pltpu.make_async_copy(sent[i], held[i], sems.at[i]) for i in range(4)]
    for copy in copies:
        copy.start()
    for copy in copies:
        copy.wait()
    pupils, starts, counts, weights = held
    tiles = starts.shape[0]
    lane = lax.broadcasted_iota(jnp.int32, (128, 2 * BLOCK), 1)
    start = starts[...]
    root = jnp.sqrt(weights[...])
    first_live = jnp.where(counts[...] > 0, root, 0.0)
    second_live = jnp.where((counts[...] > 1) & (start + 1 < total_blocks), root, 0.0)
    for t in range(tiles):
        first_column = jnp.broadcast_to(first_live[t : t + 1, :], (128, 128)).T
        second_column = jnp.broadcast_to(second_live[t : t + 1, :], (128, 128)).T
        first = pupils[pl.ds(256 * t, 128, stride=2), :] * first_column
        second = pupils[pl.ds(256 * t + 1, 128, stride=2), :] * second_column
        real = jnp.where(lane < BLOCK, first, pltpu.roll(second, BLOCK, 1))
        imag = jnp.where(lane < BLOCK, pltpu.roll(first, BLOCK, 1), second)
        out[128 * t : 128 * t + 128, :] = real
        out[128 * (tiles + t) : 128 * (tiles + t) + 128, :] = imag
    out[256 * tiles :, :] = jnp.zeros((8, 128), F32)
    out[256 * tiles : 256 * tiles + tiles, :] = lax.rem(start, RB).astype(F32)
    out[256 * tiles + 7 :, :] = lax.rem(lax.div(start[:1, :], RB), 2).astype(F32)


def pack(pupils, starts, counts, weights, total_blocks):
    slots = pupils.shape[0]
    return pl.pallas_call(
        partial(pack_kernel, total_blocks),
        out_shape=jax.ShapeDtypeStruct((2 * slots + 8, 128), F32),
        in_specs=[pl.BlockSpec(memory_space=pl.ANY)] * 4,
        out_specs=VMEM,
        scratch_shapes=[
            pltpu.VMEM((2 * slots, 128), F32),
            pltpu.VMEM((slots // 128, 128), jnp.int32),
            pltpu.VMEM((slots // 128, 128), jnp.int32),
            pltpu.VMEM((slots // 128, 128), F32),
            pltpu.SemaphoreType.DMA((4,)),
        ],
        compiler_params=PARAMS,
        name="pack",
    )(
        *(
            pltpu.with_memory_space_constraint(x, pltpu.HBM)
            for x in (
                pupils.reshape(2 * slots, 128),
                starts.reshape(-1, 128),
                counts.reshape(-1, 128),
                weights.reshape(-1, 128),
            )
        )
    )


def factors(chunk):
    count = (chunk.shape[0] - 8) // 2
    real = chunk[:count, :]
    imag = chunk[count : 2 * count, :]
    left = jnp.concatenate([real.T, imag.T], axis=1).astype(BF16)
    right = []
    for scale, real, imag in zip((0.5, 1.0), split(real), split(imag)):
        right.append(
            jnp.concatenate(
                [
                    jnp.concatenate([real, -imag], axis=1),
                    jnp.concatenate([imag, real], axis=1),
                ],
                axis=0,
            )
            * jnp.asarray(scale, BF16)
        )
    places = [chunk[2 * count + t : 2 * count + t + 1, :] for t in range(count // 128)]
    place = jnp.broadcast_to(jnp.concatenate(places + places, axis=1), (16, 2 * count))
    return left, right[0], right[1], place


def at_block(part, place, b):
    mask = jnp.where(place == b, 1.0, 0.0).astype(BF16)[None]
    return (part.reshape(8, 16, -1) * mask).reshape(part.shape)


def hermitian(q):
    real, imag = q[:, :128], q[:, 128:]
    return jnp.concatenate([real + real.T, imag - imag.T], axis=1)


def build_kernel(add, last, chunk, *refs):
    refs = list(refs)
    before = refs.pop(0) if add else None
    lhs = refs.pop()
    left, right_hi, right_lo, place = factors(chunk)

    def one_group(g, carry):
        for j in range(GROUP):
            b = (g * GROUP + j).astype(F32)
            lhs[j * 128 : (j + 1) * 128, :] = at_block(left, place, b)
        at = pl.ds(pl.multiple_of(g * GROUP * 128, GROUP * 128), GROUP * 128)
        hi = lhs[...]
        total = dot(hi, right_hi) + dot(hi, right_lo)
        if add:
            total = before[at, :] + total
        if last:
            for j in range(GROUP):
                one = pl.ds(pl.multiple_of((g * GROUP + j) * 128, 128), 128)
                refs[0][one, :], refs[1][one, :] = split(
                    hermitian(total[j * 128 : (j + 1) * 128, :])
                )
        else:
            refs[0][at, :] = total
        return carry

    lax.fori_loop(0, RB // GROUP, one_group, 0, unroll=RB // GROUP)


def build(chunk, before, last=False):
    count = (chunk.shape[0] - 8) // 2
    add = before is not None
    shape = (RB * 128, 256)
    out = [jax.ShapeDtypeStruct(shape, BF16)] * 2 if last else [jax.ShapeDtypeStruct(shape, F32)]
    result = pl.pallas_call(
        partial(build_kernel, add, last),
        out_shape=out,
        in_specs=[VMEM] * (1 + add),
        out_specs=[VMEM] * len(out),
        scratch_shapes=[pltpu.VMEM((GROUP * 128, 2 * count), BF16)],
        input_output_aliases={1: 0} if add and not last else {},
        compiler_params=PARAMS,
        cost_estimate=pl.CostEstimate(
            flops=1 << 20, bytes_accessed=1 << 16, transcendentals=0
        ),
        name="band_terms",
    )(chunk, *([before] if add else []))
    return result if last else result[0]


def wide(parts):
    return jnp.concatenate([parts[0], parts[1]], axis=1)


def real_form(rows):
    return jnp.concatenate(
        [rows, jnp.concatenate([-rows[:, M:], rows[:, :M]], axis=1)], axis=0
    )


def times(g_hi, g_lo, hi, lo):
    hi, lo = real_form(hi), real_form(lo)
    return dot(g_hi, hi) + dot(g_hi, lo) + dot(g_lo, hi)


def gram_of(hi, lo):
    half = jnp.asarray(0.5, BF16)
    q = 0.0
    for cols in (slice(0, M), slice(M, 2 * M)):
        q += dot_t(hi[:, cols], jnp.concatenate([hi[:, cols] * half, lo[:, cols]], axis=1))
    q = q[:, :M] + q[:, M:]
    return q + q.T


def in_odd_region(chunk):
    row = chunk[chunk.shape[0] - 1 :, :]
    return jnp.concatenate([row, row], axis=1) == 1.0


def edge_kernel(chunk, before, x, first_out, second_out):
    left, right_hi, right_lo, place = factors(chunk)
    blocks = (0, RB - 2, RB - 1)
    left = jnp.concatenate([at_block(left, place, float(b)) for b in blocks], axis=0)
    total = dot(left, right_hi) + dot(left, right_lo)
    head, next_last, last = [
        hermitian(before[b * 128 : (b + 1) * 128, :] + total[i * 128 : (i + 1) * 128, :])
        for i, b in enumerate(blocks)
    ]
    size = x.shape[1]
    start = wide(x[:, : 2 * BLOCK, :])
    stop = wide(x[:, size - 2 * BLOCK :, :])
    held = jnp.concatenate([stop[BLOCK:], jnp.zeros((BLOCK, 256), F32)], axis=0)
    own = times(*split(last), *split(held))
    to_after = jnp.concatenate(
        [
            own[:BLOCK] + times(*split(next_last[BLOCK:]), *split(stop)),
            own[BLOCK:],
            last[BLOCK:],
        ],
        axis=0,
    )
    to_before = jnp.concatenate(
        [times(*split(head[:BLOCK]), *split(start)), start[:BLOCK], jnp.zeros((BLOCK, 256), F32)],
        axis=0,
    )
    is_odd = in_odd_region(chunk)
    first_out[...] = jnp.where(is_odd, to_after, to_before)
    second_out[...] = jnp.where(is_odd, to_before, to_after)


def build_edges(chunk, before, x):
    shape = jax.ShapeDtypeStruct((3 * BLOCK, 256), F32)
    return pl.pallas_call(
        edge_kernel,
        out_shape=(shape, shape),
        in_specs=[VMEM] * 3,
        out_specs=(VMEM, VMEM),
        compiler_params=PARAMS,
        name="edge_terms",
    )(chunk, before, x)


def prepare_kernel(x, hi_out, lo_out):
    for i in range(0, x.shape[1], 256):
        hi_out[i : i + 256, :], lo_out[i : i + 256, :] = split(wide(x[:, i : i + 256, :]))


def prepare(x):
    shape = jax.ShapeDtypeStruct((x.shape[1], 256), BF16)
    return pl.pallas_call(
        prepare_kernel,
        out_shape=(shape, shape),
        in_specs=[VMEM],
        out_specs=(VMEM, VMEM),
        compiler_params=PARAMS,
        cost_estimate=pl.CostEstimate(flops=1 << 20, bytes_accessed=4 << 20, transcendentals=0),
        name="prepare",
    )(x)


def apply_kernel(own, g_hi, g_lo, swap_1, swap_2, x_hi, x_lo, z_hi, z_lo, grams, p_hi, p_lo):
    rows = RB * BLOCK
    is_odd = in_odd_region(own)
    left = jnp.where(is_odd, swap_2[...], swap_1[...])
    right = jnp.where(is_odd, swap_1[...], swap_2[...])
    into = left[2 * BLOCK :]
    into_hi, into_lo = split(into)
    none = jnp.zeros((BLOCK, 128), F32)
    out_of = [jnp.concatenate([none, part], axis=0).T[:BLOCK] for part in (into[:, :M], into[:, M:])]
    out_hi, out_lo = split(jnp.concatenate([out_of[0], -out_of[1]], axis=1))
    tail = split(right[BLOCK : 2 * BLOCK])
    nothing = jnp.zeros((BLOCK, 256), BF16)

    def put(e, block):
        at = pl.ds(pl.multiple_of(e * BLOCK, BLOCK), BLOCK)
        p_hi[at, :], p_lo[at, :] = split(block)

    def join(a, b):
        return jnp.concatenate([a, b], axis=0)

    both = times(
        join(out_hi, into_hi),
        join(out_lo, into_lo),
        join(nothing, x_hi[:BLOCK, :]),
        join(nothing, x_lo[:BLOCK, :]),
    ) + left[: 2 * BLOCK]
    first_block = both[:BLOCK]
    put(0, first_block)

    def first(b, carry):
        spill, top = carry
        at = pl.ds(pl.multiple_of(b * 128, 128), 128)
        win = pl.ds(pl.multiple_of(b * BLOCK, BLOCK), 128)
        both = times(g_hi[at, :], g_lo[at, :], x_hi[win, :], x_lo[win, :])
        block = both[:BLOCK] + spill
        put(b + 1, block)
        return both[BLOCK:], jnp.maximum(top, jnp.abs(block))

    carry = first(0, (both[BLOCK:], jnp.abs(first_block)))
    spill, top = lax.fori_loop(1, RB - 1, first, carry, unroll=RB - 2)
    both = times(
        g_hi[(RB - 1) * 128 :, :],
        g_lo[(RB - 1) * 128 :, :],
        join(x_hi[rows - BLOCK :, :], tail[0]),
        join(x_lo[rows - BLOCK :, :], tail[1]),
    )
    block = both[:BLOCK] + spill
    put(RB, block)
    last_block = both[BLOCK:] + right[:BLOCK]
    put(RB + 1, last_block)
    top = jnp.maximum(jnp.maximum(top, jnp.abs(block)), jnp.abs(last_block))
    top = jnp.max(top, axis=0, keepdims=True)
    top = jnp.maximum(top[:, :M], top[:, M:])
    scale = jnp.where(top > 0, 1.0 / jnp.where(top > 0, top, 1.0), 0.0)
    scale = jnp.concatenate([scale, scale], axis=1)

    inner = pl.ds(BLOCK, rows)
    gram_1 = gram_of(p_hi[inner, :], p_lo[inner, :])

    def second(b, spill):
        at = pl.ds(pl.multiple_of(b * 128, 128), 128)
        win = pl.ds(pl.multiple_of((b + 1) * BLOCK, BLOCK), 128)
        both = times(g_hi[at, :], g_lo[at, :], p_hi[win, :], p_lo[win, :])
        out = pl.ds(pl.multiple_of(b * BLOCK, BLOCK), BLOCK)
        z_hi[out, :], z_lo[out, :] = split((both[:BLOCK] + spill) * scale)
        return both[BLOCK:]

    spill = times(into_hi, into_lo, p_hi[:128, :], p_lo[:128, :])
    lax.fori_loop(0, RB, second, spill, unroll=RB // 2)
    gram_2 = gram_of(z_hi[...], z_lo[...])
    row = lax.broadcasted_iota(jnp.int32, (M, M), 0)
    col = lax.broadcasted_iota(jnp.int32, (M, M), 1)
    grams[:M, :] = jnp.where(row >= col, gram_1, gram_2)
    diagonal = jnp.sum(jnp.where(row == col, gram_2, 0.0), axis=0, keepdims=True)
    grams[M:, :] = jnp.concatenate([diagonal, top, jnp.zeros((6, M), F32)], axis=0)


def apply_twice(own, g_hi, g_lo, swap_1, swap_2, x_hi, x_lo):
    rows = RB * BLOCK
    return pl.pallas_call(
        apply_kernel,
        out_shape=(
            jax.ShapeDtypeStruct((rows, 256), BF16),
            jax.ShapeDtypeStruct((rows, 256), BF16),
            jax.ShapeDtypeStruct((M + 8, M), F32),
        ),
        in_specs=[VMEM] * 7,
        out_specs=(VMEM, VMEM, VMEM),
        scratch_shapes=[pltpu.VMEM((rows + 2 * BLOCK, 256), BF16)] * 2,
        compiler_params=PARAMS,
        cost_estimate=pl.CostEstimate(
            flops=12 * RB * 128 * 256 * 256, bytes_accessed=12 << 20, transcendentals=0
        ),
        name="apply_twice",
    )(own, g_hi, g_lo, swap_1, swap_2, x_hi, x_lo)


def inverse_factor(a, work):
    row = lax.broadcasted_iota(jnp.int32, (M, M), 0)
    col = lax.broadcasted_iota(jnp.int32, (M, M), 1)
    work[:, :M] = a
    work[:, M:] = jnp.where(row == col, 1.0, 0.0)
    sub = lax.broadcasted_iota(jnp.int32, (8, M), 0)
    groups = OUTER // 8

    def line(x, j):
        return x[j : j + 1, :]

    def tall(x, j):
        return jnp.broadcast_to(line(x, j), (8, M))

    def spread(x, at):
        return [jnp.broadcast_to(x[:, at + k : at + k + 1], (8, M)) for k in range(8)]

    for top in range(0, M, OUTER):
        left = [work[top + 8 * g : top + 8 * g + 8, :M] for g in range(groups)]
        right = [work[top + 8 * g : top + 8 * g + 8, M:] for g in range(groups)]
        ahead = spread(left[0], top)
        for q in range(groups):
            at = top + 8 * q
            cols = {q: ahead, **{g: spread(left[g], at) for g in range(q + 1, groups)}}
            more = q + 1 < groups
            if more:
                ahead, mine = spread(left[q + 1], at + 8), spread(left[q], at + 8)
            scales = jnp.zeros((8, M), F32)
            for j in range(0, 8, 2):
                a0, a1, a2 = tall(cols[q][j], j), tall(cols[q][j], j + 1), tall(cols[q][j + 1], j + 1)
                det = a0 * a2 - a1 * a1
                inverse = pltpu.reciprocal(det, approx=False)
                root = lax.rsqrt(a0)
                ratio = a1 * (root * root)
                scales = jnp.where(sub == j, root, scales)
                scales = jnp.where(sub == j + 1, lax.rsqrt(det) * (a0 * root), scales)
                row_0 = [line(cols[q][k], j) for k in range(8)]
                row_1 = [line(cols[q][k], j + 1) for k in range(8)]
                left_0, left_1 = line(left[q], j), line(left[q], j + 1)
                right_0, right_1 = line(right[q], j), line(right[q], j + 1)
                if more:
                    mine_0 = [line(x, j) for x in mine]
                    mine_1 = [line(x, j + 1) for x in mine]
                for g in range(q, groups):
                    c0, c1 = cols[g][j], cols[g][j + 1]
                    y0 = a2 * c0 - a1 * c1
                    y1 = a0 * c1 - a1 * c0
                    if g == q:
                        y0 = jnp.where(sub > j + 1, y0, 0.0)
                        y1 = jnp.where(sub > j + 1, y1, 0.0)
                    for k in range(j + 2, 8):
                        cols[g][k] = cols[g][k] - (y0 * row_0[k] + y1 * row_1[k]) * inverse
                    x0, x1 = y0 * inverse, y1 * inverse
                    if g == q:
                        x0 = jnp.where(sub == j + 1, ratio, x0)
                    left[g] = left[g] - (x0 * left_0 + x1 * left_1)
                    right[g] = right[g] - (x0 * right_0 + x1 * right_1)
                    if more and g <= q + 1:
                        part = mine if g == q else ahead
                        for k in range(8):
                            part[k] = part[k] - (x0 * mine_0[k] + x1 * mine_1[k])
            left[q] = left[q] * scales
            right[q] = right[q] * scales
        for g in range(groups):
            work[top + 8 * g : top + 8 * g + 8, :M] = left[g]
            work[top + 8 * g : top + 8 * g + 8, M:] = right[g]
        if top + OUTER < M:
            panel = work[top : top + OUTER, :]
            update = lax.dot_general(
                panel[:, :M], panel, (((0,), (0,)), ((), ())),
                precision=HIGHEST, preferred_element_type=F32,
            )
            work[top + OUTER :, :] = work[top + OUTER :, :] - update[top + OUTER :, :]
    return work[:, M:]


def finish_kernel(total_rows, *refs):
    grams, (z_hi, z_lo, out, work) = refs[:-4], refs[-4:]
    own = grams[0]
    row = lax.broadcasted_iota(jnp.int32, (M, M), 0)
    col = lax.broadcasted_iota(jnp.int32, (M, M), 1)
    eye = jnp.where(row == col, 1.0, 0.0)

    def as_column(v):
        return jnp.sum(eye * v, axis=1, keepdims=True)

    def row_of(x):
        return jnp.sum(eye * x, axis=0, keepdims=True)

    total = own[:M, :]
    for one in grams[1:]:
        total = total + one[:M, :]
    gram = jnp.where(row >= col, total, total.T)
    norm = lax.rsqrt(row_of(gram))
    inverse = inverse_factor(gram * norm * as_column(norm), work)
    total = jnp.zeros((M, M), F32)
    for one in grams:
        size = norm * one[M + 1 : M + 2, :]
        second = jnp.where(row == col, one[M : M + 1, :], one[:M, :])
        total = total + second * size * as_column(size)
    gram = jnp.where(row <= col, total, total.T)
    gram = dot_f32(dot_f32(inverse, gram), inverse.T)
    scale = lax.rsqrt(row_of(gram))
    second = inverse_factor(gram * scale * as_column(scale), work) * scale
    inverse = dot_f32(second, inverse)
    change = (inverse * (norm * own[M + 1 : M + 2, :] * (total_rows**0.5))).T
    c_hi, c_lo = split(change)
    right = jnp.concatenate(
        [
            jnp.concatenate([c_hi, c_lo], axis=1),
            jnp.concatenate([c_hi, jnp.zeros_like(c_lo)], axis=1),
        ],
        axis=0,
    )
    step = 256

    def rows_of(i, carry):
        at = pl.ds(pl.multiple_of(i * step, step), step)
        hi, lo = z_hi[at, :], z_lo[at, :]
        for part in range(2):
            cols = slice(part * M, part * M + M)
            both = dot(jnp.concatenate([hi[:, cols], lo[:, cols]], axis=1), right)
            out[part, at, :] = both[:, :M] + both[:, M:]
        return carry

    lax.fori_loop(0, z_hi.shape[0] // step, rows_of, 0, unroll=True)


def finish(grams, z_hi, z_lo, total_rows):
    return pl.pallas_call(
        partial(finish_kernel, total_rows),
        out_shape=jax.ShapeDtypeStruct((2, z_hi.shape[0], M), F32),
        in_specs=[VMEM] * (len(grams) + 2),
        out_specs=VMEM,
        scratch_shapes=[pltpu.VMEM((M, 2 * M), F32)],
        compiler_params=PARAMS,
        name="finish",
    )(*grams, z_hi, z_lo)


def neighbours(x, begin):
    pairs = [(i, i + 1) for i in range(begin, lax.axis_size("blk") - 1, 2)]
    return lax.ppermute(x, "blk", pairs + [(j, i) for i, j in pairs])


def swapped(x, far, axis="src"):
    return lax.ppermute(x, axis, [(i, i ^ far) for i in range(lax.axis_size(axis))])


def gathered(own, ready, axis="src"):
    peers = lax.axis_size(axis)
    if peers & (peers - 1):
        chunks = [
            lax.ppermute(own, axis, [(i, (i + k) % peers) for i in range(peers)])
            for k in range(1, peers)
        ]
        return chunks, ready
    far = peers // 2
    chunks = []
    while far:
        if chunks and ready:
            chunks, ready = lax.optimization_barrier((chunks, ready))
        chunks = chunks + [swapped(c, far, axis) for c in [own] + chunks]
        far //= 2
    return chunks, ready


def per_device(pupils, starts, counts, weights, start_block):
    regions = lax.axis_size("blk")
    size = start_block.shape[1]

    own = pack(pupils, starts, counts, weights, regions * RB)
    ready = (build(own, None), *prepare(start_block))
    chunks, ready = gathered(own, ready)
    band, x_hi, x_lo = ready
    for chunk in chunks[:-1]:
        band = build(chunk, band)
    swap_1, swap_2 = build_edges(chunks[-1], band, start_block)
    swap_1, swap_2 = neighbours(swap_1, 1), neighbours(swap_2, 0)
    g_hi, g_lo = build(chunks[-1], band, last=True)
    z_hi, z_lo, grams = apply_twice(own, g_hi, g_lo, swap_1, swap_2, x_hi, x_lo)
    grams = [grams] + gathered(grams, (), "blk")[0]
    return finish(grams, z_hi, z_lo, 2.0 * size * regions)


def solution(mesh):
    placed = (
        P(("groups", "src", "blk"), None, None),
        P(("groups", "src", "blk")),
        P(("groups", "src", "blk")),
        P(("groups", "src", "blk")),
        P("groups", "blk", None),
    )
    return jax.shard_map(
        per_device, mesh=mesh, in_specs=placed, out_specs=P("groups", "blk", None), check_vma=False
    )
```

```python
from functools import partial

import jax
import jax.numpy as jnp
from jax import lax
from jax.experimental import pallas as pl
from jax.experimental.pallas import tpu as pltpu
from jax.sharding import PartitionSpec as P

BLOCK = 64
RB = 32
GROUP = 2
OUTER = 64
M = 128
F32 = jnp.float32
BF16 = jnp.bfloat16
HIGHEST = lax.Precision.HIGHEST
VMEM = pl.BlockSpec(memory_space=pltpu.VMEM)
PARAMS = pltpu.CompilerParams(vmem_limit_bytes=16 * 1024 * 1024)


def split(x):
    hi = x.astype(BF16)
    return hi, (x - hi.astype(F32)).astype(BF16)


def dot(a, b):
    return jnp.dot(a, b, preferred_element_type=F32)


def dot_t(a, b):
    return lax.dot_general(a, b, (((0,), (0,)), ((), ())), preferred_element_type=F32)


def dot_f32(a, b):
    return jnp.dot(a, b, precision=HIGHEST, preferred_element_type=F32)


def pack_kernel(total_blocks, *refs):
    sent, out, held, sems = refs[:4], refs[4], refs[5:9], refs[9]
    copies = [pltpu.make_async_copy(sent[i], held[i], sems.at[i]) for i in range(4)]
    for copy in copies:
        copy.start()
    for copy in copies:
        copy.wait()
    pupils, starts, counts, weights = held
    tiles = starts.shape[0]
    lane = lax.broadcasted_iota(jnp.int32, (128, 2 * BLOCK), 1)
    start = starts[...]
    root = jnp.sqrt(weights[...])
    first_live = jnp.where(counts[...] > 0, root, 0.0)
    second_live = jnp.where((counts[...] > 1) & (start + 1 < total_blocks), root, 0.0)
    for t in range(tiles):
        first_column = jnp.broadcast_to(first_live[t : t + 1, :], (128, 128)).T
        second_column = jnp.broadcast_to(second_live[t : t + 1, :], (128, 128)).T
        first = pupils[pl.ds(256 * t, 128, stride=2), :] * first_column
        second = pupils[pl.ds(256 * t + 1, 128, stride=2), :] * second_column
        real = jnp.where(lane < BLOCK, first, pltpu.roll(second, BLOCK, 1))
        imag = jnp.where(lane < BLOCK, pltpu.roll(first, BLOCK, 1), second)
        out[128 * t : 128 * t + 128, :] = real
        out[128 * (tiles + t) : 128 * (tiles + t) + 128, :] = imag
    out[256 * tiles :, :] = jnp.zeros((8, 128), F32)
    out[256 * tiles : 256 * tiles + tiles, :] = lax.rem(start, RB).astype(F32)
    out[256 * tiles + 7 :, :] = lax.rem(lax.div(start[:1, :], RB), 2).astype(F32)


def pack(pupils, starts, counts, weights, total_blocks):
    slots = pupils.shape[0]
    return pl.pallas_call(
        partial(pack_kernel, total_blocks),
        out_shape=jax.ShapeDtypeStruct((2 * slots + 8, 128), F32),
        in_specs=[pl.BlockSpec(memory_space=pl.ANY)] * 4,
        out_specs=VMEM,
        scratch_shapes=[
            pltpu.VMEM((2 * slots, 128), F32),
            pltpu.VMEM((slots // 128, 128), jnp.int32),
            pltpu.VMEM((slots // 128, 128), jnp.int32),
            pltpu.VMEM((slots // 128, 128), F32),
            pltpu.SemaphoreType.DMA((4,)),
        ],
        compiler_params=PARAMS,
        name="pack",
    )(
        *(
            pltpu.with_memory_space_constraint(x, pltpu.HBM)
            for x in (
                pupils.reshape(2 * slots, 128),
                starts.reshape(-1, 128),
                counts.reshape(-1, 128),
                weights.reshape(-1, 128),
            )
        )
    )


def factors(chunk):
    count = (chunk.shape[0] - 8) // 2
    real = chunk[:count, :]
    imag = chunk[count : 2 * count, :]
    left = jnp.concatenate([real.T, imag.T], axis=1).astype(BF16)
    right = []
    for scale, real, imag in zip((0.5, 1.0), split(real), split(imag)):
        right.append(
            jnp.concatenate(
                [
                    jnp.concatenate([real, -imag], axis=1),
                    jnp.concatenate([imag, real], axis=1),
                ],
                axis=0,
            )
            * jnp.asarray(scale, BF16)
        )
    places = [chunk[2 * count + t : 2 * count + t + 1, :] for t in range(count // 128)]
    place = jnp.broadcast_to(jnp.concatenate(places + places, axis=1), (16, 2 * count))
    return left, right[0], right[1], place


def at_block(part, place, b):
    mask = jnp.where(place == b, 1.0, 0.0).astype(BF16)[None]
    return (part.reshape(8, 16, -1) * mask).reshape(part.shape)


def hermitian(q):
    real, imag = q[:, :128], q[:, 128:]
    return jnp.concatenate([real + real.T, imag - imag.T], axis=1)


def build_kernel(add, last, chunk, *refs):
    refs = list(refs)
    before = refs.pop(0) if add else None
    lhs = refs.pop()
    left, right_hi, right_lo, place = factors(chunk)

    def one_group(g, carry):
        for j in range(GROUP):
            b = (g * GROUP + j).astype(F32)
            lhs[j * 128 : (j + 1) * 128, :] = at_block(left, place, b)
        at = pl.ds(pl.multiple_of(g * GROUP * 128, GROUP * 128), GROUP * 128)
        hi = lhs[...]
        total = dot(hi, right_hi) + dot(hi, right_lo)
        if add:
            total = before[at, :] + total
        if last:
            for j in range(GROUP):
                one = pl.ds(pl.multiple_of((g * GROUP + j) * 128, 128), 128)
                refs[0][one, :], refs[1][one, :] = split(
                    hermitian(total[j * 128 : (j + 1) * 128, :])
                )
        else:
            refs[0][at, :] = total
        return carry

    lax.fori_loop(0, RB // GROUP, one_group, 0, unroll=RB // GROUP)


def build(chunk, before, last=False):
    count = (chunk.shape[0] - 8) // 2
    add = before is not None
    shape = (RB * 128, 256)
    out = [jax.ShapeDtypeStruct(shape, BF16)] * 2 if last else [jax.ShapeDtypeStruct(shape, F32)]
    result = pl.pallas_call(
        partial(build_kernel, add, last),
        out_shape=out,
        in_specs=[VMEM] * (1 + add),
        out_specs=[VMEM] * len(out),
        scratch_shapes=[pltpu.VMEM((GROUP * 128, 2 * count), BF16)],
        input_output_aliases={1: 0} if add and not last else {},
        compiler_params=PARAMS,
        cost_estimate=pl.CostEstimate(
            flops=1 << 20, bytes_accessed=1 << 16, transcendentals=0
        ),
        name="band_terms",
    )(chunk, *([before] if add else []))
    return result if last else result[0]


def wide(parts):
    return jnp.concatenate([parts[0], parts[1]], axis=1)


def real_form(rows):
    return jnp.concatenate(
        [rows, jnp.concatenate([-rows[:, M:], rows[:, :M]], axis=1)], axis=0
    )


def times(g_hi, g_lo, hi, lo):
    hi, lo = real_form(hi), real_form(lo)
    return dot(g_hi, hi) + dot(g_hi, lo) + dot(g_lo, hi)


def gram_of(hi, lo):
    half = jnp.asarray(0.5, BF16)
    q = 0.0
    for cols in (slice(0, M), slice(M, 2 * M)):
        q += dot_t(hi[:, cols], jnp.concatenate([hi[:, cols] * half, lo[:, cols]], axis=1))
    q = q[:, :M] + q[:, M:]
    return q + q.T


def in_odd_region(chunk):
    row = chunk[chunk.shape[0] - 1 :, :]
    return jnp.concatenate([row, row], axis=1) == 1.0


def edge_kernel(chunk, before, x, first_out, second_out):
    left, right_hi, right_lo, place = factors(chunk)
    blocks = (0, RB - 2, RB - 1)
    left = jnp.concatenate([at_block(left, place, float(b)) for b in blocks], axis=0)
    total = dot(left, right_hi) + dot(left, right_lo)
    head, next_last, last = [
        hermitian(before[b * 128 : (b + 1) * 128, :] + total[i * 128 : (i + 1) * 128, :])
        for i, b in enumerate(blocks)
    ]
    size = x.shape[1]
    start = wide(x[:, : 2 * BLOCK, :])
    stop = wide(x[:, size - 2 * BLOCK :, :])
    held = jnp.concatenate([stop[BLOCK:], jnp.zeros((BLOCK, 256), F32)], axis=0)
    own = times(*split(last), *split(held))
    to_after = jnp.concatenate(
        [
            own[:BLOCK] + times(*split(next_last[BLOCK:]), *split(stop)),
            own[BLOCK:],
            last[BLOCK:],
        ],
        axis=0,
    )
    to_before = jnp.concatenate(
        [times(*split(head[:BLOCK]), *split(start)), start[:BLOCK], jnp.zeros((BLOCK, 256), F32)],
        axis=0,
    )
    is_odd = in_odd_region(chunk)
    first_out[...] = jnp.where(is_odd, to_after, to_before)
    second_out[...] = jnp.where(is_odd, to_before, to_after)


def build_edges(chunk, before, x):
    shape = jax.ShapeDtypeStruct((3 * BLOCK, 256), F32)
    return pl.pallas_call(
        edge_kernel,
        out_shape=(shape, shape),
        in_specs=[VMEM] * 3,
        out_specs=(VMEM, VMEM),
        compiler_params=PARAMS,
        name="edge_terms",
    )(chunk, before, x)


def prepare_kernel(x, hi_out, lo_out):
    for i in range(0, x.shape[1], 256):
        hi_out[i : i + 256, :], lo_out[i : i + 256, :] = split(wide(x[:, i : i + 256, :]))


def prepare(x):
    shape = jax.ShapeDtypeStruct((x.shape[1], 256), BF16)
    return pl.pallas_call(
        prepare_kernel,
        out_shape=(shape, shape),
        in_specs=[VMEM],
        out_specs=(VMEM, VMEM),
        compiler_params=PARAMS,
        cost_estimate=pl.CostEstimate(flops=1 << 20, bytes_accessed=4 << 20, transcendentals=0),
        name="prepare",
    )(x)


def join(a, b):
    return jnp.concatenate([a, b], axis=0)


def put(hi, lo, e, block):
    at = pl.ds(pl.multiple_of(e * BLOCK, BLOCK), BLOCK)
    hi[at, :], lo[at, :] = split(block)


def first_kernel(g_hi, g_lo, x_hi, x_lo, p_hi, p_lo, ends):
    rows = RB * BLOCK
    nothing = jnp.zeros((BLOCK, 256), BF16)

    def pair(b):
        at = pl.ds(pl.multiple_of(b * 128, 128), 128)
        win = pl.ds(pl.multiple_of(b * BLOCK, BLOCK), 128)
        return times(g_hi[at, :], g_lo[at, :], x_hi[win, :], x_lo[win, :])

    def one(b, carry):
        spill, top = carry
        both = pair(b)
        block = both[:BLOCK] + spill
        put(p_hi, p_lo, b + 1, block)
        return both[BLOCK:], jnp.maximum(top, jnp.abs(block))

    both = pair(0)
    ends[:BLOCK, :] = both[:BLOCK]
    carry = both[BLOCK:], jnp.zeros((BLOCK, 256), F32)
    spill, top = lax.fori_loop(1, RB - 1, one, carry, unroll=RB - 2)
    both = times(
        g_hi[(RB - 1) * 128 :, :],
        g_lo[(RB - 1) * 128 :, :],
        join(x_hi[rows - BLOCK :, :], nothing),
        join(x_lo[rows - BLOCK :, :], nothing),
    )
    ends[BLOCK : 2 * BLOCK, :] = both[:BLOCK] + spill
    ends[2 * BLOCK : 3 * BLOCK, :] = both[BLOCK:]
    ends[3 * BLOCK :, :] = jnp.broadcast_to(jnp.max(top, axis=0, keepdims=True), (8, 256))


def first_product(g_hi, g_lo, x_hi, x_lo):
    shape = jax.ShapeDtypeStruct(((RB + 2) * BLOCK, 256), BF16)
    return pl.pallas_call(
        first_kernel,
        out_shape=(shape, shape, jax.ShapeDtypeStruct((3 * BLOCK + 8, 256), F32)),
        in_specs=[VMEM] * 4,
        out_specs=(VMEM, VMEM, VMEM),
        compiler_params=PARAMS,
        cost_estimate=pl.CostEstimate(flops=1 << 20, bytes_accessed=1 << 16, transcendentals=0),
        name="first_product",
    )(g_hi, g_lo, x_hi, x_lo)


def second_kernel(own, g_hi, g_lo, swap_1, swap_2, x_hi, x_lo, ends, p_hi_in, p_lo_in,
                  z_hi, z_lo, grams, p_hi, p_lo):
    rows = RB * BLOCK
    is_odd = in_odd_region(own)
    left = jnp.where(is_odd, swap_2[...], swap_1[...])
    right = jnp.where(is_odd, swap_1[...], swap_2[...])
    into = left[2 * BLOCK :]
    into_hi, into_lo = split(into)
    none = jnp.zeros((BLOCK, 128), F32)
    out_of = [jnp.concatenate([none, part], axis=0).T[:BLOCK] for part in (into[:, :M], into[:, M:])]
    out_hi, out_lo = split(jnp.concatenate([out_of[0], -out_of[1]], axis=1))
    tail = split(right[BLOCK : 2 * BLOCK])
    nothing = jnp.zeros((BLOCK, 256), BF16)
    both = times(
        join(out_hi, into_hi),
        join(out_lo, into_lo),
        join(nothing, x_hi[:BLOCK, :]),
        join(nothing, x_lo[:BLOCK, :]),
    ) + left[: 2 * BLOCK]
    after = times(
        g_hi[(RB - 1) * 128 :, :],
        g_lo[(RB - 1) * 128 :, :],
        join(nothing, tail[0]),
        join(nothing, tail[1]),
    )
    top = ends[3 * BLOCK : 3 * BLOCK + 1, :]
    for e, block in (
        (0, both[:BLOCK]),
        (1, both[BLOCK:] + ends[:BLOCK, :]),
        (RB, after[:BLOCK] + ends[BLOCK : 2 * BLOCK, :]),
        (RB + 1, after[BLOCK:] + ends[2 * BLOCK : 3 * BLOCK, :] + right[:BLOCK]),
    ):
        put(p_hi, p_lo, e, block)
        top = jnp.maximum(top, jnp.max(jnp.abs(block), axis=0, keepdims=True))
    top = jnp.maximum(top[:, :M], top[:, M:])
    scale = jnp.where(top > 0, 1.0 / jnp.where(top > 0, top, 1.0), 0.0)
    scale = jnp.concatenate([scale, scale], axis=1)

    inner = pl.ds(BLOCK, rows)
    gram_1 = gram_of(p_hi[inner, :], p_lo[inner, :])

    def second(b, spill):
        at = pl.ds(pl.multiple_of(b * 128, 128), 128)
        win = pl.ds(pl.multiple_of((b + 1) * BLOCK, BLOCK), 128)
        both = times(g_hi[at, :], g_lo[at, :], p_hi[win, :], p_lo[win, :])
        out = pl.ds(pl.multiple_of(b * BLOCK, BLOCK), BLOCK)
        z_hi[out, :], z_lo[out, :] = split((both[:BLOCK] + spill) * scale)
        return both[BLOCK:]

    spill = times(into_hi, into_lo, p_hi[:128, :], p_lo[:128, :])
    lax.fori_loop(0, RB, second, spill, unroll=RB)
    gram_2 = gram_of(z_hi[...], z_lo[...])
    row = lax.broadcasted_iota(jnp.int32, (M, M), 0)
    col = lax.broadcasted_iota(jnp.int32, (M, M), 1)
    grams[:M, :] = jnp.where(row >= col, gram_1, gram_2)
    diagonal = jnp.sum(jnp.where(row == col, gram_2, 0.0), axis=0, keepdims=True)
    grams[M:, :] = jnp.concatenate([diagonal, top, jnp.zeros((6, M), F32)], axis=0)


def second_product(own, g_hi, g_lo, swap_1, swap_2, x_hi, x_lo, ends, p_hi, p_lo):
    part = jax.ShapeDtypeStruct((RB * BLOCK, 256), BF16)
    whole = jax.ShapeDtypeStruct(p_hi.shape, BF16)
    return pl.pallas_call(
        second_kernel,
        out_shape=(part, part, jax.ShapeDtypeStruct((M + 8, M), F32), whole, whole),
        in_specs=[VMEM] * 10,
        out_specs=(VMEM,) * 5,
        input_output_aliases={8: 3, 9: 4},
        compiler_params=PARAMS,
        cost_estimate=pl.CostEstimate(
            flops=6 * RB * 128 * 256 * 256, bytes_accessed=8 << 20, transcendentals=0
        ),
        name="second_product",
    )(own, g_hi, g_lo, swap_1, swap_2, x_hi, x_lo, ends, p_hi, p_lo)[:3]


def inverse_factor(a, work):
    row = lax.broadcasted_iota(jnp.int32, (M, M), 0)
    col = lax.broadcasted_iota(jnp.int32, (M, M), 1)
    work[:, :M] = a
    work[:, M:] = jnp.where(row == col, 1.0, 0.0)
    sub = lax.broadcasted_iota(jnp.int32, (8, M), 0)
    groups = OUTER // 8

    def line(x, j):
        return x[j : j + 1, :]

    def tall(x, j):
        return jnp.broadcast_to(line(x, j), (8, M))

    def spread(x, at):
        return [jnp.broadcast_to(x[:, at + k : at + k + 1], (8, M)) for k in range(8)]

    for top in range(0, M, OUTER):
        left = [work[top + 8 * g : top + 8 * g + 8, :M] for g in range(groups)]
        right = [work[top + 8 * g : top + 8 * g + 8, M:] for g in range(groups)]
        ahead = spread(left[0], top)
        for q in range(groups):
            at = top + 8 * q
            cols = {q: ahead, **{g: spread(left[g], at) for g in range(q + 1, groups)}}
            more = q + 1 < groups
            if more:
                ahead, mine = spread(left[q + 1], at + 8), spread(left[q], at + 8)
            scales = jnp.zeros((8, M), F32)
            for j in range(0, 8, 2):
                a0, a1, a2 = tall(cols[q][j], j), tall(cols[q][j], j + 1), tall(cols[q][j + 1], j + 1)
                det = a0 * a2 - a1 * a1
                inverse = pltpu.reciprocal(det, approx=False)
                root = lax.rsqrt(a0)
                ratio = a1 * (root * root)
                scales = jnp.where(sub == j, root, scales)
                scales = jnp.where(sub == j + 1, lax.rsqrt(det) * (a0 * root), scales)
                row_0 = [line(cols[q][k], j) for k in range(8)]
                row_1 = [line(cols[q][k], j + 1) for k in range(8)]
                left_0, left_1 = line(left[q], j), line(left[q], j + 1)
                right_0, right_1 = line(right[q], j), line(right[q], j + 1)
                if more:
                    mine_0 = [line(x, j) for x in mine]
                    mine_1 = [line(x, j + 1) for x in mine]
                for g in range(q, groups):
                    c0, c1 = cols[g][j], cols[g][j + 1]
                    y0 = a2 * c0 - a1 * c1
                    y1 = a0 * c1 - a1 * c0
                    if g == q:
                        y0 = jnp.where(sub > j + 1, y0, 0.0)
                        y1 = jnp.where(sub > j + 1, y1, 0.0)
                    for k in range(j + 2, 8):
                        cols[g][k] = cols[g][k] - (y0 * row_0[k] + y1 * row_1[k]) * inverse
                    x0, x1 = y0 * inverse, y1 * inverse
                    if g == q:
                        x0 = jnp.where(sub == j + 1, ratio, x0)
                    left[g] = left[g] - (x0 * left_0 + x1 * left_1)
                    right[g] = right[g] - (x0 * right_0 + x1 * right_1)
                    if more and g <= q + 1:
                        part = mine if g == q else ahead
                        for k in range(8):
                            part[k] = part[k] - (x0 * mine_0[k] + x1 * mine_1[k])
            left[q] = left[q] * scales
            right[q] = right[q] * scales
        for g in range(groups):
            work[top + 8 * g : top + 8 * g + 8, :M] = left[g]
            work[top + 8 * g : top + 8 * g + 8, M:] = right[g]
        if top + OUTER < M:
            panel = work[top : top + OUTER, :]
            update = lax.dot_general(
                panel[:, :M], panel, (((0,), (0,)), ((), ())),
                precision=HIGHEST, preferred_element_type=F32,
            )
            work[top + OUTER :, :] = work[top + OUTER :, :] - update[top + OUTER :, :]
    return work[:, M:]


def finish_kernel(total_rows, *refs):
    grams, (z_hi, z_lo, out, work) = refs[:-4], refs[-4:]
    own = grams[0]
    row = lax.broadcasted_iota(jnp.int32, (M, M), 0)
    col = lax.broadcasted_iota(jnp.int32, (M, M), 1)
    eye = jnp.where(row == col, 1.0, 0.0)

    def as_column(v):
        return jnp.sum(eye * v, axis=1, keepdims=True)

    def row_of(x):
        return jnp.sum(eye * x, axis=0, keepdims=True)

    total = own[:M, :]
    for one in grams[1:]:
        total = total + one[:M, :]
    gram = jnp.where(row >= col, total, total.T)
    norm = lax.rsqrt(row_of(gram))
    inverse = inverse_factor(gram * norm * as_column(norm), work)
    total = jnp.zeros((M, M), F32)
    for one in grams:
        size = norm * one[M + 1 : M + 2, :]
        second = jnp.where(row == col, one[M : M + 1, :], one[:M, :])
        total = total + second * size * as_column(size)
    gram = jnp.where(row <= col, total, total.T)
    gram = dot_f32(dot_f32(inverse, gram), inverse.T)
    scale = lax.rsqrt(row_of(gram))
    second = inverse_factor(gram * scale * as_column(scale), work) * scale
    inverse = dot_f32(second, inverse)
    change = (inverse * (norm * own[M + 1 : M + 2, :] * (total_rows**0.5))).T
    c_hi, c_lo = split(change)
    right = jnp.concatenate(
        [
            jnp.concatenate([c_hi, c_lo], axis=1),
            jnp.concatenate([c_hi, jnp.zeros_like(c_lo)], axis=1),
        ],
        axis=0,
    )
    step = 256

    def rows_of(i, carry):
        at = pl.ds(pl.multiple_of(i * step, step), step)
        hi, lo = z_hi[at, :], z_lo[at, :]
        for part in range(2):
            cols = slice(part * M, part * M + M)
            both = dot(jnp.concatenate([hi[:, cols], lo[:, cols]], axis=1), right)
            out[part, at, :] = both[:, :M] + both[:, M:]
        return carry

    lax.fori_loop(0, z_hi.shape[0] // step, rows_of, 0, unroll=True)


def finish(grams, z_hi, z_lo, total_rows):
    return pl.pallas_call(
        partial(finish_kernel, total_rows),
        out_shape=jax.ShapeDtypeStruct((2, z_hi.shape[0], M), F32),
        in_specs=[VMEM] * (len(grams) + 2),
        out_specs=VMEM,
        scratch_shapes=[pltpu.VMEM((M, 2 * M), F32)],
        compiler_params=PARAMS,
        name="finish",
    )(*grams, z_hi, z_lo)


def neighbours(x, begin):
    pairs = [(i, i + 1) for i in range(begin, lax.axis_size("blk") - 1, 2)]
    return lax.ppermute(x, "blk", pairs + [(j, i) for i, j in pairs])


def swapped(x, far, axis="src"):
    return lax.ppermute(x, axis, [(i, i ^ far) for i in range(lax.axis_size(axis))])


def gathered(own, ready, axis="src"):
    peers = lax.axis_size(axis)
    if peers & (peers - 1):
        chunks = [
            lax.ppermute(own, axis, [(i, (i + k) % peers) for i in range(peers)])
            for k in range(1, peers)
        ]
        return chunks, ready
    far = peers // 2
    chunks = []
    while far:
        if chunks and ready:
            chunks, ready = lax.optimization_barrier((chunks, ready))
        chunks = chunks + [swapped(c, far, axis) for c in [own] + chunks]
        far //= 2
    return chunks, ready


def per_device(pupils, starts, counts, weights, start_block):
    regions = lax.axis_size("blk")
    size = start_block.shape[1]

    own = pack(pupils, starts, counts, weights, regions * RB)
    ready = (build(own, None), *prepare(start_block))
    chunks, ready = gathered(own, ready)
    band, x_hi, x_lo = ready
    for chunk in chunks[:-1]:
        band = build(chunk, band)
    swap_1, swap_2 = build_edges(chunks[-1], band, start_block)
    swap_2 = neighbours(swap_2, 0)
    swap_1 = neighbours(swap_1, 1)
    g_hi, g_lo = build(chunks[-1], band, last=True)
    p_hi, p_lo, ends = first_product(g_hi, g_lo, x_hi, x_lo)
    z_hi, z_lo, grams = second_product(
        own, g_hi, g_lo, swap_1, swap_2, x_hi, x_lo, ends, p_hi, p_lo
    )
    grams = [grams] + gathered(grams, (), "blk")[0]
    return finish(grams, z_hi, z_lo, 2.0 * size * regions)


def solution(mesh):
    placed = (
        P(("groups", "src", "blk"), None, None),
        P(("groups", "src", "blk")),
        P(("groups", "src", "blk")),
        P(("groups", "src", "blk")),
        P("groups", "blk", None),
    )
    return jax.shard_map(
        per_device, mesh=mesh, in_specs=placed, out_specs=P("groups", "blk", None), check_vma=False
    )
```

```python
from functools import partial

import jax
import jax.numpy as jnp
from jax import lax
from jax.experimental import pallas as pl
from jax.experimental.pallas import tpu as pltpu
from jax.sharding import PartitionSpec as P

BLOCK = 64
RB = 32
GROUP = 2
OUTER = 64
STEP = 256
M = 128
F32 = jnp.float32
BF16 = jnp.bfloat16
HIGHEST = lax.Precision.HIGHEST
VMEM = pl.BlockSpec(memory_space=pltpu.VMEM)
PARAMS = pltpu.CompilerParams(vmem_limit_bytes=16 * 1024 * 1024)


def split(x):
    hi = x.astype(BF16)
    return hi, (x - hi.astype(F32)).astype(BF16)


def dot(a, b):
    return jnp.dot(a, b, preferred_element_type=F32)


def dot_t(a, b):
    return lax.dot_general(a, b, (((0,), (0,)), ((), ())), preferred_element_type=F32)


def dot_f32(a, b):
    return jnp.dot(a, b, precision=HIGHEST, preferred_element_type=F32)


def pack_kernel(total_blocks, *refs):
    sent, out, held, sems = refs[:4], refs[4], refs[5:9], refs[9]
    copies = [pltpu.make_async_copy(sent[i], held[i], sems.at[i]) for i in range(4)]
    for copy in copies:
        copy.start()
    for copy in copies:
        copy.wait()
    pupils, starts, counts, weights = held
    tiles = starts.shape[0]
    lane = lax.broadcasted_iota(jnp.int32, (128, 2 * BLOCK), 1)
    start = starts[...]
    root = jnp.sqrt(weights[...])
    first_live = jnp.where(counts[...] > 0, root, 0.0)
    second_live = jnp.where((counts[...] > 1) & (start + 1 < total_blocks), root, 0.0)
    for t in range(tiles):
        first_column = jnp.broadcast_to(first_live[t : t + 1, :], (128, 128)).T
        second_column = jnp.broadcast_to(second_live[t : t + 1, :], (128, 128)).T
        first = pupils[pl.ds(256 * t, 128, stride=2), :] * first_column
        second = pupils[pl.ds(256 * t + 1, 128, stride=2), :] * second_column
        real = jnp.where(lane < BLOCK, first, pltpu.roll(second, BLOCK, 1))
        imag = jnp.where(lane < BLOCK, pltpu.roll(first, BLOCK, 1), second)
        out[128 * t : 128 * t + 128, :] = real
        out[128 * (tiles + t) : 128 * (tiles + t) + 128, :] = imag
    out[256 * tiles :, :] = jnp.zeros((8, 128), F32)
    out[256 * tiles : 256 * tiles + tiles, :] = lax.rem(start, RB).astype(F32)
    out[256 * tiles + 7 :, :] = lax.rem(lax.div(start[:1, :], RB), 2).astype(F32)


def pack(pupils, starts, counts, weights, total_blocks):
    slots = pupils.shape[0]
    return pl.pallas_call(
        partial(pack_kernel, total_blocks),
        out_shape=jax.ShapeDtypeStruct((2 * slots + 8, 128), F32),
        in_specs=[pl.BlockSpec(memory_space=pl.ANY)] * 4,
        out_specs=VMEM,
        scratch_shapes=[
            pltpu.VMEM((2 * slots, 128), F32),
            pltpu.VMEM((slots // 128, 128), jnp.int32),
            pltpu.VMEM((slots // 128, 128), jnp.int32),
            pltpu.VMEM((slots // 128, 128), F32),
            pltpu.SemaphoreType.DMA((4,)),
        ],
        compiler_params=PARAMS,
        name="pack",
    )(
        *(
            pltpu.with_memory_space_constraint(x, pltpu.HBM)
            for x in (
                pupils.reshape(2 * slots, 128),
                starts.reshape(-1, 128),
                counts.reshape(-1, 128),
                weights.reshape(-1, 128),
            )
        )
    )


def factors(chunk):
    count = (chunk.shape[0] - 8) // 2
    real = chunk[:count, :]
    imag = chunk[count : 2 * count, :]
    left = jnp.concatenate([real.T, imag.T], axis=1).astype(BF16)
    right = []
    for scale, real, imag in zip((0.5, 1.0), split(real), split(imag)):
        right.append(
            jnp.concatenate(
                [
                    jnp.concatenate([real, -imag], axis=1),
                    jnp.concatenate([imag, real], axis=1),
                ],
                axis=0,
            )
            * jnp.asarray(scale, BF16)
        )
    places = [chunk[2 * count + t : 2 * count + t + 1, :] for t in range(count // 128)]
    place = jnp.broadcast_to(jnp.concatenate(places + places, axis=1), (16, 2 * count))
    return left, right[0], right[1], place


def at_block(part, place, b):
    mask = jnp.where(place == b, 1.0, 0.0).astype(BF16)[None]
    return (part.reshape(8, 16, -1) * mask).reshape(part.shape)


def hermitian(q):
    real, imag = q[:, :128], q[:, 128:]
    return jnp.concatenate([real + real.T, imag - imag.T], axis=1)


def build_kernel(add, last, chunk, *refs):
    refs = list(refs)
    before = refs.pop(0) if add else None
    lhs = refs.pop()
    left, right_hi, right_lo, place = factors(chunk)

    def one_group(g, carry):
        for j in range(GROUP):
            b = (g * GROUP + j).astype(F32)
            lhs[j * 128 : (j + 1) * 128, :] = at_block(left, place, b)
        at = pl.ds(pl.multiple_of(g * GROUP * 128, GROUP * 128), GROUP * 128)
        hi = lhs[...]
        total = dot(hi, right_hi) + dot(hi, right_lo)
        if add:
            total = before[at, :] + total
        if last:
            for j in range(GROUP):
                one = pl.ds(pl.multiple_of((g * GROUP + j) * 128, 128), 128)
                refs[0][one, :], refs[1][one, :] = split(
                    hermitian(total[j * 128 : (j + 1) * 128, :])
                )
        else:
            refs[0][at, :] = total
        return carry

    lax.fori_loop(0, RB // GROUP, one_group, 0, unroll=RB // GROUP)


def build(chunk, before, last=False):
    count = (chunk.shape[0] - 8) // 2
    add = before is not None
    shape = (RB * 128, 256)
    out = [jax.ShapeDtypeStruct(shape, BF16)] * 2 if last else [jax.ShapeDtypeStruct(shape, F32)]
    result = pl.pallas_call(
        partial(build_kernel, add, last),
        out_shape=out,
        in_specs=[VMEM] * (1 + add),
        out_specs=[VMEM] * len(out),
        scratch_shapes=[pltpu.VMEM((GROUP * 128, 2 * count), BF16)],
        input_output_aliases={1: 0} if add and not last else {},
        compiler_params=PARAMS,
        cost_estimate=pl.CostEstimate(
            flops=1 << 20, bytes_accessed=1 << 16, transcendentals=0
        ),
        name="band_terms",
    )(chunk, *([before] if add else []))
    return result if last else result[0]


def wide(parts):
    return jnp.concatenate([parts[0], parts[1]], axis=1)


def real_form(rows):
    return jnp.concatenate(
        [rows, jnp.concatenate([-rows[:, M:], rows[:, :M]], axis=1)], axis=0
    )


def times(g_hi, g_lo, hi, lo):
    hi, lo = real_form(hi), real_form(lo)
    return dot(g_hi, hi) + dot(g_hi, lo) + dot(g_lo, hi)


def gram_of(hi, lo):
    half = jnp.asarray(0.5, BF16)
    q = 0.0
    for cols in (slice(0, M), slice(M, 2 * M)):
        q += dot_t(hi[:, cols], jnp.concatenate([hi[:, cols] * half, lo[:, cols]], axis=1))
    q = q[:, :M] + q[:, M:]
    return q + q.T


def in_odd_region(chunk):
    row = chunk[chunk.shape[0] - 1 :, :]
    return jnp.concatenate([row, row], axis=1) == 1.0


def edge_kernel(chunk, before, x, first_out, second_out):
    left, right_hi, right_lo, place = factors(chunk)
    blocks = (0, RB - 2, RB - 1)
    left = jnp.concatenate([at_block(left, place, float(b)) for b in blocks], axis=0)
    total = dot(left, right_hi) + dot(left, right_lo)
    head, next_last, last = [
        hermitian(before[b * 128 : (b + 1) * 128, :] + total[i * 128 : (i + 1) * 128, :])
        for i, b in enumerate(blocks)
    ]
    size = x.shape[1]
    start = wide(x[:, : 2 * BLOCK, :])
    stop = wide(x[:, size - 2 * BLOCK :, :])
    held = jnp.concatenate([stop[BLOCK:], jnp.zeros((BLOCK, 256), F32)], axis=0)
    own = times(*split(last), *split(held))
    to_after = jnp.concatenate(
        [
            own[:BLOCK] + times(*split(next_last[BLOCK:]), *split(stop)),
            own[BLOCK:],
            last[BLOCK:],
        ],
        axis=0,
    )
    to_before = jnp.concatenate(
        [times(*split(head[:BLOCK]), *split(start)), start[:BLOCK], jnp.zeros((BLOCK, 256), F32)],
        axis=0,
    )
    is_odd = in_odd_region(chunk)
    first_out[...] = jnp.where(is_odd, to_after, to_before)
    second_out[...] = jnp.where(is_odd, to_before, to_after)


def build_edges(chunk, before, x):
    shape = jax.ShapeDtypeStruct((3 * BLOCK, 256), F32)
    return pl.pallas_call(
        edge_kernel,
        out_shape=(shape, shape),
        in_specs=[VMEM] * 3,
        out_specs=(VMEM, VMEM),
        compiler_params=PARAMS,
        name="edge_terms",
    )(chunk, before, x)


def prepare_kernel(x, hi_out, lo_out):
    for i in range(0, x.shape[1], 256):
        hi_out[i : i + 256, :], lo_out[i : i + 256, :] = split(wide(x[:, i : i + 256, :]))


def prepare(x):
    shape = jax.ShapeDtypeStruct((x.shape[1], 256), BF16)
    return pl.pallas_call(
        prepare_kernel,
        out_shape=(shape, shape),
        in_specs=[VMEM],
        out_specs=(VMEM, VMEM),
        compiler_params=PARAMS,
        cost_estimate=pl.CostEstimate(flops=1 << 20, bytes_accessed=4 << 20, transcendentals=0),
        name="prepare",
    )(x)


def join(a, b):
    return jnp.concatenate([a, b], axis=0)


def put(hi, lo, e, block):
    at = pl.ds(pl.multiple_of(e * BLOCK, BLOCK), BLOCK)
    hi[at, :], lo[at, :] = split(block)


def first_kernel(g_hi, g_lo, x_hi, x_lo, p_hi, p_lo, ends):
    rows = RB * BLOCK
    nothing = jnp.zeros((BLOCK, 256), BF16)

    def pair(b):
        at = pl.ds(pl.multiple_of(b * 128, 128), 128)
        win = pl.ds(pl.multiple_of(b * BLOCK, BLOCK), 128)
        return times(g_hi[at, :], g_lo[at, :], x_hi[win, :], x_lo[win, :])

    def one(b, carry):
        spill, top = carry
        both = pair(b)
        block = both[:BLOCK] + spill
        put(p_hi, p_lo, b + 1, block)
        return both[BLOCK:], jnp.maximum(top, jnp.abs(block))

    both = pair(0)
    ends[:BLOCK, :] = both[:BLOCK]
    carry = both[BLOCK:], jnp.zeros((BLOCK, 256), F32)
    spill, top = lax.fori_loop(1, RB - 1, one, carry, unroll=RB - 2)
    both = times(
        g_hi[(RB - 1) * 128 :, :],
        g_lo[(RB - 1) * 128 :, :],
        join(x_hi[rows - BLOCK :, :], nothing),
        join(x_lo[rows - BLOCK :, :], nothing),
    )
    ends[BLOCK : 2 * BLOCK, :] = both[:BLOCK] + spill
    ends[2 * BLOCK : 3 * BLOCK, :] = both[BLOCK:]
    ends[3 * BLOCK :, :] = jnp.broadcast_to(jnp.max(top, axis=0, keepdims=True), (8, 256))


def first_product(g_hi, g_lo, x_hi, x_lo):
    shape = jax.ShapeDtypeStruct(((RB + 2) * BLOCK, 256), BF16)
    return pl.pallas_call(
        first_kernel,
        out_shape=(shape, shape, jax.ShapeDtypeStruct((3 * BLOCK + 8, 256), F32)),
        in_specs=[VMEM] * 4,
        out_specs=(VMEM, VMEM, VMEM),
        compiler_params=PARAMS,
        cost_estimate=pl.CostEstimate(flops=1 << 20, bytes_accessed=1 << 16, transcendentals=0),
        name="first_product",
    )(g_hi, g_lo, x_hi, x_lo)


def second_kernel(own, g_hi, g_lo, swap_1, swap_2, x_hi, x_lo, ends, p_hi_in, p_lo_in,
                  z_hi, z_lo, grams, p_hi, p_lo):
    rows = RB * BLOCK
    is_odd = in_odd_region(own)
    left = jnp.where(is_odd, swap_2[...], swap_1[...])
    right = jnp.where(is_odd, swap_1[...], swap_2[...])
    into = left[2 * BLOCK :]
    into_hi, into_lo = split(into)
    none = jnp.zeros((BLOCK, 128), F32)
    out_of = [jnp.concatenate([none, part], axis=0).T[:BLOCK] for part in (into[:, :M], into[:, M:])]
    out_hi, out_lo = split(jnp.concatenate([out_of[0], -out_of[1]], axis=1))
    tail = split(right[BLOCK : 2 * BLOCK])
    nothing = jnp.zeros((BLOCK, 256), BF16)
    both = times(
        join(out_hi, into_hi),
        join(out_lo, into_lo),
        join(nothing, x_hi[:BLOCK, :]),
        join(nothing, x_lo[:BLOCK, :]),
    ) + left[: 2 * BLOCK]
    after = times(
        g_hi[(RB - 1) * 128 :, :],
        g_lo[(RB - 1) * 128 :, :],
        join(nothing, tail[0]),
        join(nothing, tail[1]),
    )
    top = ends[3 * BLOCK : 3 * BLOCK + 1, :]
    for e, block in (
        (0, both[:BLOCK]),
        (1, both[BLOCK:] + ends[:BLOCK, :]),
        (RB, after[:BLOCK] + ends[BLOCK : 2 * BLOCK, :]),
        (RB + 1, after[BLOCK:] + ends[2 * BLOCK : 3 * BLOCK, :] + right[:BLOCK]),
    ):
        put(p_hi, p_lo, e, block)
        top = jnp.maximum(top, jnp.max(jnp.abs(block), axis=0, keepdims=True))
    top = jnp.maximum(top[:, :M], top[:, M:])
    scale = jnp.where(top > 0, 1.0 / jnp.where(top > 0, top, 1.0), 0.0)
    scale = jnp.concatenate([scale, scale], axis=1)

    inner = pl.ds(BLOCK, rows)
    gram_1 = gram_of(p_hi[inner, :], p_lo[inner, :])

    def second(b, spill):
        at = pl.ds(pl.multiple_of(b * 128, 128), 128)
        win = pl.ds(pl.multiple_of((b + 1) * BLOCK, BLOCK), 128)
        both = times(g_hi[at, :], g_lo[at, :], p_hi[win, :], p_lo[win, :])
        out = pl.ds(pl.multiple_of(b * BLOCK, BLOCK), BLOCK)
        z_hi[out, :], z_lo[out, :] = split((both[:BLOCK] + spill) * scale)
        return both[BLOCK:]

    spill = times(into_hi, into_lo, p_hi[:128, :], p_lo[:128, :])
    lax.fori_loop(0, RB, second, spill, unroll=RB)
    gram_2 = gram_of(z_hi[...], z_lo[...])
    row = lax.broadcasted_iota(jnp.int32, (M, M), 0)
    col = lax.broadcasted_iota(jnp.int32, (M, M), 1)
    grams[:M, :] = jnp.where(row >= col, gram_1, gram_2)
    diagonal = jnp.sum(jnp.where(row == col, gram_2, 0.0), axis=0, keepdims=True)
    grams[M:, :] = jnp.concatenate([diagonal, top, jnp.zeros((6, M), F32)], axis=0)


def second_product(own, g_hi, g_lo, swap_1, swap_2, x_hi, x_lo, ends, p_hi, p_lo):
    part = jax.ShapeDtypeStruct((RB * BLOCK, 256), BF16)
    whole = jax.ShapeDtypeStruct(p_hi.shape, BF16)
    return pl.pallas_call(
        second_kernel,
        out_shape=(part, part, jax.ShapeDtypeStruct((M + 8, M), F32), whole, whole),
        in_specs=[VMEM] * 10,
        out_specs=(VMEM,) * 5,
        input_output_aliases={8: 3, 9: 4},
        compiler_params=PARAMS,
        cost_estimate=pl.CostEstimate(
            flops=6 * RB * 128 * 256 * 256, bytes_accessed=8 << 20, transcendentals=0
        ),
        name="second_product",
    )(own, g_hi, g_lo, swap_1, swap_2, x_hi, x_lo, ends, p_hi, p_lo)[:3]


def inverse_factor(a, work):
    row = lax.broadcasted_iota(jnp.int32, (M, M), 0)
    col = lax.broadcasted_iota(jnp.int32, (M, M), 1)
    work[:, :M] = a
    work[:, M:] = jnp.where(row == col, 1.0, 0.0)
    sub = lax.broadcasted_iota(jnp.int32, (8, M), 0)
    groups = OUTER // 8

    def line(x, j):
        return x[j : j + 1, :]

    def tall(x, j):
        return jnp.broadcast_to(line(x, j), (8, M))

    def spread(x, at):
        return [jnp.broadcast_to(x[:, at + k : at + k + 1], (8, M)) for k in range(8)]

    for top in range(0, M, OUTER):
        left = [work[top + 8 * g : top + 8 * g + 8, :M] for g in range(groups)]
        right = [work[top + 8 * g : top + 8 * g + 8, M:] for g in range(groups)]
        ahead = spread(left[0], top)
        for q in range(groups):
            at = top + 8 * q
            cols = {q: ahead, **{g: spread(left[g], at) for g in range(q + 1, groups)}}
            more = q + 1 < groups
            if more:
                ahead, mine = spread(left[q + 1], at + 8), spread(left[q], at + 8)
            scales = jnp.zeros((8, M), F32)
            for j in range(0, 8, 2):
                a0, a1, a2 = tall(cols[q][j], j), tall(cols[q][j], j + 1), tall(cols[q][j + 1], j + 1)
                det = a0 * a2 - a1 * a1
                inverse = pltpu.reciprocal(det, approx=False)
                root = lax.rsqrt(a0)
                ratio = a1 * (root * root)
                scales = jnp.where(sub == j, root, scales)
                scales = jnp.where(sub == j + 1, lax.rsqrt(det) * (a0 * root), scales)
                row_0 = [line(cols[q][k], j) for k in range(8)]
                row_1 = [line(cols[q][k], j + 1) for k in range(8)]
                left_0, left_1 = line(left[q], j), line(left[q], j + 1)
                right_0, right_1 = line(right[q], j), line(right[q], j + 1)
                if more:
                    mine_0 = [line(x, j) for x in mine]
                    mine_1 = [line(x, j + 1) for x in mine]
                for g in range(q, groups):
                    c0, c1 = cols[g][j], cols[g][j + 1]
                    y0 = a2 * c0 - a1 * c1
                    y1 = a0 * c1 - a1 * c0
                    if g == q:
                        y0 = jnp.where(sub > j + 1, y0, 0.0)
                        y1 = jnp.where(sub > j + 1, y1, 0.0)
                    for k in range(j + 2, 8):
                        cols[g][k] = cols[g][k] - (y0 * row_0[k] + y1 * row_1[k]) * inverse
                    x0, x1 = y0 * inverse, y1 * inverse
                    if g == q:
                        x0 = jnp.where(sub == j + 1, ratio, x0)
                    left[g] = left[g] - (x0 * left_0 + x1 * left_1)
                    right[g] = right[g] - (x0 * right_0 + x1 * right_1)
                    if more and g <= q + 1:
                        part = mine if g == q else ahead
                        for k in range(8):
                            part[k] = part[k] - (x0 * mine_0[k] + x1 * mine_1[k])
            left[q] = left[q] * scales
            right[q] = right[q] * scales
        for g in range(groups):
            work[top + 8 * g : top + 8 * g + 8, :M] = left[g]
            work[top + 8 * g : top + 8 * g + 8, M:] = right[g]
        if top + OUTER < M:
            panel = work[top : top + OUTER, :]
            update = lax.dot_general(
                panel[:, :M], panel, (((0,), (0,)), ((), ())),
                precision=HIGHEST, preferred_element_type=F32,
            )
            work[top + OUTER :, :] = work[top + OUTER :, :] - update[top + OUTER :, :]
    return work[:, M:]


def finish_kernel(total_rows, *refs):
    grams, (z_hi, z_lo, out, work, held, sems) = refs[:-6], refs[-6:]
    own = grams[0]
    row = lax.broadcasted_iota(jnp.int32, (M, M), 0)
    col = lax.broadcasted_iota(jnp.int32, (M, M), 1)
    eye = jnp.where(row == col, 1.0, 0.0)

    def as_column(v):
        return jnp.sum(eye * v, axis=1, keepdims=True)

    def row_of(x):
        return jnp.sum(eye * x, axis=0, keepdims=True)

    total = own[:M, :]
    for one in grams[1:]:
        total = total + one[:M, :]
    gram = jnp.where(row >= col, total, total.T)
    norm = lax.rsqrt(row_of(gram))
    inverse = inverse_factor(gram * norm * as_column(norm), work)
    total = jnp.zeros((M, M), F32)
    for one in grams:
        size = norm * one[M + 1 : M + 2, :]
        second = jnp.where(row == col, one[M : M + 1, :], one[:M, :])
        total = total + second * size * as_column(size)
    gram = jnp.where(row <= col, total, total.T)
    gram = dot_f32(dot_f32(inverse, gram), inverse.T)
    scale = lax.rsqrt(row_of(gram))
    second = inverse_factor(gram * scale * as_column(scale), work) * scale
    inverse = dot_f32(second, inverse)
    change = (inverse * (norm * own[M + 1 : M + 2, :] * (total_rows**0.5))).T
    c_hi, c_lo = split(change)
    right = jnp.concatenate(
        [
            jnp.concatenate([c_hi, c_lo], axis=1),
            jnp.concatenate([c_hi, jnp.zeros_like(c_lo)], axis=1),
        ],
        axis=0,
    )
    copies = []
    for i in range(z_hi.shape[0] // STEP):
        at = pl.ds(i * STEP, STEP)
        hi, lo = z_hi[at, :], z_lo[at, :]
        for part in range(2):
            cols = slice(part * M, part * M + M)
            both = dot(jnp.concatenate([hi[:, cols], lo[:, cols]], axis=1), right)
            held[part, at, :] = both[:, :M] + both[:, M:]
        copies.append(pltpu.make_async_copy(held.at[:, at, :], out.at[:, at, :], sems.at[i]))
        copies[-1].start()
    for copy in copies:
        copy.wait()


def finish(grams, z_hi, z_lo, total_rows):
    return pl.pallas_call(
        partial(finish_kernel, total_rows),
        out_shape=jax.ShapeDtypeStruct((2, z_hi.shape[0], M), F32),
        in_specs=[VMEM] * (len(grams) + 2),
        out_specs=pl.BlockSpec(memory_space=pl.ANY),
        scratch_shapes=[
            pltpu.VMEM((M, 2 * M), F32),
            pltpu.VMEM((2, z_hi.shape[0], M), F32),
            pltpu.SemaphoreType.DMA((z_hi.shape[0] // STEP,)),
        ],
        compiler_params=PARAMS,
        name="finish",
    )(*grams, z_hi, z_lo)


def neighbours(x, begin):
    pairs = [(i, i + 1) for i in range(begin, lax.axis_size("blk") - 1, 2)]
    return lax.ppermute(x, "blk", pairs + [(j, i) for i, j in pairs])


def swapped(x, far, axis="src"):
    return lax.ppermute(x, axis, [(i, i ^ far) for i in range(lax.axis_size(axis))])


def gathered(own, ready, axis="src"):
    peers = lax.axis_size(axis)
    if peers & (peers - 1):
        chunks = [
            lax.ppermute(own, axis, [(i, (i + k) % peers) for i in range(peers)])
            for k in range(1, peers)
        ]
        return chunks, ready
    far = peers // 2
    chunks = []
    while far:
        if chunks and ready:
            chunks, ready = lax.optimization_barrier((chunks, ready))
        chunks = chunks + [swapped(c, far, axis) for c in [own] + chunks]
        far //= 2
    return chunks, ready


def per_device(pupils, starts, counts, weights, start_block):
    regions = lax.axis_size("blk")
    size = start_block.shape[1]

    own = pack(pupils, starts, counts, weights, regions * RB)
    ready = (build(own, None), *prepare(start_block))
    chunks, ready = gathered(own, ready)
    band, x_hi, x_lo = ready
    for chunk in chunks[:-1]:
        band = build(chunk, band)
    swap_1, swap_2 = build_edges(chunks[-1], band, start_block)
    swap_2 = neighbours(swap_2, 0)
    swap_1 = neighbours(swap_1, 1)
    g_hi, g_lo = build(chunks[-1], band, last=True)
    p_hi, p_lo, ends = first_product(g_hi, g_lo, x_hi, x_lo)
    z_hi, z_lo, grams = second_product(
        own, g_hi, g_lo, swap_1, swap_2, x_hi, x_lo, ends, p_hi, p_lo
    )
    grams = [grams] + gathered(grams, (), "blk")[0]
    return finish(grams, z_hi, z_lo, 2.0 * size * regions)


def solution(mesh):
    placed = (
        P(("groups", "src", "blk"), None, None),
        P(("groups", "src", "blk")),
        P(("groups", "src", "blk")),
        P(("groups", "src", "blk")),
        P("groups", "blk", None),
    )
    return jax.shard_map(
        per_device, mesh=mesh, in_specs=placed, out_specs=P("groups", "blk", None), check_vma=False
    )
```

```python
from functools import partial

import jax
import jax.numpy as jnp
from jax import lax
from jax.experimental import pallas as pl
from jax.experimental.pallas import tpu as pltpu
from jax.sharding import PartitionSpec as P

BLOCK = 64
RB = 32
GROUP = 2
OUTER = 64
STEP = 256
M = 128
F32 = jnp.float32
BF16 = jnp.bfloat16
HIGHEST = lax.Precision.HIGHEST
VMEM = pl.BlockSpec(memory_space=pltpu.VMEM)
PARAMS = pltpu.CompilerParams(vmem_limit_bytes=16 * 1024 * 1024)


def split(x):
    hi = x.astype(BF16)
    return hi, (x - hi.astype(F32)).astype(BF16)


def dot(a, b):
    return jnp.dot(a, b, preferred_element_type=F32)


def dot_t(a, b):
    return lax.dot_general(a, b, (((0,), (0,)), ((), ())), preferred_element_type=F32)


def dot_f32(a, b):
    return jnp.dot(a, b, precision=HIGHEST, preferred_element_type=F32)


def pack_kernel(total_blocks, *refs):
    sent, out, held, sems = refs[:4], refs[4], refs[5:9], refs[9]
    copies = [pltpu.make_async_copy(sent[i], held[i], sems.at[i]) for i in range(4)]
    for copy in copies:
        copy.start()
    for copy in copies:
        copy.wait()
    pupils, starts, counts, weights = held
    tiles = starts.shape[0]
    lane = lax.broadcasted_iota(jnp.int32, (128, 2 * BLOCK), 1)
    start = starts[...]
    root = jnp.sqrt(weights[...])
    first_live = jnp.where(counts[...] > 0, root, 0.0)
    second_live = jnp.where((counts[...] > 1) & (start + 1 < total_blocks), root, 0.0)
    for t in range(tiles):
        first_column = jnp.broadcast_to(first_live[t : t + 1, :], (128, 128)).T
        second_column = jnp.broadcast_to(second_live[t : t + 1, :], (128, 128)).T
        first = pupils[pl.ds(256 * t, 128, stride=2), :] * first_column
        second = pupils[pl.ds(256 * t + 1, 128, stride=2), :] * second_column
        real = jnp.where(lane < BLOCK, first, pltpu.roll(second, BLOCK, 1))
        imag = jnp.where(lane < BLOCK, pltpu.roll(first, BLOCK, 1), second)
        out[128 * t : 128 * t + 128, :] = real
        out[128 * (tiles + t) : 128 * (tiles + t) + 128, :] = imag
    out[256 * tiles :, :] = jnp.zeros((8, 128), F32)
    out[256 * tiles : 256 * tiles + tiles, :] = lax.rem(start, RB).astype(F32)
    out[256 * tiles + 7 :, :] = lax.rem(lax.div(start[:1, :], RB), 2).astype(F32)


def pack(pupils, starts, counts, weights, total_blocks):
    slots = pupils.shape[0]
    return pl.pallas_call(
        partial(pack_kernel, total_blocks),
        out_shape=jax.ShapeDtypeStruct((2 * slots + 8, 128), F32),
        in_specs=[pl.BlockSpec(memory_space=pl.ANY)] * 4,
        out_specs=VMEM,
        scratch_shapes=[
            pltpu.VMEM((2 * slots, 128), F32),
            pltpu.VMEM((slots // 128, 128), jnp.int32),
            pltpu.VMEM((slots // 128, 128), jnp.int32),
            pltpu.VMEM((slots // 128, 128), F32),
            pltpu.SemaphoreType.DMA((4,)),
        ],
        compiler_params=PARAMS,
        name="pack",
    )(
        *(
            pltpu.with_memory_space_constraint(x, pltpu.HBM)
            for x in (
                pupils.reshape(2 * slots, 128),
                starts.reshape(-1, 128),
                counts.reshape(-1, 128),
                weights.reshape(-1, 128),
            )
        )
    )


def factors(chunk):
    count = (chunk.shape[0] - 8) // 2
    real = chunk[:count, :]
    imag = chunk[count : 2 * count, :]
    left = jnp.concatenate([real.T, imag.T], axis=1).astype(BF16)
    right = []
    for scale, real, imag in zip((0.5, 1.0), split(real), split(imag)):
        right.append(
            jnp.concatenate(
                [
                    jnp.concatenate([real, -imag], axis=1),
                    jnp.concatenate([imag, real], axis=1),
                ],
                axis=0,
            )
            * jnp.asarray(scale, BF16)
        )
    places = [chunk[2 * count + t : 2 * count + t + 1, :] for t in range(count // 128)]
    place = jnp.broadcast_to(jnp.concatenate(places + places, axis=1), (16, 2 * count))
    return left, right[0], right[1], place


def at_block(part, place, b):
    mask = jnp.where(place == b, 1.0, 0.0).astype(BF16)[None]
    return (part.reshape(8, 16, -1) * mask).reshape(part.shape)


def hermitian(q):
    real, imag = q[:, :128], q[:, 128:]
    return jnp.concatenate([real + real.T, imag - imag.T], axis=1)


def build_kernel(add, last, chunk, *refs):
    refs = list(refs)
    before = refs.pop(0) if add else None
    lhs = refs.pop()
    left, right_hi, right_lo, place = factors(chunk)

    def one_group(g, carry):
        for j in range(GROUP):
            b = (g * GROUP + j).astype(F32)
            lhs[j * 128 : (j + 1) * 128, :] = at_block(left, place, b)
        at = pl.ds(pl.multiple_of(g * GROUP * 128, GROUP * 128), GROUP * 128)
        hi = lhs[...]
        total = dot(hi, right_hi) + dot(hi, right_lo)
        if add:
            total = before[at, :] + total
        if last:
            for j in range(GROUP):
                one = pl.ds(pl.multiple_of((g * GROUP + j) * 128, 128), 128)
                refs[0][one, :], refs[1][one, :] = split(
                    hermitian(total[j * 128 : (j + 1) * 128, :])
                )
        else:
            refs[0][at, :] = total
        return carry

    lax.fori_loop(0, RB // GROUP, one_group, 0, unroll=RB // GROUP)


def build(chunk, before, last=False):
    count = (chunk.shape[0] - 8) // 2
    add = before is not None
    shape = (RB * 128, 256)
    out = [jax.ShapeDtypeStruct(shape, BF16)] * 2 if last else [jax.ShapeDtypeStruct(shape, F32)]
    result = pl.pallas_call(
        partial(build_kernel, add, last),
        out_shape=out,
        in_specs=[VMEM] * (1 + add),
        out_specs=[VMEM] * len(out),
        scratch_shapes=[pltpu.VMEM((GROUP * 128, 2 * count), BF16)],
        input_output_aliases={1: 0} if add and not last else {},
        compiler_params=PARAMS,
        cost_estimate=pl.CostEstimate(
            flops=1 << 20, bytes_accessed=1 << 16, transcendentals=0
        ),
        name="band_terms",
    )(chunk, *([before] if add else []))
    return result if last else result[0]


def wide(parts):
    return jnp.concatenate([parts[0], parts[1]], axis=1)


def real_form(rows):
    return jnp.concatenate(
        [rows, jnp.concatenate([-rows[:, M:], rows[:, :M]], axis=1)], axis=0
    )


def times(g_hi, g_lo, hi, lo):
    hi, lo = real_form(hi), real_form(lo)
    return dot(g_hi, hi) + dot(g_hi, lo) + dot(g_lo, hi)


def gram_of(hi, lo):
    half = jnp.asarray(0.5, BF16)
    q = 0.0
    for cols in (slice(0, M), slice(M, 2 * M)):
        q += dot_t(hi[:, cols], jnp.concatenate([hi[:, cols] * half, lo[:, cols]], axis=1))
    q = q[:, :M] + q[:, M:]
    return q + q.T


def in_odd_region(chunk):
    row = chunk[chunk.shape[0] - 1 :, :]
    return jnp.concatenate([row, row], axis=1) == 1.0


def edge_kernel(chunk, before, x, first_out, second_out):
    left, right_hi, right_lo, place = factors(chunk)
    blocks = (0, RB - 2, RB - 1)
    left = jnp.concatenate([at_block(left, place, float(b)) for b in blocks], axis=0)
    total = dot(left, right_hi) + dot(left, right_lo)
    head, next_last, last = [
        hermitian(before[b * 128 : (b + 1) * 128, :] + total[i * 128 : (i + 1) * 128, :])
        for i, b in enumerate(blocks)
    ]
    size = x.shape[1]
    start = wide(x[:, : 2 * BLOCK, :])
    stop = wide(x[:, size - 2 * BLOCK :, :])
    held = jnp.concatenate([stop[BLOCK:], jnp.zeros((BLOCK, 256), F32)], axis=0)
    own = times(*split(last), *split(held))
    to_after = jnp.concatenate(
        [
            own[:BLOCK] + times(*split(next_last[BLOCK:]), *split(stop)),
            own[BLOCK:],
            last[BLOCK:],
        ],
        axis=0,
    )
    to_before = jnp.concatenate(
        [times(*split(head[:BLOCK]), *split(start)), start[:BLOCK], jnp.zeros((BLOCK, 256), F32)],
        axis=0,
    )
    is_odd = in_odd_region(chunk)
    first_out[...] = jnp.where(is_odd, to_after, to_before)
    second_out[...] = jnp.where(is_odd, to_before, to_after)


def build_edges(chunk, before, x):
    shape = jax.ShapeDtypeStruct((3 * BLOCK, 256), F32)
    return pl.pallas_call(
        edge_kernel,
        out_shape=(shape, shape),
        in_specs=[VMEM] * 3,
        out_specs=(VMEM, VMEM),
        compiler_params=PARAMS,
        name="edge_terms",
    )(chunk, before, x)


def prepare_kernel(x, hi_out, lo_out):
    for i in range(0, x.shape[1], 256):
        hi_out[i : i + 256, :], lo_out[i : i + 256, :] = split(wide(x[:, i : i + 256, :]))


def prepare(x):
    shape = jax.ShapeDtypeStruct((x.shape[1], 256), BF16)
    return pl.pallas_call(
        prepare_kernel,
        out_shape=(shape, shape),
        in_specs=[VMEM],
        out_specs=(VMEM, VMEM),
        compiler_params=PARAMS,
        cost_estimate=pl.CostEstimate(flops=1 << 20, bytes_accessed=4 << 20, transcendentals=0),
        name="prepare",
    )(x)


def join(a, b):
    return jnp.concatenate([a, b], axis=0)


def put(hi, lo, e, block):
    at = pl.ds(pl.multiple_of(e * BLOCK, BLOCK), BLOCK)
    hi[at, :], lo[at, :] = split(block)


def first_kernel(g_hi, g_lo, x_hi, x_lo, p_hi, p_lo, ends):
    rows = RB * BLOCK
    nothing = jnp.zeros((BLOCK, 256), BF16)

    def pair(b):
        at = pl.ds(pl.multiple_of(b * 128, 128), 128)
        win = pl.ds(pl.multiple_of(b * BLOCK, BLOCK), 128)
        return times(g_hi[at, :], g_lo[at, :], x_hi[win, :], x_lo[win, :])

    def one(b, carry):
        spill, top = carry
        both = pair(b)
        block = both[:BLOCK] + spill
        put(p_hi, p_lo, b + 1, block)
        return both[BLOCK:], jnp.maximum(top, jnp.abs(block))

    both = pair(0)
    ends[:BLOCK, :] = both[:BLOCK]
    carry = both[BLOCK:], jnp.zeros((BLOCK, 256), F32)
    spill, top = lax.fori_loop(1, RB - 1, one, carry, unroll=RB - 2)
    both = times(
        g_hi[(RB - 1) * 128 :, :],
        g_lo[(RB - 1) * 128 :, :],
        join(x_hi[rows - BLOCK :, :], nothing),
        join(x_lo[rows - BLOCK :, :], nothing),
    )
    ends[BLOCK : 2 * BLOCK, :] = both[:BLOCK] + spill
    ends[2 * BLOCK : 3 * BLOCK, :] = both[BLOCK:]
    ends[3 * BLOCK :, :] = jnp.broadcast_to(jnp.max(top, axis=0, keepdims=True), (8, 256))


def first_product(g_hi, g_lo, x_hi, x_lo):
    shape = jax.ShapeDtypeStruct(((RB + 2) * BLOCK, 256), BF16)
    return pl.pallas_call(
        first_kernel,
        out_shape=(shape, shape, jax.ShapeDtypeStruct((3 * BLOCK + 8, 256), F32)),
        in_specs=[VMEM] * 4,
        out_specs=(VMEM, VMEM, VMEM),
        compiler_params=PARAMS,
        cost_estimate=pl.CostEstimate(flops=1 << 20, bytes_accessed=1 << 16, transcendentals=0),
        name="first_product",
    )(g_hi, g_lo, x_hi, x_lo)


def second_kernel(own, g_hi, g_lo, swap_1, swap_2, x_hi, x_lo, ends, p_hi_in, p_lo_in,
                  z_hi, z_lo, grams, p_hi, p_lo):
    rows = RB * BLOCK
    is_odd = in_odd_region(own)
    left = jnp.where(is_odd, swap_2[...], swap_1[...])
    right = jnp.where(is_odd, swap_1[...], swap_2[...])
    into = left[2 * BLOCK :]
    into_hi, into_lo = split(into)
    none = jnp.zeros((BLOCK, 128), F32)
    out_of = [jnp.concatenate([none, part], axis=0).T[:BLOCK] for part in (into[:, :M], into[:, M:])]
    out_hi, out_lo = split(jnp.concatenate([out_of[0], -out_of[1]], axis=1))
    tail = split(right[BLOCK : 2 * BLOCK])
    nothing = jnp.zeros((BLOCK, 256), BF16)
    both = times(
        join(out_hi, into_hi),
        join(out_lo, into_lo),
        join(nothing, x_hi[:BLOCK, :]),
        join(nothing, x_lo[:BLOCK, :]),
    ) + left[: 2 * BLOCK]
    after = times(
        g_hi[(RB - 1) * 128 :, :],
        g_lo[(RB - 1) * 128 :, :],
        join(nothing, tail[0]),
        join(nothing, tail[1]),
    )
    top = ends[3 * BLOCK : 3 * BLOCK + 1, :]
    for e, block in (
        (0, both[:BLOCK]),
        (1, both[BLOCK:] + ends[:BLOCK, :]),
        (RB, after[:BLOCK] + ends[BLOCK : 2 * BLOCK, :]),
        (RB + 1, after[BLOCK:] + ends[2 * BLOCK : 3 * BLOCK, :] + right[:BLOCK]),
    ):
        put(p_hi, p_lo, e, block)
        top = jnp.maximum(top, jnp.max(jnp.abs(block), axis=0, keepdims=True))
    top = jnp.maximum(top[:, :M], top[:, M:])
    scale = jnp.where(top > 0, 1.0 / jnp.where(top > 0, top, 1.0), 0.0)
    scale = jnp.concatenate([scale, scale], axis=1)

    inner = pl.ds(BLOCK, rows)
    gram_1 = gram_of(p_hi[inner, :], p_lo[inner, :])

    def second(b, spill):
        at = pl.ds(pl.multiple_of(b * 128, 128), 128)
        win = pl.ds(pl.multiple_of((b + 1) * BLOCK, BLOCK), 128)
        both = times(g_hi[at, :], g_lo[at, :], p_hi[win, :], p_lo[win, :])
        out = pl.ds(pl.multiple_of(b * BLOCK, BLOCK), BLOCK)
        z_hi[out, :], z_lo[out, :] = split((both[:BLOCK] + spill) * scale)
        return both[BLOCK:]

    spill = times(into_hi, into_lo, p_hi[:128, :], p_lo[:128, :])
    lax.fori_loop(0, RB, second, spill, unroll=RB)
    gram_2 = gram_of(z_hi[...], z_lo[...])
    row = lax.broadcasted_iota(jnp.int32, (M, M), 0)
    col = lax.broadcasted_iota(jnp.int32, (M, M), 1)
    grams[:M, :] = jnp.where(row >= col, gram_1, gram_2)
    diagonal = jnp.sum(jnp.where(row == col, gram_2, 0.0), axis=0, keepdims=True)
    grams[M:, :] = jnp.concatenate([diagonal, top, jnp.zeros((6, M), F32)], axis=0)


def second_product(own, g_hi, g_lo, swap_1, swap_2, x_hi, x_lo, ends, p_hi, p_lo):
    part = jax.ShapeDtypeStruct((RB * BLOCK, 256), BF16)
    whole = jax.ShapeDtypeStruct(p_hi.shape, BF16)
    return pl.pallas_call(
        second_kernel,
        out_shape=(part, part, jax.ShapeDtypeStruct((M + 8, M), F32), whole, whole),
        in_specs=[VMEM] * 10,
        out_specs=(VMEM,) * 5,
        input_output_aliases={8: 3, 9: 4},
        compiler_params=PARAMS,
        cost_estimate=pl.CostEstimate(
            flops=6 * RB * 128 * 256 * 256, bytes_accessed=8 << 20, transcendentals=0
        ),
        name="second_product",
    )(own, g_hi, g_lo, swap_1, swap_2, x_hi, x_lo, ends, p_hi, p_lo)[:3]


def inverse_factor(a, work):
    row = lax.broadcasted_iota(jnp.int32, (M, M), 0)
    col = lax.broadcasted_iota(jnp.int32, (M, M), 1)
    work[:, :M] = a
    work[:, M:] = jnp.where(row == col, 1.0, 0.0)
    sub = lax.broadcasted_iota(jnp.int32, (8, M), 0)
    groups = OUTER // 8

    def line(x, j):
        return x[j : j + 1, :]

    def tall(x, j):
        return jnp.broadcast_to(line(x, j), (8, M))

    def spread(x, at):
        return [jnp.broadcast_to(x[:, at + k : at + k + 1], (8, M)) for k in range(8)]

    for top in range(0, M, OUTER):
        left = [work[top + 8 * g : top + 8 * g + 8, :M] for g in range(groups)]
        right = [work[top + 8 * g : top + 8 * g + 8, M:] for g in range(groups)]
        ahead = spread(left[0], top)
        for q in range(groups):
            at = top + 8 * q
            cols = {q: ahead, **{g: spread(left[g], at) for g in range(q + 1, groups)}}
            more = q + 1 < groups
            if more:
                ahead, mine = spread(left[q + 1], at + 8), spread(left[q], at + 8)
            scales = jnp.zeros((8, M), F32)
            for j in range(0, 8, 2):
                a0, a1, a2 = tall(cols[q][j], j), tall(cols[q][j], j + 1), tall(cols[q][j + 1], j + 1)
                det = a0 * a2 - a1 * a1
                inverse = pltpu.reciprocal(det, approx=False)
                root = lax.rsqrt(a0)
                ratio = a1 * (root * root)
                scales = jnp.where(sub == j, root, scales)
                scales = jnp.where(sub == j + 1, lax.rsqrt(det) * (a0 * root), scales)
                row_0 = [line(cols[q][k], j) for k in range(8)]
                row_1 = [line(cols[q][k], j + 1) for k in range(8)]
                left_0, left_1 = line(left[q], j), line(left[q], j + 1)
                right_0, right_1 = line(right[q], j), line(right[q], j + 1)
                if more:
                    mine_0 = [line(x, j) for x in mine]
                    mine_1 = [line(x, j + 1) for x in mine]
                for g in range(q, groups):
                    c0, c1 = cols[g][j], cols[g][j + 1]
                    y0 = a2 * c0 - a1 * c1
                    y1 = a0 * c1 - a1 * c0
                    if g == q:
                        y0 = jnp.where(sub > j + 1, y0, 0.0)
                        y1 = jnp.where(sub > j + 1, y1, 0.0)
                    for k in range(j + 2, 8):
                        cols[g][k] = cols[g][k] - (y0 * row_0[k] + y1 * row_1[k]) * inverse
                    x0, x1 = y0 * inverse, y1 * inverse
                    if g == q:
                        x0 = jnp.where(sub == j + 1, ratio, x0)
                    left[g] = left[g] - (x0 * left_0 + x1 * left_1)
                    right[g] = right[g] - (x0 * right_0 + x1 * right_1)
                    if more and g <= q + 1:
                        part = mine if g == q else ahead
                        for k in range(8):
                            part[k] = part[k] - (x0 * mine_0[k] + x1 * mine_1[k])
            left[q] = left[q] * scales
            right[q] = right[q] * scales
        for g in range(groups):
            work[top + 8 * g : top + 8 * g + 8, :M] = left[g]
            work[top + 8 * g : top + 8 * g + 8, M:] = right[g]
        if top + OUTER < M:
            panel = work[top : top + OUTER, :]
            update = lax.dot_general(
                panel[:, :M], panel, (((0,), (0,)), ((), ())),
                precision=HIGHEST, preferred_element_type=F32,
            )
            work[top + OUTER :, :] = work[top + OUTER :, :] - update[top + OUTER :, :]
    return work[:, M:]


def finish_kernel(total_rows, *refs):
    grams, (z_hi, z_lo, out, work, held, sems) = refs[:-6], refs[-6:]
    own = grams[0]
    row = lax.broadcasted_iota(jnp.int32, (M, M), 0)
    col = lax.broadcasted_iota(jnp.int32, (M, M), 1)
    eye = jnp.where(row == col, 1.0, 0.0)

    def as_column(v):
        return jnp.sum(eye * v, axis=1, keepdims=True)

    def row_of(x):
        return jnp.sum(eye * x, axis=0, keepdims=True)

    total = own[:M, :]
    for one in grams[1:]:
        total = total + one[:M, :]
    gram = jnp.where(row >= col, total, total.T)
    norm = lax.rsqrt(row_of(gram))
    inverse = inverse_factor(gram * norm * as_column(norm), work)
    total = jnp.zeros((M, M), F32)
    for one in grams:
        size = norm * one[M + 1 : M + 2, :]
        second = jnp.where(row == col, one[M : M + 1, :], one[:M, :])
        total = total + second * size * as_column(size)
    gram = jnp.where(row <= col, total, total.T)
    gram = dot_f32(dot_f32(inverse, gram), inverse.T)
    scale = lax.rsqrt(row_of(gram))
    second = inverse_factor(gram * scale * as_column(scale), work) * scale
    inverse = dot_f32(second, inverse)
    change = (inverse * (norm * own[M + 1 : M + 2, :] * (total_rows**0.5))).T
    c_hi, c_lo = split(change)
    right = jnp.concatenate(
        [
            jnp.concatenate([c_hi, c_lo], axis=1),
            jnp.concatenate([c_hi, jnp.zeros_like(c_lo)], axis=1),
        ],
        axis=0,
    )
    copies = []
    for i in range(z_hi.shape[0] // STEP):
        at = pl.ds(i * STEP, STEP)
        hi, lo = z_hi[at, :], z_lo[at, :]
        for part in range(2):
            cols = slice(part * M, part * M + M)
            both = dot(jnp.concatenate([hi[:, cols], lo[:, cols]], axis=1), right)
            held[part, at, :] = both[:, :M] + both[:, M:]
        copies.append(pltpu.make_async_copy(held.at[:, at, :], out.at[:, at, :], sems.at[i]))
        copies[-1].start()
    for copy in copies:
        copy.wait()


def finish(grams, z_hi, z_lo, total_rows):
    return pl.pallas_call(
        partial(finish_kernel, total_rows),
        out_shape=jax.ShapeDtypeStruct((2, z_hi.shape[0], M), F32),
        in_specs=[VMEM] * (len(grams) + 2),
        out_specs=pl.BlockSpec(memory_space=pl.ANY),
        scratch_shapes=[
            pltpu.VMEM((M, 2 * M), F32),
            pltpu.VMEM((2, z_hi.shape[0], M), F32),
            pltpu.SemaphoreType.DMA((z_hi.shape[0] // STEP,)),
        ],
        compiler_params=PARAMS,
        name="finish",
    )(*grams, z_hi, z_lo)


def neighbours(x, begin):
    pairs = [(i, i + 1) for i in range(begin, lax.axis_size("blk") - 1, 2)]
    return lax.ppermute(x, "blk", pairs + [(j, i) for i, j in pairs])


def swapped(x, far, axis="src"):
    return lax.ppermute(x, axis, [(i, i ^ far) for i in range(lax.axis_size(axis))])


def gathered(own, ready, axis="src"):
    peers = lax.axis_size(axis)
    if peers & (peers - 1):
        chunks = [
            lax.ppermute(own, axis, [(i, (i + k) % peers) for i in range(peers)])
            for k in range(1, peers)
        ]
        return chunks, ready
    far = peers // 2
    chunks = []
    while far:
        if chunks and ready:
            chunks, ready = lax.optimization_barrier((chunks, ready))
        chunks = chunks + [swapped(c, far, axis) for c in [own] + chunks]
        far //= 2
    return chunks, ready


def per_device(pupils, starts, counts, weights, start_block):
    regions = lax.axis_size("blk")
    size = start_block.shape[1]

    own = pack(pupils, starts, counts, weights, regions * RB)
    ready = (build(own, None), *prepare(start_block))
    chunks, ready = gathered(own, ready)
    band, x_hi, x_lo = ready
    for chunk in chunks[:-1]:
        band = build(chunk, band)
    swap_1, swap_2 = build_edges(chunks[-1], band, start_block)
    swap_2 = neighbours(swap_2, 0)
    swap_1 = neighbours(swap_1, 1)
    g_hi, g_lo = build(chunks[-1], band, last=True)
    swap_2, g_hi, g_lo = lax.optimization_barrier((swap_2, g_hi, g_lo))
    p_hi, p_lo, ends = first_product(g_hi, g_lo, x_hi, x_lo)
    z_hi, z_lo, grams = second_product(
        own, g_hi, g_lo, swap_1, swap_2, x_hi, x_lo, ends, p_hi, p_lo
    )
    grams = [grams] + gathered(grams, (), "blk")[0]
    return finish(grams, z_hi, z_lo, 2.0 * size * regions)


def solution(mesh):
    placed = (
        P(("groups", "src", "blk"), None, None),
        P(("groups", "src", "blk")),
        P(("groups", "src", "blk")),
        P(("groups", "src", "blk")),
        P("groups", "blk", None),
    )
    return jax.shard_map(
        per_device, mesh=mesh, in_specs=placed, out_specs=P("groups", "blk", None), check_vma=False
    )
```
